256 devices in a mesh: dap: 64 (over y, z, x_lo), head: 4 (over x_hi, core).
Axes of the slice: x: 4 (x_hi: 2, x_lo: 2; x = x_hi * 2 + x_lo), y: 4, z: 8, core: 2. Of those that a mesh axis runs over, the one named last changes fastest.
Arguments:
- lineup_embedding: float32 [256, 1024, 256], P('dap'), may hold values from -6 to 6
- pairwise_state: float32 [1024, 1024, 128], P('dap', 'head'), may hold values from -6 to 6
- lineup_scaling_coefficients: float32 [256], replicated, may hold values from 0.1 to 1.9
- focus_projection_matrix: float32 [4, 256, 256], P(None, None, 'head'), may hold values from -0.375 to 0.375
- attention_gate_bias: float32 [256], P('head'), may hold values from -4 to 4
- focus_merge_matrix: float32 [256, 256], P('head'), may hold values from -0.375 to 0.375
- pairwise_bias_weight: float32 [128, 8], replicated, may hold values from -0.5 to 0.5
- relative_bias_table: float32 [66, 8], replicated, may hold values from -4 to 250
- tensor_operand_matrices: float32 [2, 256, 32], replicated, may hold values from -0.375 to 0.375
- outer_output_weight: float32 [1024, 128], replicated, may hold values from -1.5 to 1.5
- outer_output_bias: float32 [128], replicated, may hold values from -4 to 4
- lineup_member_flags: int32 [256], replicated, may hold values 0 or 1
- residue_presence_mask: int32 [1024], replicated, may hold values 0 or 1
- chain_label: int32 [1024], replicated, may hold values from 0 to 3, never falling along the last dimension, each value on 1 to 512 neighbouring positions
- residue_numbering: int32 [1024], replicated, may hold values from 0 to 1535, as said below
Outputs:
- alignment_state_next: float32 [256, 1024, 256], P('dap')
- pairwise_state_next: float32 [1024, 1024, 128], P('dap', 'head')
The draws below stay inside these ranges and needn't reach their ends.
Inputs may be any that keep to these rules, and one draw needn't show every extreme that they name: `residue_numbering`: starts at 0 and rises by 1 or 2 from each residue to the next, by 2 at exactly 512 of the steps.
All inputs are finite; a program needn't handle non-finite values.
Results may differ from the reference program's by a relative error of at most 0.0003.
Values sent between devices are 32-bit elements; how exact they have to be, the bound alone decides.
No kernel may reach another device: no remote copies, remote signals or barrier semaphores. Data moves between devices by JAX's collectives and lax.ppermute only.
A program may use at most 128 MiB of HBM per device.

```python
import math
from functools import partial
import jax
import jax.numpy as jnp
import numpy as np
from jax import lax

WINDOW_POSITIONS = 1024
LINEUP_MEMBERS = 256
LINEUP_FEATURES = 256
PAIR_CHANNELS = 128
FOCUS_GROUPS = 8
GROUP_FEATURES = 32
RANK_WIDTH = 32
BUCKETS = 66


def draw_relative_bias_table(key, part):
    key = jax.random.fold_in(key, 11)
    return jnp.clip(jax.random.normal(key, (BUCKETS, FOCUS_GROUPS), jnp.float32), -4.0, 4.0)


def draw_residue_numbering(key, part):
    key = jax.random.fold_in(key, 7)
    order = jax.random.permutation(key, jnp.arange(WINDOW_POSITIONS - 1, dtype=jnp.int32))
    steps_up = jnp.where(order < WINDOW_POSITIONS // 2, 2, 1).astype(jnp.int32)
    return jnp.concatenate([jnp.zeros((1,), jnp.int32), jnp.cumsum(steps_up).astype(jnp.int32)])


def touch_ends(values, rng, low, largest):
    extent = values.shape
    place = [jax.random.randint(jax.random.fold_in(rng, axis), (), 0, extent[axis]) for axis in range(len(extent))]
    values = values.at[tuple(place)].set(low)
    longest = extent.index(max(extent))
    place[longest] = (place[longest] + 1) % extent[longest]
    return values.at[tuple(place)].set(largest)


def block_scale(stream_key, extent, cuts, least, largest):
    def one(dim, parts):
        draws = jax.random.uniform(jax.random.fold_in(jax.random.fold_in(stream_key, 6), dim), (parts,), jnp.float32, least / len(cuts), largest / len(cuts))
        return jnp.repeat(jnp.exp(draws), extent[dim] // parts).reshape((-1,) + (1,) * (len(extent) - dim - 1))

    factor_of = one(*cuts[0])
    for cut in cuts[1:]:
        factor_of = factor_of * one(*cut)
    return factor_of


def profile(number_of, total, bound, slope):
    weights = [(1 << 20) // math.isqrt(grade ** slope) + 1 for grade in range(2, number_of + 1)]
    rest, given = total - bound - (number_of - 1), [1] * (number_of - 1)
    while rest > 0:
        candidates = [i for i in range(number_of - 1) if given[i] < bound]
        whole, left = sum([weights[i] for i in candidates]), rest
        for i in candidates:
            addition = min(bound - given[i], max(1, left * weights[i] // whole), rest)
            given[i] = given[i] + addition
            rest = rest - addition
    return np.array([bound] + given)


def uneven(stream_key, amount, total, limit, slope):
    if amount == 2:
        one = jax.random.randint(stream_key, (), max(1, total - limit), min(limit, total - 1) + 1)
        return jnp.stack([one, total - one])
    tallies = jnp.asarray(profile(amount, total, limit, slope), jnp.int32)
    couples = (amount - 1) // 2
    source_of, receiver = tallies[1:1 + 2 * couples:2], tallies[2:2 + 2 * couples:2]
    room = jnp.minimum(source_of - 1, limit - receiver)
    shifted = jax.random.randint(jax.random.fold_in(stream_key, 1), (couples,), 0, 1 << 20) % (room + 1)
    tallies = tallies.at[1:1 + 2 * couples:2].set(source_of - shifted).at[2:2 + 2 * couples:2].set(receiver + shifted)
    return tallies[jax.random.permutation(jax.random.fold_in(stream_key, 2), amount)]


def scatter_about(stream_key, shape, scale, most, shards=(), held_as=jnp.bfloat16):
    drawn = scale * jax.random.normal(stream_key, shape, jnp.float32)
    if shards:
        drawn = drawn * block_scale(stream_key, shape, shards, -0.22, 0.18)
    return jnp.clip(drawn, -most, most).astype(held_as)


def setup_inputs(seed: int = 0) -> dict:
    keys = jax.random.split(jax.random.key(seed), 16)
    return {
        "lineup_embedding": scatter_about(keys[0], (LINEUP_MEMBERS, WINDOW_POSITIONS, LINEUP_FEATURES), 1.0, 6.0, ((0, 64),), jnp.float32),
        "pairwise_state": scatter_about(keys[1], (WINDOW_POSITIONS, WINDOW_POSITIONS, PAIR_CHANNELS), 1.0, 6.0, ((0, 64), (1, 4)), jnp.float32),
        "lineup_scaling_coefficients": jnp.clip(1.0 + 0.18 * jax.random.normal(keys[2], (LINEUP_FEATURES,), jnp.float32), 0.1, 1.9),
        "focus_projection_matrix": scatter_about(keys[3], (4, LINEUP_FEATURES, FOCUS_GROUPS * GROUP_FEATURES), LINEUP_FEATURES ** -0.5, 0.375, ((2, 4),), jnp.float32),
        "attention_gate_bias": scatter_about(keys[4], (FOCUS_GROUPS * GROUP_FEATURES,), 1.0, 4.0, ((0, 4),), jnp.float32),
        "focus_merge_matrix": scatter_about(keys[5], (FOCUS_GROUPS * GROUP_FEATURES, LINEUP_FEATURES), (FOCUS_GROUPS * GROUP_FEATURES) ** -0.5, 0.375, ((0, 4),), jnp.float32),
        "pairwise_bias_weight": scatter_about(keys[6], (PAIR_CHANNELS, FOCUS_GROUPS), PAIR_CHANNELS ** -0.5, 0.5, (), jnp.float32),
        "relative_bias_table": draw_relative_bias_table(jax.random.fold_in(keys[15], 71), 0),
        "tensor_operand_matrices": scatter_about(keys[8], (2, LINEUP_FEATURES, RANK_WIDTH), LINEUP_FEATURES ** -0.5, 0.375, (), jnp.float32),
        "outer_output_weight": scatter_about(keys[9], (RANK_WIDTH * RANK_WIDTH, PAIR_CHANNELS), (8.0 / RANK_WIDTH), 1.5, (), jnp.float32),
        "outer_output_bias": scatter_about(keys[10], (PAIR_CHANNELS,), 1.0, 4.0, (), jnp.float32),
        "lineup_member_flags": touch_ends((jax.random.randint(keys[11], (LINEUP_MEMBERS,), 0, 8) < 7).astype(jnp.int32), jax.random.fold_in(keys[11], 1), 0, 1),
        "residue_presence_mask": touch_ends((jax.random.randint(keys[12], (WINDOW_POSITIONS,), 0, 16) < 15).astype(jnp.int32), jax.random.fold_in(keys[12], 1), 0, 1),
        "chain_label": jnp.searchsorted(jnp.cumsum(uneven(keys[13], 4, WINDOW_POSITIONS, WINDOW_POSITIONS // 2, 0)), jnp.arange(WINDOW_POSITIONS), side="right").astype(jnp.int32),
        "residue_numbering": draw_residue_numbering(jax.random.fold_in(keys[15], 71), 0),
    }


precise_einsum = partial(jnp.einsum, precision=lax.Precision.HIGHEST)

def layer_normalize(values):
    center = values - lax.optimization_barrier(jnp.mean(values, axis=-1, keepdims=True))
    spread = lax.optimization_barrier(jnp.mean(center * center, axis=-1, keepdims=True))
    return center * lax.rsqrt(spread + 1e-05)

def relative_buckets(index_rows, index_cols, chain_rows, chain_cols):
    reach = (BUCKETS - 2) // 2
    offset = jnp.clip(index_rows[:, None] - index_cols[None, :], -reach, reach) + reach
    return jnp.where(chain_rows[:, None] == chain_cols[None, :], offset, BUCKETS - 1)

def bias_block(pair_rows, index_rows, index_cols, chain_rows, chain_cols, pairwise_bias_weight, relative_bias_table):
    normalized_input = layer_normalize(pair_rows)
    linear = precise_einsum('ijc,ch->hij', normalized_input, pairwise_bias_weight)
    buckets = relative_buckets(index_rows, index_cols, chain_rows, chain_cols)
    onehot = (buckets[:, :, None] == jnp.arange(BUCKETS)[None, None, :]).astype(jnp.float32)
    return linear + precise_einsum('ijb,bh->hij', onehot, relative_bias_table)

def row_attention(alignment_row, pairwise_head_bias, key_presence_mask, lineup_scaling_coefficients, focus_projection_matrix, attention_gate_bias):
    normalized_input = layer_normalize(alignment_row) * lineup_scaling_coefficients
    projected_input = precise_einsum('ic,tcf->tif', normalized_input, focus_projection_matrix)
    heads_number = focus_projection_matrix.shape[2] // GROUP_FEATURES
    query_key_value_gate = projected_input.reshape(4, alignment_row.shape[0], heads_number, GROUP_FEATURES)
    logits = precise_einsum('ihd,jhd->hij', query_key_value_gate[0], query_key_value_gate[1]) / math.sqrt(GROUP_FEATURES)
    logits = logits + pairwise_head_bias + key_presence_mask[None, None, :]
    weights = jax.nn.softmax(logits, axis=-1)
    attention_output = precise_einsum('hij,jhd->ihd', weights, query_key_value_gate[2])
    gate_activations = jax.nn.sigmoid(query_key_value_gate[3] + attention_gate_bias.reshape(heads_number, GROUP_FEATURES))
    return (gate_activations * attention_output).reshape(alignment_row.shape[0], heads_number * GROUP_FEATURES)

def outer_factor_pair(alignment_rows, tensor_operand_matrices, row_mask_slice):
    normalized_input = layer_normalize(alignment_rows)
    factors = precise_einsum('sic,tce->tsie', normalized_input, tensor_operand_matrices)
    return (factors[0] * row_mask_slice[..., None], factors[1] * row_mask_slice[..., None])

def reference(lineup_embedding, pairwise_state, lineup_scaling_coefficients, focus_projection_matrix, attention_gate_bias, focus_merge_matrix, pairwise_bias_weight, relative_bias_table, tensor_operand_matrices, outer_output_weight, outer_output_bias, lineup_member_flags, residue_presence_mask, chain_label, residue_numbering):
    batch_extent = 16
    batches_needed = WINDOW_POSITIONS // batch_extent
    pair_blocks = pairwise_state.reshape(batches_needed, batch_extent, WINDOW_POSITIONS, PAIR_CHANNELS)
    index_blocks = residue_numbering.reshape(batches_needed, batch_extent)
    chain_blocks = chain_label.reshape(batches_needed, batch_extent)

    def bias_step(inputs):
        pair_rows, index_rows, chain_rows = inputs
        return bias_block(pair_rows, index_rows, residue_numbering, chain_rows, chain_label, pairwise_bias_weight, relative_bias_table)
    pairwise_head_bias = lax.map(bias_step, (pair_blocks, index_blocks, chain_blocks))
    pairwise_head_bias = jnp.transpose(pairwise_head_bias, (1, 0, 2, 3)).reshape(FOCUS_GROUPS, WINDOW_POSITIONS, WINDOW_POSITIONS)
    residue_count_float = residue_presence_mask.astype(jnp.float32)
    row_count_float = lineup_member_flags.astype(jnp.float32)
    key_presence_mask = (residue_count_float - 1.0) * 1000000000.0
    gated_output = lax.map(lambda alignment_row: row_attention(alignment_row, pairwise_head_bias, key_presence_mask, lineup_scaling_coefficients, focus_projection_matrix, attention_gate_bias), lineup_embedding)
    alignment_state_next = lineup_embedding + precise_einsum('amk,ku->amu', gated_output, focus_merge_matrix)
    first_operand, right_factor = outer_factor_pair(alignment_state_next, tensor_operand_matrices, row_count_float[:, None] * residue_count_float[None, :])
    total_rows = jnp.sum(row_count_float)
    lineup_batches = jnp.transpose(first_operand.reshape(LINEUP_MEMBERS, batches_needed, batch_extent, RANK_WIDTH), (1, 0, 2, 3))

    def outer_step(inputs):
        a_rows, pair_rows, res_rows = inputs
        outer_sum = precise_einsum('sic,sje->ijce', a_rows, right_factor)
        projected_input = precise_einsum('ijf,fz->ijz', outer_sum.reshape(batch_extent, WINDOW_POSITIONS, RANK_WIDTH * RANK_WIDTH), outer_output_weight) + outer_output_bias
        pair_count = res_rows[:, None] * residue_count_float[None, :] * total_rows
        return pair_rows + projected_input / jnp.maximum(pair_count, 1.0)[..., None]
    pairwise_state_next = lax.map(outer_step, (lineup_batches, pair_blocks, residue_count_float.reshape(batches_needed, batch_extent)))
    return (alignment_state_next, pairwise_state_next.reshape(WINDOW_POSITIONS, WINDOW_POSITIONS, PAIR_CHANNELS))
```

```python
import math
from functools import partial

import jax
import jax.numpy as jnp
from jax import lax
from jax.experimental import pallas as pl
from jax.experimental.pallas import tpu as pltpu
from jax.sharding import Mesh, PartitionSpec as P

F32, BF16 = jnp.float32, jnp.bfloat16
HEADS, DEPTH, RANK, BUCKETS = 8, 32, 32, 66
TABLE_ROWS = 72
LANES = 128
LOG2E = math.log2(math.e)
HEAD_AXES = ("xh", "c")
DAP_AXES = ("y", "z", "xl")


def dot(a, b, contract=((1,), (0,))):
    return lax.dot_general(a, b, (contract, ((), ())), preferred_element_type=F32)


def split(a):
    high = a.astype(BF16)
    return high, (a - high.astype(F32)).astype(BF16)


def dot3(a, b, contract=((1,), (0,))):
    return dot(a[0], b[0], contract) + (dot(a[0], b[1], contract) + dot(a[1], b[0], contract))


def normalize(values):
    center = values - jnp.mean(values, axis=-1, keepdims=True)
    spread = jnp.mean(center * center, axis=-1, keepdims=True)
    return center * lax.rsqrt(spread + 1e-05)


def params(n_axes, mib):
    return pltpu.CompilerParams(
        dimension_semantics=("arbitrary",) * n_axes, vmem_limit_bytes=mib * 2**20
    )


def bias_kernel(place, index_s, chain_s, pair, weight_t, table_t, index_c, chain_c, mask_c, out):
    step = pl.program_id(0)
    rows = pair.shape[0]
    columns = pair.shape[1]
    w = weight_t[...]
    table = table_t[...]
    cols_index = index_c[0]
    cols_chain = chain_c[0]
    mask = mask_c[0]
    reach = (BUCKETS - 2) // 2
    for r in range(rows):
        i = place[0] * (rows * pl.num_programs(0)) + step * rows + r
        normed = normalize(pair[r])
        linear = lax.dot_general(
            w, normed, (((1,), (1,)), ((), ())), precision=lax.Precision.HIGHEST,
            preferred_element_type=F32,
        )
        offset = jnp.clip(index_s[i] - cols_index, -reach, reach) + reach
        bucket = jnp.where(chain_s[i] == cols_chain, offset, BUCKETS - 1)
        classes = lax.broadcasted_iota(jnp.int32, (TABLE_ROWS, columns), 0)
        onehot = (classes == bucket).astype(F32)
        relative = lax.dot_general(
            table, onehot, (((1,), (0,)), ((), ())), precision=lax.Precision.HIGHEST,
            preferred_element_type=F32,
        )
        out[:, r, :] = (linear + relative + mask) * LOG2E


def pair_bias(place, numbering, chain, mask_add, pair, weight, table):
    rows, columns, channels = pair.shape
    part = 8
    return pl.pallas_call(
        bias_kernel,
        out_shape=jax.ShapeDtypeStruct((HEADS, rows, columns), F32),
        grid_spec=pltpu.PrefetchScalarGridSpec(
            num_scalar_prefetch=3,
            grid=(rows // part,),
            in_specs=[
                pl.BlockSpec((part, columns, channels), lambda r, *_: (r, 0, 0)),
                pl.BlockSpec((HEADS, channels), lambda r, *_: (0, 0)),
                pl.BlockSpec((HEADS, TABLE_ROWS), lambda r, *_: (0, 0)),
                pl.BlockSpec((1, 1, columns), lambda r, place, *_: (place[1], 0, 0)),
                pl.BlockSpec((1, 1, columns), lambda r, place, *_: (place[1], 0, 0)),
                pl.BlockSpec((1, 1, columns), lambda r, place, *_: (place[1], 0, 0)),
            ],
            out_specs=pl.BlockSpec((HEADS, part, columns), lambda r, *_: (0, r, 0)),
        ),
        compiler_params=params(1, 32),
        name="pair_bias",
    )(
        place, numbering, chain, pair, weight.T,
        jnp.pad(table, ((0, TABLE_ROWS - BUCKETS), (0, 0))).T,
        numbering.reshape(-1, 1, columns), chain.reshape(-1, 1, columns),
        mask_add.reshape(-1, 1, columns),
    )


def project_kernel(place, row, own, gain, wk, wv, wq, wg, gate_bias, kp, vp, qp, gp,
                   wk2, wv2, wq2, wg2):
    @pl.when(pl.program_id(0) == 0)
    def _():
        for source, target in ((wk, wk2), (wv, wv2), (wq, wq2), (wg, wg2)):
            target[0], target[1] = split(source[...])

    positions = row.shape[1]
    own_positions = own.shape[1]
    n = split(normalize(row[0]) * gain[...])
    keys = split(dot3((wk2[0], wk2[1]), n, ((1,), (1,))))
    for h in range(HEADS):
        for part in range(4):
            kp[0, h, pl.ds(part * DEPTH, DEPTH), :] = keys[part % 2][h * DEPTH:(h + 1) * DEPTH]
    pair_lanes = 2 * LANES
    lane = lax.broadcasted_iota(jnp.int32, (positions, LANES), 1)
    for h in range(0, HEADS, 2):
        cut = pl.ds(h * LANES, pair_lanes)
        both = dot3(n, (wv2[0, :, cut], wv2[1, :, cut]))
        for k in range(2):
            value = both[:, k * LANES:(k + 1) * LANES]
            high = value.astype(BF16).astype(F32)
            packed = jnp.where(lane < DEPTH, high, jnp.where(lane < 2 * DEPTH, value - high, 1.0))
            vp[0, h + k] = packed.astype(BF16)
    m = split(normalize(own[0]) * gain[...])
    lane = lax.broadcasted_iota(jnp.int32, (own_positions, LANES), 1)
    for h in range(0, HEADS, 2):
        cut = pl.ds(h * LANES, pair_lanes)
        both = dot3(m, (wq2[0, :, cut], wq2[1, :, cut])) * (LOG2E / math.sqrt(DEPTH))
        gates = dot3(m, (wg2[0, :, cut], wg2[1, :, cut])) + gate_bias[:, cut]
        gates = jax.nn.sigmoid(gates)
        for k in range(2):
            value = both[:, k * LANES:(k + 1) * LANES]
            high = value.astype(BF16).astype(F32)
            qp[0, h + k] = jnp.where(lane < 2 * DEPTH, high, value - high).astype(BF16)
            gp[0, h + k] = gates[:, k * LANES:(k + 1) * LANES]


def project(place, rows, gain, wk, wv, wq, wg, gate_bias, quarter):
    count, positions, channels = rows.shape
    wide = HEADS * LANES

    def whole(shape):
        return pl.BlockSpec(shape, lambda s, place: (0,) * len(shape))

    def out(rows_, columns, dtype):
        return (
            jax.ShapeDtypeStruct((count, HEADS, rows_, columns), dtype),
            pl.BlockSpec((1, HEADS, rows_, columns), lambda s, place: (s, 0, 0, 0)),
        )

    outs = [out(LANES, positions, BF16), out(positions, LANES, BF16),
            out(quarter, LANES, BF16), out(quarter, LANES, F32)]
    return pl.pallas_call(
        project_kernel,
        out_shape=[o[0] for o in outs],
        grid_spec=pltpu.PrefetchScalarGridSpec(
            num_scalar_prefetch=1,
            grid=(count,),
            in_specs=[
                pl.BlockSpec((1, positions, channels), lambda s, place: (s, 0, 0)),
                pl.BlockSpec((1, quarter, channels), lambda s, place: (s, place[1], 0)),
                whole((1, channels)), whole((HEADS * DEPTH, channels)),
                whole((channels, wide)), whole((channels, wide)), whole((channels, wide)),
                whole((1, wide)),
            ],
            out_specs=[o[1] for o in outs],
            scratch_shapes=[pltpu.VMEM((2, HEADS * DEPTH, channels), BF16)]
            + [pltpu.VMEM((2, channels, wide), BF16)] * 3,
        ),
        compiler_params=params(1, 52),
        name="project",
    )(place, rows, rows, gain[None], wk, wv, wq, wg, gate_bias)


def attend_kernel(place, flags_s, bias, kp, vp, qp, gp, merge, own, operand_t, mask_c,
                  state_out, first_out, second_out, total):
    h = pl.program_id(0)
    count = own.shape[0]
    positions = kp.shape[3]
    quarter = own.shape[1]
    cuts = bias.shape[1]
    width = bias.shape[5]
    m2 = split(merge[0])

    @pl.when(h == 0)
    def _():
        total[...] = jnp.zeros_like(total)

    head_bias = jnp.concatenate(
        [bias[:, y, :, 0].reshape(quarter, width) for y in range(cuts)], axis=1
    )
    for s in range(count):
        logits = dot(qp[s, 0], kp[s, 0]) + head_bias
        peak = jnp.max(logits, axis=1, keepdims=True)
        weights = jnp.exp2(logits - peak)
        high, low = split(weights)
        mixed = dot(high, vp[s, 0]) + dot(low, vp[s, 0])
        total_weight = pltpu.roll(mixed, LANES // 2, 1)
        lane = lax.broadcasted_iota(jnp.int32, mixed.shape, 1)
        total_weight = jnp.where(lane < 2 * DEPTH, total_weight, 1.0)
        gated = jnp.where(lane < 2 * DEPTH, mixed * gp[s, 0] / total_weight, 0.0)
        total[s] += dot3(split(gated), m2)

    @pl.when(h == pl.num_programs(0) - 1)
    def _():
        ops = split(operand_t[...])
        for s in range(count):
            state = own[s] + total[s]
            state_out[s] = state
            n = split(normalize(state))
            flag = flags_s[place[0] * count + s].astype(F32)
            factors = dot3(ops, n, ((1,), (1,))) * (mask_c[0] * flag)
            first_out[s] = factors[:RANK]
            for e in range(RANK):
                second_out[pl.ds(s, 1), pl.ds(e * quarter, quarter)] = factors[RANK + e:RANK + e + 1]


def attend(place, flags, bias, kp, vp, qp, gp, merge, rows, operand_t, mask, quarter):
    count, positions, channels = rows.shape
    z, y, xl, heads, i, width = bias.shape

    def head_block(rows_, columns):
        return pl.BlockSpec((count, 1, rows_, columns), lambda h, *_: (0, h, 0, 0))

    return pl.pallas_call(
        attend_kernel,
        out_shape=[
            jax.ShapeDtypeStruct((count, quarter, channels), F32),
            jax.ShapeDtypeStruct((count, RANK, quarter), F32),
            jax.ShapeDtypeStruct((count, RANK * quarter), F32),
        ],
        grid_spec=pltpu.PrefetchScalarGridSpec(
            num_scalar_prefetch=2,
            grid=(HEADS,),
            in_specs=[
                pl.BlockSpec((z, y, xl, 1, i, width), lambda h, *_: (0, 0, 0, h, 0, 0)),
                head_block(LANES, positions), head_block(positions, LANES),
                head_block(quarter, LANES), head_block(quarter, LANES),
                pl.BlockSpec((1, LANES, channels), lambda h, *_: (h, 0, 0)),
                pl.BlockSpec((count, quarter, channels), lambda h, place, *_: (0, place[1], 0)),
                pl.BlockSpec((2 * RANK, channels), lambda h, *_: (0, 0)),
                pl.BlockSpec((1, 1, quarter), lambda h, place, *_: (place[1], 0, 0)),
            ],
            out_specs=[
                pl.BlockSpec((count, quarter, channels), lambda h, *_: (0, 0, 0)),
                pl.BlockSpec((count, RANK, quarter), lambda h, *_: (0, 0, 0)),
                pl.BlockSpec((count, RANK * quarter), lambda h, *_: (0, 0)),
            ],
            scratch_shapes=[pltpu.VMEM((count, quarter, channels), F32)],
        ),
        compiler_params=params(1, 52),
        name="attend",
    )(place, flags, bias, kp, vp, qp, gp, merge, rows, operand_t, mask.reshape(-1, 1, quarter))


def outer_kernel(group, place, mask_s, first, second, weight_t, out_bias, count_c, pair, out,
                 a2, w2, r2):
    step = pl.program_id(0)
    steps = RANK // group
    i_rows = r2.shape[1]
    columns = pair.shape[1]

    @pl.when(step == 0)
    def _():
        high, low = split(first[...].T)
        a2[0], a2[1] = high, low
        high, low = split(weight_t[...])
        w2[:LANES], w2[LANES:] = high, low

    @pl.when(step < steps)
    def _():
        for g in range(group):
            b = split(second[:, g * columns:(g + 1) * columns])
            r = split(dot3((a2[0], a2[1]), b))
            at = pl.multiple_of((step * group + g) * RANK, RANK)
            for part in range(2):
                for i in range(i_rows):
                    r2[part, i, pl.ds(at, RANK), :] = r[part][i * RANK:(i + 1) * RANK]

    @pl.when(step >= steps)
    def _():
        i = step - steps
        both = dot(w2[...], r2[0, i])
        value = both[:LANES] + (both[LANES:] + dot(w2[:LANES], r2[1, i])) + out_bias[...]
        count = jnp.maximum(mask_s[place[0] * i_rows + i].astype(F32) * count_c[0], 1.0)
        out[0] = pair[0] + (value / count).T


def outer_mean(place, mask, first, second, weight_t, out_bias, count, pair):
    rows, columns, channels = pair.shape
    members = first.shape[0]
    group = 4
    steps = RANK // group

    def own(t, *_):
        return (jnp.maximum(t - steps, 0), 0, 0)

    return pl.pallas_call(
        partial(outer_kernel, group),
        out_shape=jax.ShapeDtypeStruct(pair.shape, F32),
        grid_spec=pltpu.PrefetchScalarGridSpec(
            num_scalar_prefetch=2,
            grid=(steps + rows,),
            in_specs=[
                pl.BlockSpec((members, rows * RANK), lambda t, *_: (0, 0)),
                pl.BlockSpec((members, group * columns),
                             lambda t, *_: (0, jnp.minimum(t, steps - 1))),
                pl.BlockSpec((channels, RANK * RANK), lambda t, *_: (0, 0)),
                pl.BlockSpec((channels, 1), lambda t, *_: (0, 0)),
                pl.BlockSpec((1, 1, columns), lambda t, place, *_: (place[1], 0, 0)),
                pl.BlockSpec((1, columns, channels), own),
            ],
            out_specs=pl.BlockSpec((1, columns, channels), own),
            scratch_shapes=[
                pltpu.VMEM((2, rows * RANK, members), BF16),
                pltpu.VMEM((2 * channels, RANK * RANK), BF16),
                pltpu.VMEM((2, rows, RANK * RANK, columns), BF16),
            ],
        ),
        compiler_params=params(1, 52),
        name="outer_mean",
    )(place, mask, first, second, weight_t, out_bias[:, None],
      count.reshape(-1, 1, columns), pair)


def in_order(mine, other):
    low = lax.axis_index("xl") == 0
    return jnp.stack([jnp.where(low, mine, other), jnp.where(low, other, mine)])


def per_device(
    sizes,
    lineup_embedding,
    pairwise_state,
    lineup_scaling_coefficients,
    focus_projection_matrix,
    attention_gate_bias,
    focus_merge_matrix,
    pairwise_bias_weight,
    relative_bias_table,
    tensor_operand_matrices,
    outer_output_weight,
    outer_output_bias,
    lineup_member_flags,
    residue_presence_mask,
    chain_label,
    residue_numbering,
):
    ny, nz, nxl, nxh, nc = (sizes[a] for a in ("y", "z", "xl", "xh", "c"))
    nq = nxh * nc
    dap = (lax.axis_index("y") * nz + lax.axis_index("z")) * nxl + lax.axis_index("xl")
    head = lax.axis_index("xh") * nc + lax.axis_index("c")
    place = jnp.stack([dap, head]).astype(jnp.int32)
    count, positions, channels = lineup_embedding.shape
    block_rows, quarter, pair_channels = pairwise_state.shape
    presence = residue_presence_mask.astype(F32)
    key_mask = (presence - 1.0) * 1000000000.0

    narrow = focus_projection_matrix.shape[2]
    packed = jnp.concatenate(
        [
            focus_projection_matrix.reshape(-1, narrow),
            focus_merge_matrix.reshape(-1, narrow),
            jnp.broadcast_to(attention_gate_bias[None], (8, narrow)),
        ]
    )
    packed = lax.all_gather(packed, HEAD_AXES)
    weights = packed[:, :4 * channels].reshape(nq, 4, channels, narrow)
    weights = jnp.transpose(weights, (1, 2, 0, 3)).reshape(4, channels, HEADS, DEPTH)
    merge = packed[:, 4 * channels:5 * channels].reshape(HEADS, DEPTH, channels)
    gate_bias = packed[:, 5 * channels].reshape(HEADS, DEPTH)

    def lanes(a, copies):
        a = jnp.concatenate([a] * copies, axis=-1)
        a = jnp.pad(a, ((0, 0),) * (a.ndim - 1) + ((0, LANES - a.shape[-1]),))
        return a.reshape(a.shape[:-2] + (HEADS * LANES,))

    wk = weights[1].reshape(channels, HEADS * DEPTH).T
    wq, wv, wg = lanes(weights[0], 4), lanes(weights[2], 2), lanes(weights[3], 2)
    merge = jnp.pad(jnp.concatenate([merge, merge], axis=1), ((0, 0), (0, LANES - 2 * DEPTH), (0, 0)))

    local = pair_bias(place, residue_numbering, chain_label, key_mask, pairwise_state,
                      pairwise_bias_weight, relative_bias_table)

    def swap(flip):
        shape = (ny, nxl, nq)
        perm = []
        for y in range(ny):
            for x in range(nxl):
                for q in range(nq):
                    to = (q * nxl + (x ^ flip)) * nq + y
                    perm.append(((y * nxl + x) * nq + q, to))
        return perm

    cross = ("y", "xl") + HEAD_AXES
    bias = in_order(lax.ppermute(local, cross, swap(0)), lax.ppermute(local, cross, swap(1)))
    bias = lax.all_gather(bias, ("y", "z"))
    bias = jnp.swapaxes(bias.reshape((ny, nz) + bias.shape[1:]), 0, 1)

    kp, vp, qp, gp = project(place, lineup_embedding, lineup_scaling_coefficients, wk, wv, wq, wg,
                             lanes(gate_bias, 2)[None], quarter)
    operand_t = jnp.swapaxes(tensor_operand_matrices, 1, 2).reshape(2 * RANK, channels)
    state, first, second = attend(place, lineup_member_flags, bias, kp, vp, qp, gp, merge,
                                  lineup_embedding, operand_t, presence, quarter)

    flip = [(0, 1), (1, 0)]
    second = in_order(second, lax.ppermute(second, "xl", flip)).reshape(nxl * count, -1)
    second = lax.all_gather(second, ("y", "z")).reshape(ny * nz * nxl * count, -1)

    parts = nz * nxl
    first = jnp.transpose(first.reshape(count, RANK, parts, block_rows), (2, 0, 3, 1))
    first = lax.all_to_all(first.reshape(parts, count, block_rows * RANK), ("z", "xl"), 0, 0, tiled=True)
    first = lax.all_gather(first.reshape(parts * count, -1), "y")
    back = [(y * nq + q, q * nq + y) for y in range(ny) for q in range(nq)]
    first = lax.ppermute(first, ("y",) + HEAD_AXES, back)
    first = first.reshape(ny * parts * count, block_rows * RANK)

    state = lax.all_gather(state, HEAD_AXES, axis=1, tiled=True)

    weight_t = jnp.transpose(
        outer_output_weight.reshape(RANK, RANK, pair_channels), (2, 1, 0)
    ).reshape(pair_channels, RANK * RANK)
    count_columns = presence * jnp.sum(lineup_member_flags.astype(F32))
    pairs = outer_mean(place, residue_presence_mask, first, second, weight_t, outer_output_bias,
                       count_columns, pairwise_state)
    return state, pairs


def solution(mesh):
    sizes = dict(y=4, z=8, xl=2, xh=2, c=2)
    fine = Mesh(mesh.devices.reshape(tuple(sizes.values())), tuple(sizes))
    placed = (
        P(DAP_AXES, None, None),
        P(DAP_AXES, HEAD_AXES, None),
        P(),
        P(None, None, HEAD_AXES),
        P(HEAD_AXES),
        P(HEAD_AXES, None),
    ) + (P(),) * 9
    return jax.shard_map(
        partial(per_device, sizes),
        mesh=fine,
        in_specs=placed,
        out_specs=(P(DAP_AXES, None, None), P(DAP_AXES, HEAD_AXES, None)),
        check_vma=False,
    )
```

```python
import math
from functools import partial

import jax
import jax.numpy as jnp
from jax import lax
from jax.experimental import pallas as pl
from jax.experimental.pallas import tpu as pltpu
from jax.sharding import Mesh, PartitionSpec as P

F32, BF16 = jnp.float32, jnp.bfloat16
HEADS, DEPTH, RANK, BUCKETS = 8, 32, 32, 66
TABLE_ROWS = 72
LANES = 128
LOG2E = math.log2(math.e)
HEAD_AXES = ("xh", "c")
DAP_AXES = ("y", "z", "xl")


def dot(a, b, contract=((1,), (0,))):
    return lax.dot_general(a, b, (contract, ((), ())), preferred_element_type=F32)


def split(a):
    high = a.astype(BF16)
    return high, (a - high.astype(F32)).astype(BF16)


def dot3(a, b, contract=((1,), (0,))):
    return dot(a[0], b[0], contract) + (dot(a[0], b[1], contract) + dot(a[1], b[0], contract))


def normalize(values):
    center = values - jnp.mean(values, axis=-1, keepdims=True)
    spread = jnp.mean(center * center, axis=-1, keepdims=True)
    return center * lax.rsqrt(spread + 1e-05)


def params(n_axes, mib):
    return pltpu.CompilerParams(
        dimension_semantics=("arbitrary",) * n_axes, vmem_limit_bytes=mib * 2**20
    )


def bias_kernel(place, index_s, chain_s, pair, weight_t, table_t, index_c, chain_c, mask_c, out):
    step = pl.program_id(0)
    rows = pair.shape[0]
    columns = pair.shape[1]
    w = weight_t[...]
    table = table_t[...]
    lines = columns // LANES

    def own_columns(ref):
        return jnp.concatenate([ref[pl.ds(place[1] * lines + k, 1), :] for k in range(lines)], axis=1)

    cols_index = own_columns(index_c)
    cols_chain = own_columns(chain_c)
    mask = (own_columns(mask_c).astype(F32) - 1.0) * 1000000000.0
    reach = (BUCKETS - 2) // 2
    for r in range(rows):
        i = place[0] * (rows * pl.num_programs(0)) + step * rows + r
        normed = normalize(pair[r])
        linear = lax.dot_general(
            w, normed, (((1,), (1,)), ((), ())), precision=lax.Precision.HIGHEST,
            preferred_element_type=F32,
        )
        offset = jnp.clip(index_s[i] - cols_index, -reach, reach) + reach
        bucket = jnp.where(chain_s[i] == cols_chain, offset, BUCKETS - 1)
        classes = lax.broadcasted_iota(jnp.int32, (TABLE_ROWS, columns), 0)
        onehot = (classes == bucket).astype(F32)
        relative = lax.dot_general(
            table, onehot, (((1,), (0,)), ((), ())), precision=lax.Precision.HIGHEST,
            preferred_element_type=F32,
        )
        out[:, r, :] = (linear + relative + mask) * LOG2E


def pair_bias(place, numbering, chain, presence, pair, weight, table):
    rows, columns, channels = pair.shape
    part = 8

    def whole(shape):
        return pl.BlockSpec(shape, lambda r, *_: (0,) * len(shape))

    lines = numbering.shape[0] // LANES
    return pl.pallas_call(
        bias_kernel,
        out_shape=jax.ShapeDtypeStruct((HEADS, rows, columns), F32),
        grid_spec=pltpu.PrefetchScalarGridSpec(
            num_scalar_prefetch=3,
            grid=(rows // part,),
            in_specs=[
                pl.BlockSpec((part, columns, channels), lambda r, *_: (r, 0, 0)),
                whole((HEADS, channels)),
                whole((HEADS, TABLE_ROWS)),
            ] + [whole((lines, LANES))] * 3,
            out_specs=pl.BlockSpec((HEADS, part, columns), lambda r, *_: (0, r, 0)),
        ),
        compiler_params=params(1, 32),
        name="pair_bias",
    )(
        place, numbering, chain, pair, weight.T,
        jnp.pad(table, ((0, TABLE_ROWS - BUCKETS), (0, 0))).T,
        numbering.reshape(lines, LANES), chain.reshape(lines, LANES), presence.reshape(lines, LANES),
    )


def project_kernel(place, row, own, gain, wk, wv, wq, wg, gate_bias, kp, vp, qp, gp,
                   wk2, wv2, wq2, wg2):
    @pl.when(pl.program_id(0) == 0)
    def _():
        for source, target in ((wk, wk2), (wv, wv2), (wq, wq2), (wg, wg2)):
            target[0], target[1] = split(source[...])

    positions = row.shape[1]
    own_positions = own.shape[1]
    n = split(normalize(row[0]) * gain[...])
    keys = split(dot3((wk2[0], wk2[1]), n, ((1,), (1,))))
    for h in range(HEADS):
        for part in range(4):
            kp[0, h, pl.ds(part * DEPTH, DEPTH), :] = keys[part % 2][h * DEPTH:(h + 1) * DEPTH]
    pair_lanes = 2 * LANES
    lane = lax.broadcasted_iota(jnp.int32, (positions, LANES), 1)
    for h in range(0, HEADS, 2):
        cut = pl.ds(h * LANES, pair_lanes)
        both = dot3(n, (wv2[0, :, cut], wv2[1, :, cut]))
        for k in range(2):
            value = both[:, k * LANES:(k + 1) * LANES]
            high = value.astype(BF16).astype(F32)
            packed = jnp.where(lane < DEPTH, high, jnp.where(lane < 2 * DEPTH, value - high, 1.0))
            vp[0, h + k] = packed.astype(BF16)
    m = split(normalize(own[0]) * gain[...])
    lane = lax.broadcasted_iota(jnp.int32, (own_positions, LANES), 1)
    for h in range(0, HEADS, 2):
        cut = pl.ds(h * LANES, pair_lanes)
        both = dot3(m, (wq2[0, :, cut], wq2[1, :, cut])) * (LOG2E / math.sqrt(DEPTH))
        gates = dot3(m, (wg2[0, :, cut], wg2[1, :, cut])) + gate_bias[:, cut]
        gates = jax.nn.sigmoid(gates)
        for k in range(2):
            value = both[:, k * LANES:(k + 1) * LANES]
            high = value.astype(BF16).astype(F32)
            qp[0, h + k] = jnp.where(lane < 2 * DEPTH, high, value - high).astype(BF16)
            gp[0, h + k] = gates[:, k * LANES:(k + 1) * LANES]


def project(place, rows, gain, wk, wv, wq, wg, gate_bias, quarter):
    count, positions, channels = rows.shape
    wide = HEADS * LANES

    def whole(shape):
        return pl.BlockSpec(shape, lambda s, place: (0,) * len(shape))

    def out(rows_, columns, dtype):
        return (
            jax.ShapeDtypeStruct((count, HEADS, rows_, columns), dtype),
            pl.BlockSpec((1, HEADS, rows_, columns), lambda s, place: (s, 0, 0, 0)),
        )

    outs = [out(LANES, positions, BF16), out(positions, LANES, BF16),
            out(quarter, LANES, BF16), out(quarter, LANES, F32)]
    return pl.pallas_call(
        project_kernel,
        out_shape=[o[0] for o in outs],
        grid_spec=pltpu.PrefetchScalarGridSpec(
            num_scalar_prefetch=1,
            grid=(count,),
            in_specs=[
                pl.BlockSpec((1, positions, channels), lambda s, place: (s, 0, 0)),
                pl.BlockSpec((1, quarter, channels), lambda s, place: (s, place[1], 0)),
                whole((1, channels)), whole((HEADS * DEPTH, channels)),
                whole((channels, wide)), whole((channels, wide)), whole((channels, wide)),
                whole((1, wide)),
            ],
            out_specs=[o[1] for o in outs],
            scratch_shapes=[pltpu.VMEM((2, HEADS * DEPTH, channels), BF16)]
            + [pltpu.VMEM((2, channels, wide), BF16)] * 3,
        ),
        compiler_params=params(1, 52),
        name="project",
    )(place, rows, rows, gain[None], wk, wv, wq, wg, gate_bias)


def attend_kernel(place, flags_s, bias_a, b0, b1, b2, b3, b4, kp, vp, qp, gp, merge, own, operand_t,
                  mask_c, state_out, first_out, second_out, gated, head_bias):
    h = pl.program_id(0)
    count = own.shape[0]
    quarter = own.shape[1]
    nz, ny, width = bias_a.shape[0], bias_a.shape[1], bias_a.shape[5]
    group = quarter // nz

    def columns(k):
        return pl.ds(pl.multiple_of(lax.rem(place[2] + Y_STEPS[k], ny) * width, width), width)

    def rows(k):
        return pl.ds(pl.multiple_of(lax.rem(place[3] + Z_STEPS[k], nz) * group, group), group)

    @pl.when(h < HEADS // 2)
    def _():
        for k in range(ny):
            head_bias[:, columns(k)] = bias_a[:, k, :, 0].reshape(quarter, width)

    @pl.when(h >= HEADS // 2)
    def _():
        for y, pieces in enumerate(((b0,), (b1,), (b2,), (b3, b4))):
            k = 0
            for piece in pieces:
                for line in range(piece.shape[0]):
                    head_bias[rows(k), columns(y)] = piece[line, :, 0].reshape(group, width)
                    k += 1

    lane = lax.broadcasted_iota(jnp.int32, (quarter, LANES), 1)
    ahead = dot(qp[0, 0], kp[0, 0]) + head_bias[...]
    for s in range(count):
        logits = ahead
        if s + 1 < count:
            ahead = dot(qp[s + 1, 0], kp[s + 1, 0]) + head_bias[...]
        peak = jnp.max(logits, axis=1, keepdims=True)
        weights = jnp.exp2(logits - peak)
        mixed = dot(jnp.concatenate(split(weights), axis=0), vp[s, 0])
        mixed = mixed[:quarter] + mixed[quarter:]
        total_weight = jnp.where(lane < 2 * DEPTH, pltpu.roll(mixed, LANES // 2, 1), 1.0)
        parts = split(jnp.where(lane < 2 * DEPTH, mixed * gp[s, 0] / total_weight, 0.0))
        at = pl.ds(pl.multiple_of(h * LANES, LANES), LANES)
        gated[0, s, :, at], gated[1, s, :, at] = parts

    @pl.when(h == pl.num_programs(0) - 1)
    def _():
        ops = split(operand_t[...])
        m2 = split(merge[...])
        for s in range(count):
            state = own[s] + dot3((gated[0, s], gated[1, s]), m2)
            state_out[s] = state
            n = split(normalize(state))
            flag = flags_s[place[0] * count + s].astype(F32)
            factors = dot3(ops, n, ((1,), (1,))) * (mask_c[0] * flag)
            first_out[s] = factors[:RANK]
            for e in range(RANK):
                second_out[pl.ds(s, 1), pl.ds(e * quarter, quarter)] = factors[RANK + e:RANK + e + 1]


def attend(place, flags, bias, kp, vp, qp, gp, merge, rows, operand_t, mask, quarter):
    count, positions, channels = rows.shape
    half = HEADS // 2

    def piece_block(piece, low, high):
        shape = list(piece.shape)
        shape[-3] = 1

        def at(h, *_):
            index = [0] * len(shape)
            index[-3] = jnp.clip(h - low, 0, high)
            return tuple(index)

        return pl.BlockSpec(tuple(shape), at)

    def head_block(rows_, columns):
        return pl.BlockSpec((count, 1, rows_, columns), lambda h, *_: (0, h, 0, 0))

    return pl.pallas_call(
        attend_kernel,
        out_shape=[
            jax.ShapeDtypeStruct((count, quarter, channels), F32),
            jax.ShapeDtypeStruct((count, RANK, quarter), F32),
            jax.ShapeDtypeStruct((count, RANK * quarter), F32),
        ],
        grid_spec=pltpu.PrefetchScalarGridSpec(
            num_scalar_prefetch=2,
            grid=(HEADS,),
            in_specs=[
                piece_block(bias[0], 0, half - 1),
            ] + [piece_block(piece, half, half - 1) for piece in bias[1]] + [
                head_block(LANES, positions), head_block(positions, LANES),
                head_block(quarter, LANES), head_block(quarter, LANES),
                pl.BlockSpec((HEADS * LANES, channels), lambda h, *_: (0, 0)),
                pl.BlockSpec((count, quarter, channels), lambda h, place, *_: (0, place[1], 0)),
                pl.BlockSpec((2 * RANK, channels), lambda h, *_: (0, 0)),
                pl.BlockSpec((1, 1, quarter), lambda h, place, *_: (place[1], 0, 0)),
            ],
            out_specs=[
                pl.BlockSpec((count, quarter, channels), lambda h, *_: (0, 0, 0)),
                pl.BlockSpec((count, RANK, quarter), lambda h, *_: (0, 0, 0)),
                pl.BlockSpec((count, RANK * quarter), lambda h, *_: (0, 0)),
            ],
            scratch_shapes=[
                pltpu.VMEM((2, count, quarter, HEADS * LANES), BF16),
                pltpu.VMEM((quarter, positions), F32),
            ],
        ),
        compiler_params=params(1, 52),
        name="attend",
    )(place, flags, bias[0], *bias[1], kp, vp, qp, gp, merge, rows, operand_t, mask.reshape(-1, 1, quarter))


def outer_kernel(group, place, mask_s, f0, f1, f2, f3, sa, s0, s1, s2, s3, s4, weight_t, out_bias,
                 count_c, pair, t0, t1, t2, t3, out, state, ordered, moved, a2, w2, r2, sems):
    step = pl.program_id(0)
    steps = RANK // group
    i_rows = r2.shape[1]
    columns = pair.shape[1]
    nz, ny, eight = sa.shape[0], sa.shape[1], sa.shape[2]
    y_at = [lax.rem(place[2] + k, ny) for k in Y_STEPS]
    z_at = [lax.rem(place[3] + k, nz) for k in Z_STEPS]

    quarter = t0.shape[1]

    def state_copy(k, piece):
        at = pl.ds(pl.multiple_of((place[1] ^ k) * quarter, quarter), quarter)
        return pltpu.make_async_copy(piece, state.at[:, at, :], sems.at[k])

    @pl.when(step == 0)
    def _():
        for k, piece in enumerate((t0, t1, t2, t3)):
            state_copy(k, piece).start()

    @pl.when(step == pl.num_programs(0) - 1)
    def _():
        for k, piece in enumerate((t0, t1, t2, t3)):
            state_copy(k, piece).wait()

    def row(y, z):
        return pl.ds(pl.multiple_of((y * nz + z) * eight, eight), eight)

    @pl.when(step == 0)
    def _():
        high, low = split(weight_t[...])
        w2[:LANES], w2[LANES:] = high, low
        for r, piece in enumerate((f0, f1, f2, f3)):
            y = lax.rem(place[1] + (ny - r), ny)
            ordered[pl.ds(pl.multiple_of(y * piece.shape[0], piece.shape[0]), piece.shape[0]), :] = piece[...]
        for z in range(nz):
            for k in range(ny):
                moved[pl.ds((z * ny + k) * eight, eight), :] = ordered[row(y_at[k], z), :]
        a2[0], a2[1] = split(moved[...].T)

    @pl.when(step == steps // 2)
    def _():
        for k in range(ny):
            for z in range(nz):
                moved[pl.ds((k * nz + z) * eight, eight), :] = ordered[row(y_at[k], z_at[z]), :]
        a2[0], a2[1] = split(moved[...].T)

    def products(blocks):
        for g in range(group):
            cut = pl.ds(g * columns, columns)
            b = [block[..., cut].reshape(-1, columns) for block in blocks]
            b = split(b[0] if len(b) == 1 else jnp.concatenate(b, axis=0))
            r = split(dot3((a2[0], a2[1]), b))
            at = pl.multiple_of((step * group + g) * RANK, RANK)
            for part in range(2):
                for i in range(i_rows):
                    r2[part, i, pl.ds(at, RANK), :] = r[part][i * RANK:(i + 1) * RANK]

    @pl.when(step < steps // 2)
    def _():
        products((sa,))

    @pl.when((step >= steps // 2) & (step < steps))
    def _():
        products((s0, s1, s2, s3, s4))

    @pl.when(step >= steps)
    def _():
        for k in range(pair.shape[0]):
            i = (step - steps) * pair.shape[0] + k
            both = dot(w2[...], r2[0, i])
            value = both[:LANES] + (both[LANES:] + dot(w2[:LANES], r2[1, i])) + out_bias[...]
            count = jnp.maximum(mask_s[place[0] * i_rows + i].astype(F32) * count_c[0], 1.0)
            out[k] = pair[k] + (value / count).T


def outer_mean(place, mask, first, second, weight_t, out_bias, count, pair, state):
    rows, columns, channels = pair.shape
    members = sum(piece.shape[0] for piece in first)
    wide = rows * RANK
    group = 8
    steps = RANK // group
    half = steps // 2
    part = 2
    whole_state = (state[0].shape[0], state[0].shape[1] * len(state), state[0].shape[2])

    def own(t, *_):
        return (jnp.maximum(t - steps, 0), 0, 0)

    def whole(shape):
        return pl.BlockSpec(shape, lambda t, *_: (0,) * len(shape))

    def columns_block(piece, low):
        lead = piece.shape[:-1]
        return pl.BlockSpec(
            lead + (group * columns,),
            lambda t, *_: (0,) * len(lead) + (jnp.clip(t - low, 0, half - 1),),
        )

    return pl.pallas_call(
        partial(outer_kernel, group),
        out_shape=[
            jax.ShapeDtypeStruct(pair.shape, F32),
            jax.ShapeDtypeStruct(whole_state, F32),
        ],
        grid_spec=pltpu.PrefetchScalarGridSpec(
            num_scalar_prefetch=2,
            grid=(steps + rows // part,),
            in_specs=[whole(piece.shape) for piece in first]
            + [columns_block(second[0], 0)]
            + [columns_block(piece, half) for piece in second[1]]
            + [
                whole((channels, RANK * RANK)),
                whole((channels, 1)),
                pl.BlockSpec((1, 1, columns), lambda t, place, *_: (place[1], 0, 0)),
                pl.BlockSpec((part, columns, channels), own),
            ] + [pl.BlockSpec(memory_space=pl.ANY)] * len(state),
            out_specs=[
                pl.BlockSpec((part, columns, channels), own),
                pl.BlockSpec(memory_space=pl.ANY),
            ],
            scratch_shapes=[
                pltpu.VMEM((members, wide), F32),
                pltpu.VMEM((members, wide), F32),
                pltpu.VMEM((2, wide, members), BF16),
                pltpu.VMEM((2 * channels, RANK * RANK), BF16),
                pltpu.VMEM((2, rows, RANK * RANK, columns), BF16),
                pltpu.SemaphoreType.DMA((len(state),)),
            ],
        ),
        compiler_params=params(1, 52),
        name="outer_mean",
    )(place, mask, *first, second[0], *second[1], weight_t, out_bias[:, None],
      count.reshape(-1, 1, columns), pair, *state)


Y_STEPS = (0, 3, 1, 2)
Z_STEPS = (0, 7, 1, 6, 2, 5, 3, 4)


def shift(block, axis, size, step):
    return lax.ppermute(block, axis, [(i, (i + step) % size) for i in range(size)])


def gather_y_then_z(block, ny):
    along = [block] + [shift(block, "y", ny, -k) for k in Y_STEPS[1:]]
    return lax.all_gather(jnp.stack(along), "z")


def gather_z(block, nz):
    one = [shift(block, "z", nz, k) for k in (1, -1)]
    two = [shift(block, "z", nz, k) for k in (2, -2)]
    three = [shift(one[0], "z", nz, 2), shift(one[1], "z", nz, -2)]
    cut = block.shape[0] // 2
    four = jnp.concatenate([shift(two[0][:cut], "z", nz, 2), shift(two[1][cut:], "z", nz, -2)])
    return jnp.stack([block] + one + two + three + [four])


def gather_y(block, ny, beside=()):
    one = [shift(block, "y", ny, k) for k in (1, -1)]
    one, beside = lax.optimization_barrier((one, beside))
    cut = block.shape[0] // 2
    two = [shift(one[0][:cut], "y", ny, 1), shift(one[1][cut:], "y", ny, -1)]
    return [block] + one + two, beside


def in_order(mine, other):
    low = lax.axis_index("xl") == 0
    return jnp.stack([jnp.where(low, mine, other), jnp.where(low, other, mine)])


def per_device(
    sizes,
    lineup_embedding,
    pairwise_state,
    lineup_scaling_coefficients,
    focus_projection_matrix,
    attention_gate_bias,
    focus_merge_matrix,
    pairwise_bias_weight,
    relative_bias_table,
    tensor_operand_matrices,
    outer_output_weight,
    outer_output_bias,
    lineup_member_flags,
    residue_presence_mask,
    chain_label,
    residue_numbering,
):
    ny, nz, nxl, nxh, nc = (sizes[a] for a in ("y", "z", "xl", "xh", "c"))
    nq = nxh * nc
    dap = (lax.axis_index("y") * nz + lax.axis_index("z")) * nxl + lax.axis_index("xl")
    head = lax.axis_index("xh") * nc + lax.axis_index("c")
    place = jnp.stack([dap, head, lax.axis_index("y"), lax.axis_index("z")]).astype(jnp.int32)
    count, positions, channels = lineup_embedding.shape
    block_rows, quarter, pair_channels = pairwise_state.shape
    presence = residue_presence_mask.astype(F32)

    narrow = focus_projection_matrix.shape[2]
    packed = jnp.concatenate(
        [
            focus_projection_matrix.reshape(-1, narrow),
            focus_merge_matrix.reshape(-1, narrow),
            jnp.broadcast_to(attention_gate_bias[None], (8, narrow)),
        ]
    )
    packed = lax.all_gather(packed, HEAD_AXES)
    weights = packed[:, :4 * channels].reshape(nq, 4, channels, narrow)
    weights = jnp.transpose(weights, (1, 2, 0, 3)).reshape(4, channels, HEADS, DEPTH)
    merge = packed[:, 4 * channels:5 * channels].reshape(HEADS, DEPTH, channels)
    gate_bias = packed[:, 5 * channels].reshape(HEADS, DEPTH)

    def lanes(a, copies):
        a = jnp.concatenate([a] * copies, axis=-1)
        a = jnp.pad(a, ((0, 0),) * (a.ndim - 1) + ((0, LANES - a.shape[-1]),))
        return a.reshape(a.shape[:-2] + (HEADS * LANES,))

    wk = weights[1].reshape(channels, HEADS * DEPTH).T
    wq, wv, wg = lanes(weights[0], 4), lanes(weights[2], 2), lanes(weights[3], 2)
    merge = jnp.pad(jnp.concatenate([merge, merge], axis=1), ((0, 0), (0, LANES - 2 * DEPTH), (0, 0)))
    merge = merge.reshape(HEADS * LANES, channels)

    local = pair_bias(place, residue_numbering, chain_label, residue_presence_mask, pairwise_state,
                      pairwise_bias_weight, relative_bias_table)

    def swap(flip):
        shape = (ny, nxl, nq)
        perm = []
        for y in range(ny):
            for x in range(nxl):
                for q in range(nq):
                    to = (q * nxl + (x ^ flip)) * nq + y
                    perm.append(((y * nxl + x) * nq + q, to))
        return perm

    cross = ("y", "xl") + HEAD_AXES
    bias = in_order(lax.ppermute(local, cross, swap(0)), lax.ppermute(local, cross, swap(1)))
    half = HEADS // 2
    bias_a = gather_y_then_z(bias[:, :half], ny)
    bias_b = gather_z(bias[:, half:], nz)
    bias_b, rows = lax.optimization_barrier((bias_b, lineup_embedding))
    projected = project(place, rows, lineup_scaling_coefficients, wk, wv, wq, wg,
                        lanes(gate_bias, 2)[None], quarter)
    bias_b, (kp, vp, qp, gp) = gather_y(bias_b, ny, projected)
    bias = (bias_a, bias_b)
    operand_t = jnp.swapaxes(tensor_operand_matrices, 1, 2).reshape(2 * RANK, channels)
    state, first, second = attend(place, lineup_member_flags, bias, kp, vp, qp, gp, merge,
                                  lineup_embedding, operand_t, presence, quarter)

    flip = [(0, 1), (1, 0)]
    second = in_order(second, lax.ppermute(second, "xl", flip)).reshape(nxl * count, -1)
    half = second.shape[1] // 2
    second_a = gather_y_then_z(second[:, :half], ny)
    second_b = gather_z(second[:, half:], nz)
    second_b, first, state = lax.optimization_barrier((second_b, first, state))

    parts = nz * nxl
    first = jnp.transpose(first.reshape(count, RANK, parts, block_rows), (2, 0, 3, 1))
    first = lax.all_to_all(first.reshape(parts, count, block_rows * RANK), ("z", "xl"), 0, 0, tiled=True)
    first = first.reshape(parts * count, -1)
    second_b, first = gather_y(second_b, ny, first)
    second = (second_a, second_b)
    first = [
        lax.ppermute(first, ("y",) + HEAD_AXES,
                     [(y * nq + q, q * nq + (y + r) % nq) for y in range(ny) for q in range(nq)])
        for r in range(nq)
    ]

    pieces = [state, shift(state, "c", nc, 1), shift(state, "xh", nxh, 1)]
    pieces.append(shift(pieces[2], "c", nc, 1))

    weight_t = jnp.transpose(
        outer_output_weight.reshape(RANK, RANK, pair_channels), (2, 1, 0)
    ).reshape(pair_channels, RANK * RANK)
    count_columns = presence * jnp.sum(lineup_member_flags.astype(F32))
    pairs, state = outer_mean(place, residue_presence_mask, first, second, weight_t,
                              outer_output_bias, count_columns, pairwise_state, pieces)
    return state, pairs


def solution(mesh):
    sizes = dict(y=4, z=8, xl=2, xh=2, c=2)
    fine = Mesh(mesh.devices.reshape(tuple(sizes.values())), tuple(sizes))
    placed = (
        P(DAP_AXES, None, None),
        P(DAP_AXES, HEAD_AXES, None),
        P(),
        P(None, None, HEAD_AXES),
        P(HEAD_AXES),
        P(HEAD_AXES, None),
    ) + (P(),) * 9
    return jax.shard_map(
        partial(per_device, sizes),
        mesh=fine,
        in_specs=placed,
        out_specs=(P(DAP_AXES, None, None), P(DAP_AXES, HEAD_AXES, None)),
        check_vma=False,
    )
```

```python
import math
from functools import partial

import jax
import jax.numpy as jnp
from jax import lax
from jax.experimental import pallas as pl
from jax.experimental.pallas import tpu as pltpu
from jax.sharding import Mesh, PartitionSpec as P

F32, BF16 = jnp.float32, jnp.bfloat16
HEADS, DEPTH, RANK, BUCKETS = 8, 32, 32, 66
TABLE_ROWS = 72
LANES = 128
LOG2E = math.log2(math.e)
HEAD_AXES = ("xh", "c")
DAP_AXES = ("y", "z", "xl")


def dot(a, b, contract=((1,), (0,))):
    return lax.dot_general(a, b, (contract, ((), ())), preferred_element_type=F32)


def split(a):
    high = a.astype(BF16)
    return high, (a - high.astype(F32)).astype(BF16)


def dot3(a, b, contract=((1,), (0,))):
    return dot(a[0], b[0], contract) + (dot(a[0], b[1], contract) + dot(a[1], b[0], contract))


def normalize(values):
    center = values - jnp.mean(values, axis=-1, keepdims=True)
    spread = jnp.mean(center * center, axis=-1, keepdims=True)
    return center * lax.rsqrt(spread + 1e-05)


def params(n_axes, mib):
    return pltpu.CompilerParams(
        dimension_semantics=("arbitrary",) * n_axes, vmem_limit_bytes=mib * 2**20
    )


def bias_kernel(place, index_s, chain_s, pair, weight_t, table_t, index_c, chain_c, mask_c, out):
    step = pl.program_id(0)
    rows = pair.shape[0]
    columns = pair.shape[1]
    w = weight_t[...]
    table = table_t[...]
    lines = columns // LANES

    def own_columns(ref):
        return jnp.concatenate([ref[pl.ds(place[1] * lines + k, 1), :] for k in range(lines)], axis=1)

    cols_index = own_columns(index_c)
    cols_chain = own_columns(chain_c)
    mask = (own_columns(mask_c).astype(F32) - 1.0) * 1000000000.0
    reach = (BUCKETS - 2) // 2
    for r in range(rows):
        i = place[0] * (rows * pl.num_programs(0)) + step * rows + r
        normed = normalize(pair[r])
        linear = lax.dot_general(
            w, normed, (((1,), (1,)), ((), ())), precision=lax.Precision.HIGHEST,
            preferred_element_type=F32,
        )
        offset = jnp.clip(index_s[i] - cols_index, -reach, reach) + reach
        bucket = jnp.where(chain_s[i] == cols_chain, offset, BUCKETS - 1)
        classes = lax.broadcasted_iota(jnp.int32, (TABLE_ROWS, columns), 0)
        onehot = (classes == bucket).astype(F32)
        relative = lax.dot_general(
            table, onehot, (((1,), (0,)), ((), ())), precision=lax.Precision.HIGHEST,
            preferred_element_type=F32,
        )
        out[:, r, :] = (linear + relative + mask) * LOG2E


def pair_bias(place, numbering, chain, presence, pair, weight, table):
    rows, columns, channels = pair.shape
    part = 8

    def whole(shape):
        return pl.BlockSpec(shape, lambda r, *_: (0,) * len(shape))

    lines = numbering.shape[0] // LANES
    return pl.pallas_call(
        bias_kernel,
        out_shape=jax.ShapeDtypeStruct((HEADS, rows, columns), F32),
        grid_spec=pltpu.PrefetchScalarGridSpec(
            num_scalar_prefetch=3,
            grid=(rows // part,),
            in_specs=[
                pl.BlockSpec((part, columns, channels), lambda r, *_: (r, 0, 0)),
                whole((HEADS, channels)),
                whole((HEADS, TABLE_ROWS)),
            ] + [whole((lines, LANES))] * 3,
            out_specs=pl.BlockSpec((HEADS, part, columns), lambda r, *_: (0, r, 0)),
        ),
        compiler_params=params(1, 32),
        name="pair_bias",
    )(
        place, numbering, chain, pair, weight.T,
        jnp.pad(table, ((0, TABLE_ROWS - BUCKETS), (0, 0))).T,
        numbering.reshape(lines, LANES), chain.reshape(lines, LANES), presence.reshape(lines, LANES),
    )


def project_kernel(place, row, own, gain, wk, wv, wq, wg, gate_bias, kp, vp, qp, gp,
                   wk2, wv2, wq2, wg2):
    @pl.when(pl.program_id(0) == 0)
    def _():
        for source, target in ((wk, wk2), (wv, wv2), (wq, wq2), (wg, wg2)):
            target[0], target[1] = split(source[...])

    positions = row.shape[1]
    own_positions = own.shape[1]
    n = split(normalize(row[0]) * gain[...])
    keys = split(dot3((wk2[0], wk2[1]), n, ((1,), (1,))))
    for h in range(HEADS):
        for part in range(4):
            kp[0, h, pl.ds(part * DEPTH, DEPTH), :] = keys[part % 2][h * DEPTH:(h + 1) * DEPTH]
    pair_lanes = 2 * LANES
    lane = lax.broadcasted_iota(jnp.int32, (positions, LANES), 1)
    for h in range(0, HEADS, 2):
        cut = pl.ds(h * LANES, pair_lanes)
        both = dot3(n, (wv2[0, :, cut], wv2[1, :, cut]))
        for k in range(2):
            value = both[:, k * LANES:(k + 1) * LANES]
            high = value.astype(BF16).astype(F32)
            packed = jnp.where(lane < DEPTH, high, jnp.where(lane < 2 * DEPTH, value - high, 1.0))
            vp[0, h + k] = packed.astype(BF16)
    m = split(normalize(own[0]) * gain[...])
    lane = lax.broadcasted_iota(jnp.int32, (own_positions, LANES), 1)
    for h in range(0, HEADS, 2):
        cut = pl.ds(h * LANES, pair_lanes)
        both = dot3(m, (wq2[0, :, cut], wq2[1, :, cut])) * (LOG2E / math.sqrt(DEPTH))
        gates = dot3(m, (wg2[0, :, cut], wg2[1, :, cut])) + gate_bias[:, cut]
        gates = jax.nn.sigmoid(gates)
        for k in range(2):
            value = both[:, k * LANES:(k + 1) * LANES]
            high = value.astype(BF16).astype(F32)
            qp[0, h + k] = jnp.where(lane < 2 * DEPTH, high, value - high).astype(BF16)
            gp[0, h + k] = gates[:, k * LANES:(k + 1) * LANES]


def project(place, rows, gain, wk, wv, wq, wg, gate_bias, quarter):
    count, positions, channels = rows.shape
    wide = HEADS * LANES

    def whole(shape):
        return pl.BlockSpec(shape, lambda s, place: (0,) * len(shape))

    def out(rows_, columns, dtype):
        return (
            jax.ShapeDtypeStruct((count, HEADS, rows_, columns), dtype),
            pl.BlockSpec((1, HEADS, rows_, columns), lambda s, place: (s, 0, 0, 0)),
        )

    outs = [out(LANES, positions, BF16), out(positions, LANES, BF16),
            out(quarter, LANES, BF16), out(quarter, LANES, F32)]
    return pl.pallas_call(
        project_kernel,
        out_shape=[o[0] for o in outs],
        grid_spec=pltpu.PrefetchScalarGridSpec(
            num_scalar_prefetch=1,
            grid=(count,),
            in_specs=[
                pl.BlockSpec((1, positions, channels), lambda s, place: (s, 0, 0)),
                pl.BlockSpec((1, quarter, channels), lambda s, place: (s, place[1], 0)),
                whole((1, channels)), whole((HEADS * DEPTH, channels)),
                whole((channels, wide)), whole((channels, wide)), whole((channels, wide)),
                whole((1, wide)),
            ],
            out_specs=[o[1] for o in outs],
            scratch_shapes=[pltpu.VMEM((2, HEADS * DEPTH, channels), BF16)]
            + [pltpu.VMEM((2, channels, wide), BF16)] * 3,
        ),
        compiler_params=params(1, 52),
        name="project",
    )(place, rows, rows, gain[None], wk, wv, wq, wg, gate_bias)


def attend_kernel(place, flags_s, bias_a, b0, b1, b2, b3, b4, kp, vp, qp, gp, merge, own, operand_t,
                  mask_c, state_out, first_out, second_out, gated, head_bias):
    h = pl.program_id(0)
    count = own.shape[0]
    quarter = own.shape[1]
    nz, ny, width = bias_a.shape[0], bias_a.shape[1], bias_a.shape[5]
    group = quarter // nz

    def columns(k):
        return pl.ds(pl.multiple_of(lax.rem(place[2] + Y_STEPS[k], ny) * width, width), width)

    def rows(k):
        return pl.ds(pl.multiple_of(lax.rem(place[3] + Z_STEPS[k], nz) * group, group), group)

    @pl.when(h < HEADS // 2)
    def _():
        for k in range(ny):
            head_bias[:, columns(k)] = bias_a[:, k, :, 0].reshape(quarter, width)

    @pl.when(h >= HEADS // 2)
    def _():
        for y, pieces in enumerate(((b0,), (b1,), (b2,), (b3, b4))):
            k = 0
            for piece in pieces:
                for line in range(piece.shape[0]):
                    head_bias[rows(k), columns(y)] = piece[line, :, 0].reshape(group, width)
                    k += 1

    lane = lax.broadcasted_iota(jnp.int32, (quarter, LANES), 1)
    ahead = dot(qp[0, 0], kp[0, 0]) + head_bias[...]
    for s in range(count):
        logits = ahead
        if s + 1 < count:
            ahead = dot(qp[s + 1, 0], kp[s + 1, 0]) + head_bias[...]
        peak = jnp.max(logits, axis=1, keepdims=True)
        weights = jnp.exp2(logits - peak)
        mixed = dot(jnp.concatenate(split(weights), axis=0), vp[s, 0])
        mixed = mixed[:quarter] + mixed[quarter:]
        total_weight = jnp.where(lane < 2 * DEPTH, pltpu.roll(mixed, LANES // 2, 1), 1.0)
        parts = split(jnp.where(lane < 2 * DEPTH, mixed * gp[s, 0] / total_weight, 0.0))
        at = pl.ds(pl.multiple_of(h * LANES, LANES), LANES)
        gated[0, s, :, at], gated[1, s, :, at] = parts

    @pl.when(h == pl.num_programs(0) - 1)
    def _():
        ops = split(operand_t[...])
        m2 = split(merge[...])
        for s in range(count):
            state = own[s] + dot3((gated[0, s], gated[1, s]), m2)
            state_out[s] = state
            n = split(normalize(state))
            flag = flags_s[place[0] * count + s].astype(F32)
            factors = dot3(ops, n, ((1,), (1,))) * (mask_c[0] * flag)
            first_out[s] = factors[:RANK]
            for e in range(RANK):
                second_out[pl.ds(s, 1), pl.ds(e * quarter, quarter)] = factors[RANK + e:RANK + e + 1]


def attend(place, flags, bias, kp, vp, qp, gp, merge, rows, operand_t, mask, quarter):
    count, positions, channels = rows.shape
    half = HEADS // 2

    def piece_block(piece, low, high):
        shape = list(piece.shape)
        shape[-3] = 1

        def at(h, *_):
            index = [0] * len(shape)
            index[-3] = jnp.clip(h - low, 0, high)
            return tuple(index)

        return pl.BlockSpec(tuple(shape), at)

    def head_block(rows_, columns):
        return pl.BlockSpec((count, 1, rows_, columns), lambda h, *_: (0, h, 0, 0))

    return pl.pallas_call(
        attend_kernel,
        out_shape=[
            jax.ShapeDtypeStruct((count, quarter, channels), F32),
            jax.ShapeDtypeStruct((count, RANK, quarter), F32),
            jax.ShapeDtypeStruct((count, RANK * quarter), F32),
        ],
        grid_spec=pltpu.PrefetchScalarGridSpec(
            num_scalar_prefetch=2,
            grid=(HEADS,),
            in_specs=[
                piece_block(bias[0], 0, half - 1),
            ] + [piece_block(piece, half, half - 1) for piece in bias[1]] + [
                head_block(LANES, positions), head_block(positions, LANES),
                head_block(quarter, LANES), head_block(quarter, LANES),
                pl.BlockSpec((HEADS * LANES, channels), lambda h, *_: (0, 0)),
                pl.BlockSpec((count, quarter, channels), lambda h, place, *_: (0, place[1], 0)),
                pl.BlockSpec((2 * RANK, channels), lambda h, *_: (0, 0)),
                pl.BlockSpec((1, 1, quarter), lambda h, place, *_: (place[1], 0, 0)),
            ],
            out_specs=[
                pl.BlockSpec((count, quarter, channels), lambda h, *_: (0, 0, 0)),
                pl.BlockSpec((count, RANK, quarter), lambda h, *_: (0, 0, 0)),
                pl.BlockSpec((count, RANK * quarter), lambda h, *_: (0, 0)),
            ],
            scratch_shapes=[
                pltpu.VMEM((2, count, quarter, HEADS * LANES), BF16),
                pltpu.VMEM((quarter, positions), F32),
            ],
        ),
        compiler_params=params(1, 52),
        name="attend",
    )(place, flags, bias[0], *bias[1], kp, vp, qp, gp, merge, rows, operand_t, mask.reshape(-1, 1, quarter))


def outer_kernel(group, place, mask_s, f0, f1, f2, f3, sa, s0, s1, s2, s3, s4, weight_t, out_bias,
                 count_c, pair, t0, t1, t2, t3, out, state, ordered, moved, a2, w2, r2):
    step = pl.program_id(0)
    steps = RANK // group
    i_rows = r2.shape[1]
    columns = pair.shape[1]
    nz, ny, eight = sa.shape[0], sa.shape[1], sa.shape[2]
    y_at = [lax.rem(place[2] + k, ny) for k in Y_STEPS]
    z_at = [lax.rem(place[3] + k, nz) for k in Z_STEPS]

    def row(y, z):
        return pl.ds(pl.multiple_of((y * nz + z) * eight, eight), eight)

    @pl.when(step == 0)
    def _():
        high, low = split(weight_t[...])
        w2[:LANES], w2[LANES:] = high, low
        for r, piece in enumerate((f0, f1, f2, f3)):
            y = lax.rem((place[1] ^ (r // 2)) + 2 * (r % 2), ny)
            ordered[pl.ds(pl.multiple_of(y * piece.shape[0], piece.shape[0]), piece.shape[0]), :] = piece[...]
        for z in range(nz):
            for k in range(ny):
                moved[pl.ds((z * ny + k) * eight, eight), :] = ordered[row(y_at[k], z), :]
        a2[0], a2[1] = split(moved[...].T)

    @pl.when(step == steps // 2)
    def _():
        for k in range(ny):
            for z in range(nz):
                moved[pl.ds((k * nz + z) * eight, eight), :] = ordered[row(y_at[k], z_at[z]), :]
        a2[0], a2[1] = split(moved[...].T)

    def products(blocks):
        for g in range(group):
            cut = pl.ds(g * columns, columns)
            b = [block[..., cut].reshape(-1, columns) for block in blocks]
            b = split(b[0] if len(b) == 1 else jnp.concatenate(b, axis=0))
            r = split(dot3((a2[0], a2[1]), b))
            at = pl.multiple_of((step * group + g) * RANK, RANK)
            for part in range(2):
                for i in range(i_rows):
                    r2[part, i, pl.ds(at, RANK), :] = r[part][i * RANK:(i + 1) * RANK]

    @pl.when(step < steps // 2)
    def _():
        products((sa,))

    @pl.when((step >= steps // 2) & (step < steps))
    def _():
        products((s0, s1, s2, s3, s4))

    @pl.when(step >= steps)
    def _():
        for k in range(pair.shape[0]):
            i = (step - steps) * pair.shape[0] + k
            both = dot(w2[...], r2[0, i])
            value = both[:LANES] + (both[LANES:] + dot(w2[:LANES], r2[1, i])) + out_bias[...]
            count = jnp.maximum(mask_s[place[0] * i_rows + i].astype(F32) * count_c[0], 1.0)
            out[k] = pair[k] + (value / count).T
        for k, piece in enumerate((t0, t1, t2, t3)):
            @pl.when((step - steps) // 2 == k)
            def _(piece=piece):
                state[...] = piece[...]


def outer_mean(place, mask, first, second, weight_t, out_bias, count, pair, state):
    rows, columns, channels = pair.shape
    members = sum(piece.shape[0] for piece in first)
    wide = rows * RANK
    group = 8
    steps = RANK // group
    half = steps // 2
    part = 2
    count_s, quarter, features = state[0].shape
    lines = count_s // 2
    whole_state = (count_s, quarter * len(state), features)

    def state_block(t, place, *_):
        at = jnp.clip(t - steps, 0, 2 * len(state) - 1)
        return (lax.rem(at, 2), place[1] ^ (at // 2), 0)

    def own(t, *_):
        return (jnp.maximum(t - steps, 0), 0, 0)

    def whole(shape):
        return pl.BlockSpec(shape, lambda t, *_: (0,) * len(shape))

    def columns_block(piece, low):
        lead = piece.shape[:-1]
        return pl.BlockSpec(
            lead + (group * columns,),
            lambda t, *_: (0,) * len(lead) + (jnp.clip(t - low, 0, half - 1),),
        )

    return pl.pallas_call(
        partial(outer_kernel, group),
        out_shape=[
            jax.ShapeDtypeStruct(pair.shape, F32),
            jax.ShapeDtypeStruct(whole_state, F32),
        ],
        grid_spec=pltpu.PrefetchScalarGridSpec(
            num_scalar_prefetch=2,
            grid=(steps + rows // part,),
            in_specs=[whole(piece.shape) for piece in first]
            + [columns_block(second[0], 0)]
            + [columns_block(piece, half) for piece in second[1]]
            + [
                whole((channels, RANK * RANK)),
                whole((channels, 1)),
                pl.BlockSpec((1, 1, columns), lambda t, place, *_: (place[1], 0, 0)),
                pl.BlockSpec((part, columns, channels), own),
            ] + [
                pl.BlockSpec((lines, quarter, features),
                             lambda t, *_, k=k: (jnp.clip(t - steps - 2 * k, 0, 1), 0, 0))
                for k in range(len(state))
            ],
            out_specs=[pl.BlockSpec((part, columns, channels), own),
                       pl.BlockSpec((lines, quarter, features), state_block)],
            scratch_shapes=[
                pltpu.VMEM((members, wide), F32),
                pltpu.VMEM((members, wide), F32),
                pltpu.VMEM((2, wide, members), BF16),
                pltpu.VMEM((2 * channels, RANK * RANK), BF16),
                pltpu.VMEM((2, rows, RANK * RANK, columns), BF16),
            ],
        ),
        compiler_params=params(1, 52),
        name="outer_mean",
    )(place, mask, *first, second[0], *second[1], weight_t, out_bias[:, None],
      count.reshape(-1, 1, columns), pair, *state)


Y_STEPS = (0, 3, 1, 2)
Z_STEPS = (0, 7, 1, 6, 2, 5, 3, 4)


def shift(block, axis, size, step):
    return lax.ppermute(block, axis, [(i, (i + step) % size) for i in range(size)])


def gather_z(block, nz):
    one = [shift(block, "z", nz, k) for k in (1, -1)]
    two = [shift(block, "z", nz, k) for k in (2, -2)]
    three = [shift(one[0], "z", nz, 2), shift(one[1], "z", nz, -2)]
    cut = block.shape[0] // 2
    four = jnp.concatenate([shift(two[0][:cut], "z", nz, 2), shift(two[1][cut:], "z", nz, -2)])
    return jnp.stack([block] + one + two + three + [four])


def gather_y(block, ny, beside=()):
    one = [shift(block, "y", ny, k) for k in (1, -1)]
    one, beside = lax.optimization_barrier((one, beside))
    cut = block.shape[0] // 2
    two = [shift(one[0][:cut], "y", ny, 1), shift(one[1][cut:], "y", ny, -1)]
    return [block] + one + two, beside


def in_order(mine, other, axis=0):
    low = lax.axis_index("xl") == 0
    return jnp.stack([jnp.where(low, mine, other), jnp.where(low, other, mine)], axis)


def per_device(
    sizes,
    lineup_embedding,
    pairwise_state,
    lineup_scaling_coefficients,
    focus_projection_matrix,
    attention_gate_bias,
    focus_merge_matrix,
    pairwise_bias_weight,
    relative_bias_table,
    tensor_operand_matrices,
    outer_output_weight,
    outer_output_bias,
    lineup_member_flags,
    residue_presence_mask,
    chain_label,
    residue_numbering,
):
    ny, nz, nxl, nxh, nc = (sizes[a] for a in ("y", "z", "xl", "xh", "c"))
    nq = nxh * nc
    dap = (lax.axis_index("y") * nz + lax.axis_index("z")) * nxl + lax.axis_index("xl")
    head = lax.axis_index("xh") * nc + lax.axis_index("c")
    place = jnp.stack([dap, head, lax.axis_index("y"), lax.axis_index("z")]).astype(jnp.int32)
    count, positions, channels = lineup_embedding.shape
    block_rows, quarter, pair_channels = pairwise_state.shape
    presence = residue_presence_mask.astype(F32)

    narrow = focus_projection_matrix.shape[2]
    packed = jnp.concatenate(
        [
            focus_projection_matrix.reshape(-1, narrow),
            focus_merge_matrix.reshape(-1, narrow),
            jnp.broadcast_to(attention_gate_bias[None], (8, narrow)),
        ]
    )
    packed = lax.all_gather(packed, HEAD_AXES)
    weights = packed[:, :4 * channels].reshape(nq, 4, channels, narrow)
    weights = jnp.transpose(weights, (1, 2, 0, 3)).reshape(4, channels, HEADS, DEPTH)
    merge = packed[:, 4 * channels:5 * channels].reshape(HEADS, DEPTH, channels)
    gate_bias = packed[:, 5 * channels].reshape(HEADS, DEPTH)

    def lanes(a, copies):
        a = jnp.concatenate([a] * copies, axis=-1)
        a = jnp.pad(a, ((0, 0),) * (a.ndim - 1) + ((0, LANES - a.shape[-1]),))
        return a.reshape(a.shape[:-2] + (HEADS * LANES,))

    wk = weights[1].reshape(channels, HEADS * DEPTH).T
    wq, wv, wg = lanes(weights[0], 4), lanes(weights[2], 2), lanes(weights[3], 2)
    merge = jnp.pad(jnp.concatenate([merge, merge], axis=1), ((0, 0), (0, LANES - 2 * DEPTH), (0, 0)))
    merge = merge.reshape(HEADS * LANES, channels)

    local = pair_bias(place, residue_numbering, chain_label, residue_presence_mask, pairwise_state,
                      pairwise_bias_weight, relative_bias_table)

    def spread(block, flip, step):
        perm = []
        for y in range(ny):
            for x in range(nxl):
                for q in range(nq):
                    to = (((q - step) % ny) * nxl + (x ^ flip)) * nq + y
                    perm.append(((y * nxl + x) * nq + q, to))
        return lax.ppermute(block, ("y", "xl") + HEAD_AXES, perm)

    half = HEADS // 2
    bias_b = in_order(*(spread(local[half:], flip, 0) for flip in range(nxl)))
    bias_a = in_order(*(jnp.stack([spread(local[:half], flip, k) for k in Y_STEPS])
                        for flip in range(nxl)), axis=1)
    bias_a = lax.all_gather(bias_a, "z")
    bias_b = gather_z(bias_b, nz)
    gate_bias = lanes(gate_bias, 2)[None]
    bias_b, rows, wk, wv, wq, wg, gate_bias = lax.optimization_barrier(
        (bias_b, lineup_embedding, wk, wv, wq, wg, gate_bias)
    )
    projected = project(place, rows, lineup_scaling_coefficients, wk, wv, wq, wg,
                        gate_bias, quarter)
    bias_b, (kp, vp, qp, gp) = gather_y(bias_b, ny, projected)
    bias = (bias_a, bias_b)
    operand_t = jnp.swapaxes(tensor_operand_matrices, 1, 2).reshape(2 * RANK, channels)
    state, first, second = attend(place, lineup_member_flags, bias, kp, vp, qp, gp, merge,
                                  lineup_embedding, operand_t, presence, quarter)

    def across(block, step):
        perm = [(y * nxl + x, (y - step) % ny * nxl + (x ^ 1)) for y in range(ny) for x in range(nxl)]
        return lax.ppermute(block, ("y", "xl"), perm)

    half = second.shape[1] // 2
    second_b = in_order(second[:, half:], across(second[:, half:], 0)).reshape(nxl * count, -1)
    mine = [second[:, :half]] + [shift(second[:, :half], "y", ny, -k) for k in Y_STEPS[1:]]
    other = [across(second[:, :half], k) for k in Y_STEPS]
    second_a = in_order(jnp.stack(mine), jnp.stack(other), axis=1).reshape(ny, nxl * count, -1)
    second_a = lax.all_gather(second_a, "z")
    second_b = gather_z(second_b, nz)
    second_b, first, state = lax.optimization_barrier((second_b, first, state))

    parts = nz * nxl
    first = jnp.transpose(first.reshape(count, RANK, parts, block_rows), (2, 0, 3, 1))
    first = lax.all_to_all(first.reshape(parts, count, block_rows * RANK), ("z", "xl"), 0, 0, tiled=True)
    first = first.reshape(parts * count, -1)
    first = [
        lax.ppermute(first, ("y",) + HEAD_AXES,
                     [(y * nq + q, q * nq + (y + r) % nq) for y in range(ny) for q in range(nq)])
        for r in (0, 2)
    ]

    pieces = [state, shift(state, "c", nc, 1), shift(state, "xh", nxh, 1)]
    second_b, (first, pieces) = gather_y(second_b, ny, (first, pieces))
    second = (second_a, second_b)
    first = first + [shift(piece, "c", nc, 1) for piece in first]
    pieces = pieces + [shift(pieces[2], "c", nc, 1)]

    weight_t = jnp.transpose(
        outer_output_weight.reshape(RANK, RANK, pair_channels), (2, 1, 0)
    ).reshape(pair_channels, RANK * RANK)
    count_columns = presence * jnp.sum(lineup_member_flags.astype(F32))
    pairs, state = outer_mean(place, residue_presence_mask, first, second, weight_t,
                              outer_output_bias, count_columns, pairwise_state, pieces)
    return state, pairs


def solution(mesh):
    sizes = dict(y=4, z=8, xl=2, xh=2, c=2)
    fine = Mesh(mesh.devices.reshape(tuple(sizes.values())), tuple(sizes))
    placed = (
        P(DAP_AXES, None, None),
        P(DAP_AXES, HEAD_AXES, None),
        P(),
        P(None, None, HEAD_AXES),
        P(HEAD_AXES),
        P(HEAD_AXES, None),
    ) + (P(),) * 9
    return jax.shard_map(
        partial(per_device, sizes),
        mesh=fine,
        in_specs=placed,
        out_specs=(P(DAP_AXES, None, None), P(DAP_AXES, HEAD_AXES, None)),
        check_vma=False,
    )
```

```python
import math
from functools import partial

import jax
import jax.numpy as jnp
from jax import lax
from jax.experimental import pallas as pl
from jax.experimental.pallas import tpu as pltpu
from jax.sharding import Mesh, PartitionSpec as P

F32, BF16 = jnp.float32, jnp.bfloat16
HEADS, DEPTH, RANK, BUCKETS = 8, 32, 32, 66
HEADS_A = 3
TABLE_ROWS = 72
LANES = 128
LOG2E = math.log2(math.e)
HEAD_AXES = ("xh", "c")
DAP_AXES = ("y", "z", "xl")


def dot(a, b, contract=((1,), (0,))):
    return lax.dot_general(a, b, (contract, ((), ())), preferred_element_type=F32)


def split(a):
    high = a.astype(BF16)
    return high, (a - high.astype(F32)).astype(BF16)


def dot3(a, b, contract=((1,), (0,))):
    return dot(a[0], b[0], contract) + (dot(a[0], b[1], contract) + dot(a[1], b[0], contract))


def normalize(values):
    center = values - jnp.mean(values, axis=-1, keepdims=True)
    spread = jnp.mean(center * center, axis=-1, keepdims=True)
    return center * lax.rsqrt(spread + 1e-05)


def params(n_axes, mib):
    return pltpu.CompilerParams(
        dimension_semantics=("arbitrary",) * n_axes, vmem_limit_bytes=mib * 2**20
    )


def bias_kernel(place, index_s, chain_s, pair, weight_t, table_t, index_c, chain_c, mask_c, out):
    step = pl.program_id(0)
    rows = pair.shape[0]
    columns = pair.shape[1]
    w = weight_t[...]
    table = table_t[...]
    lines = columns // LANES

    def own_columns(ref):
        return jnp.concatenate([ref[pl.ds(place[1] * lines + k, 1), :] for k in range(lines)], axis=1)

    cols_index = own_columns(index_c)
    cols_chain = own_columns(chain_c)
    mask = (own_columns(mask_c).astype(F32) - 1.0) * 1000000000.0
    reach = (BUCKETS - 2) // 2
    for r in range(rows):
        i = place[0] * (rows * pl.num_programs(0)) + step * rows + r
        normed = normalize(pair[r])
        linear = lax.dot_general(
            w, normed, (((1,), (1,)), ((), ())), precision=lax.Precision.HIGHEST,
            preferred_element_type=F32,
        )
        offset = jnp.clip(index_s[i] - cols_index, -reach, reach) + reach
        bucket = jnp.where(chain_s[i] == cols_chain, offset, BUCKETS - 1)
        classes = lax.broadcasted_iota(jnp.int32, (TABLE_ROWS, columns), 0)
        onehot = (classes == bucket).astype(F32)
        relative = lax.dot_general(
            table, onehot, (((1,), (0,)), ((), ())), precision=lax.Precision.HIGHEST,
            preferred_element_type=F32,
        )
        out[:, r, :] = (linear + relative + mask) * LOG2E


def pair_bias(place, numbering, chain, presence, pair, weight, table):
    rows, columns, channels = pair.shape
    part = 8

    def whole(shape):
        return pl.BlockSpec(shape, lambda r, *_: (0,) * len(shape))

    lines = numbering.shape[0] // LANES
    return pl.pallas_call(
        bias_kernel,
        out_shape=jax.ShapeDtypeStruct((HEADS, rows, columns), F32),
        grid_spec=pltpu.PrefetchScalarGridSpec(
            num_scalar_prefetch=3,
            grid=(rows // part,),
            in_specs=[
                pl.BlockSpec((part, columns, channels), lambda r, *_: (r, 0, 0)),
                whole((HEADS, channels)),
                whole((HEADS, TABLE_ROWS)),
            ] + [whole((lines, LANES))] * 3,
            out_specs=pl.BlockSpec((HEADS, part, columns), lambda r, *_: (0, r, 0)),
        ),
        compiler_params=params(1, 32),
        name="pair_bias",
    )(
        place, numbering, chain, pair, weight.T,
        jnp.pad(table, ((0, TABLE_ROWS - BUCKETS), (0, 0))).T,
        numbering.reshape(lines, LANES), chain.reshape(lines, LANES), presence.reshape(lines, LANES),
    )


def project_kernel(place, row, own, gain, packed, kp, vp, qp, gp, wk2, wv2, wq2, wg2, gate_bias):
    channels = row.shape[2]

    @pl.when(pl.program_id(0) == 0)
    def _():
        for q in range(0, packed.shape[0], 2):
            block = pl.ds(channels, channels)
            both = jnp.concatenate([packed[q, block, :], packed[q + 1, block, :]], axis=1).T
            at = pl.ds(q // 2 * both.shape[0], both.shape[0])
            wk2[0, at], wk2[1, at] = split(both)
        for h in range(HEADS):
            q, column = h // 2, h % 2 * DEPTH
            at = pl.ds(h * LANES, LANES)

            def lanes(start, rows, copies):
                part = packed[q, pl.ds(start, rows), :][:, column:column + DEPTH]
                rest = [jnp.zeros((rows, LANES - copies * DEPTH), F32)] if copies * DEPTH < LANES else []
                return jnp.concatenate([part] * copies + rest, axis=1)

            for t, copies, target in ((0, 4, wq2), (2, 2, wv2), (3, 2, wg2)):
                target[0, :, at], target[1, :, at] = split(lanes(t * channels, channels, copies))
            gate_bias[:, at] = lanes(5 * channels, 8, 2)[:1]

    positions = row.shape[1]
    own_positions = own.shape[1]
    n = split(normalize(row[0]) * gain[...])
    keys = split(dot3((wk2[0], wk2[1]), n, ((1,), (1,))))
    for h in range(HEADS):
        for part in range(4):
            kp[0, h, pl.ds(part * DEPTH, DEPTH), :] = keys[part % 2][h * DEPTH:(h + 1) * DEPTH]
    pair_lanes = 2 * LANES
    lane = lax.broadcasted_iota(jnp.int32, (positions, LANES), 1)
    for h in range(0, HEADS, 2):
        cut = pl.ds(h * LANES, pair_lanes)
        both = dot3(n, (wv2[0, :, cut], wv2[1, :, cut]))
        for k in range(2):
            value = both[:, k * LANES:(k + 1) * LANES]
            high = value.astype(BF16).astype(F32)
            packed = jnp.where(lane < DEPTH, high, jnp.where(lane < 2 * DEPTH, value - high, 1.0))
            vp[0, h + k] = packed.astype(BF16)
    m = split(normalize(own[0]) * gain[...])
    lane = lax.broadcasted_iota(jnp.int32, (own_positions, LANES), 1)
    for h in range(0, HEADS, 2):
        cut = pl.ds(h * LANES, pair_lanes)
        both = dot3(m, (wq2[0, :, cut], wq2[1, :, cut])) * (LOG2E / math.sqrt(DEPTH))
        gates = dot3(m, (wg2[0, :, cut], wg2[1, :, cut])) + gate_bias[:, cut]
        gates = jax.nn.sigmoid(gates)
        for k in range(2):
            value = both[:, k * LANES:(k + 1) * LANES]
            high = value.astype(BF16).astype(F32)
            qp[0, h + k] = jnp.where(lane < 2 * DEPTH, high, value - high).astype(BF16)
            gp[0, h + k] = gates[:, k * LANES:(k + 1) * LANES]


def project(place, rows, gain, packed, quarter):
    count, positions, channels = rows.shape
    wide = HEADS * LANES

    def whole(shape):
        return pl.BlockSpec(shape, lambda s, place: (0,) * len(shape))

    def out(rows_, columns, dtype):
        return (
            jax.ShapeDtypeStruct((count, HEADS, rows_, columns), dtype),
            pl.BlockSpec((1, HEADS, rows_, columns), lambda s, place: (s, 0, 0, 0)),
        )

    outs = [out(LANES, positions, BF16), out(positions, LANES, BF16),
            out(quarter, LANES, BF16), out(quarter, LANES, F32)]
    return pl.pallas_call(
        project_kernel,
        out_shape=[o[0] for o in outs],
        grid_spec=pltpu.PrefetchScalarGridSpec(
            num_scalar_prefetch=1,
            grid=(count,),
            in_specs=[
                pl.BlockSpec((1, positions, channels), lambda s, place: (s, 0, 0)),
                pl.BlockSpec((1, quarter, channels), lambda s, place: (s, place[1], 0)),
                whole((1, channels)), whole(packed.shape),
            ],
            out_specs=[o[1] for o in outs],
            scratch_shapes=[pltpu.VMEM((2, HEADS * DEPTH, channels), BF16)]
            + [pltpu.VMEM((2, channels, wide), BF16)] * 3 + [pltpu.VMEM((1, wide), F32)],
        ),
        compiler_params=params(1, 52),
        name="project",
    )(place, rows, rows, gain[None], packed)


def attend_kernel(place, flags_s, bias_a, b0, b1, b2, b3, b4, kp, vp, qp, gp, merge, own, operand_t,
                  mask_c, state_out, first_out, second_out, gated, head_bias):
    h = pl.program_id(0)
    count = own.shape[0]
    quarter = own.shape[1]
    nz, ny, width = bias_a.shape[0], bias_a.shape[1], bias_a.shape[5]
    group = quarter // nz

    def columns(k):
        return pl.ds(pl.multiple_of(lax.rem(place[2] + Y_STEPS[k], ny) * width, width), width)

    def rows(k):
        return pl.ds(pl.multiple_of(lax.rem(place[3] + Z_STEPS[k], nz) * group, group), group)

    @pl.when(h < HEADS_A)
    def _():
        for k in range(ny):
            head_bias[:, columns(k)] = bias_a[:, k, :, 0].reshape(quarter, width)

    @pl.when(h >= HEADS_A)
    def _():
        for y, pieces in enumerate(((b0,), (b1,), (b2,), (b3, b4))):
            k = 0
            for piece in pieces:
                for line in range(piece.shape[0]):
                    head_bias[rows(k), columns(y)] = piece[line, :, 0].reshape(group, width)
                    k += 1

    lane = lax.broadcasted_iota(jnp.int32, (quarter, LANES), 1)
    ahead = dot(qp[0, 0], kp[0, 0]) + head_bias[...]
    for s in range(count):
        logits = ahead
        if s + 1 < count:
            ahead = dot(qp[s + 1, 0], kp[s + 1, 0]) + head_bias[...]
        peak = jnp.max(logits, axis=1, keepdims=True)
        weights = jnp.exp2(logits - peak)
        mixed = dot(jnp.concatenate(split(weights), axis=0), vp[s, 0])
        mixed = mixed[:quarter] + mixed[quarter:]
        total_weight = jnp.where(lane < 2 * DEPTH, pltpu.roll(mixed, LANES // 2, 1), 1.0)
        parts = split(jnp.where(lane < 2 * DEPTH, mixed * gp[s, 0] / total_weight, 0.0))
        at = pl.ds(pl.multiple_of(h * LANES, LANES), LANES)
        gated[0, s, :, at], gated[1, s, :, at] = parts

    @pl.when(h == pl.num_programs(0) - 1)
    def _():
        ops = split(operand_t[...])
        m2 = split(merge[...])
        for s in range(count):
            state = own[s] + dot3((gated[0, s], gated[1, s]), m2)
            state_out[s] = state
            n = split(normalize(state))
            flag = flags_s[place[0] * count + s].astype(F32)
            factors = dot3(ops, n, ((1,), (1,))) * (mask_c[0] * flag)
            first_out[s] = factors[:RANK]
            for e in range(RANK):
                second_out[pl.ds(s, 1), pl.ds(e * quarter, quarter)] = factors[RANK + e:RANK + e + 1]


def attend(place, flags, bias, kp, vp, qp, gp, merge, rows, operand_t, mask, quarter):
    count, positions, channels = rows.shape

    def piece_block(piece, low, high):
        shape = list(piece.shape)
        shape[-3] = 1

        def at(h, *_):
            index = [0] * len(shape)
            index[-3] = jnp.clip(h - low, 0, high)
            return tuple(index)

        return pl.BlockSpec(tuple(shape), at)

    def head_block(rows_, columns):
        return pl.BlockSpec((count, 1, rows_, columns), lambda h, *_: (0, h, 0, 0))

    return pl.pallas_call(
        attend_kernel,
        out_shape=[
            jax.ShapeDtypeStruct((count, quarter, channels), F32),
            jax.ShapeDtypeStruct((count, RANK, quarter), F32),
            jax.ShapeDtypeStruct((count, RANK * quarter), F32),
        ],
        grid_spec=pltpu.PrefetchScalarGridSpec(
            num_scalar_prefetch=2,
            grid=(HEADS,),
            in_specs=[
                piece_block(bias[0], 0, HEADS_A - 1),
            ] + [piece_block(piece, HEADS_A, HEADS - HEADS_A - 1) for piece in bias[1]] + [
                head_block(LANES, positions), head_block(positions, LANES),
                head_block(quarter, LANES), head_block(quarter, LANES),
                pl.BlockSpec((HEADS * LANES, channels), lambda h, *_: (0, 0)),
                pl.BlockSpec((count, quarter, channels), lambda h, place, *_: (0, place[1], 0)),
                pl.BlockSpec((2 * RANK, channels), lambda h, *_: (0, 0)),
                pl.BlockSpec((1, 1, quarter), lambda h, place, *_: (place[1], 0, 0)),
            ],
            out_specs=[
                pl.BlockSpec((count, quarter, channels), lambda h, *_: (0, 0, 0)),
                pl.BlockSpec((count, RANK, quarter), lambda h, *_: (0, 0, 0)),
                pl.BlockSpec((count, RANK * quarter), lambda h, *_: (0, 0)),
            ],
            scratch_shapes=[
                pltpu.VMEM((2, count, quarter, HEADS * LANES), BF16),
                pltpu.VMEM((quarter, positions), F32),
            ],
        ),
        compiler_params=params(1, 52),
        name="attend",
    )(place, flags, bias[0], *bias[1], kp, vp, qp, gp, merge, rows, operand_t, mask.reshape(-1, 1, quarter))


def outer_kernel(group, place, mask_s, f0, f1, f2, f3, sa, s0, s1, s2, s3, s4, weight_t, out_bias,
                 count_c, pair, t0, t1, t2, t3, out, state, ordered, moved, a2, w2, r2):
    step = pl.program_id(0)
    steps = RANK // group
    i_rows = r2.shape[1]
    columns = pair.shape[1]
    nz, ny, eight = sa.shape[0], sa.shape[1], sa.shape[2]
    y_at = [lax.rem(place[2] + k, ny) for k in Y_STEPS]
    z_at = [lax.rem(place[3] + k, nz) for k in Z_STEPS]

    def row(y, z):
        return pl.ds(pl.multiple_of((y * nz + z) * eight, eight), eight)

    @pl.when(step == 0)
    def _():
        high, low = split(weight_t[...])
        w2[:LANES], w2[LANES:] = high, low
        for r, piece in enumerate((f0, f1, f2, f3)):
            y = lax.rem((place[1] ^ (r // 2)) + 2 * (r % 2), ny)
            ordered[pl.ds(pl.multiple_of(y * piece.shape[0], piece.shape[0]), piece.shape[0]), :] = piece[...]
        for z in range(nz):
            for k in range(ny):
                moved[pl.ds((z * ny + k) * eight, eight), :] = ordered[row(y_at[k], z), :]
        a2[0], a2[1] = split(moved[...].T)

    @pl.when(step == steps // 2)
    def _():
        for k in range(ny):
            for z in range(nz):
                moved[pl.ds((k * nz + z) * eight, eight), :] = ordered[row(y_at[k], z_at[z]), :]
        a2[0], a2[1] = split(moved[...].T)

    def products(blocks):
        for g in range(group):
            cut = pl.ds(g * columns, columns)
            b = [block[..., cut].reshape(-1, columns) for block in blocks]
            b = split(b[0] if len(b) == 1 else jnp.concatenate(b, axis=0))
            r = split(dot3((a2[0], a2[1]), b))
            at = pl.multiple_of((step * group + g) * RANK, RANK)
            for part in range(2):
                for i in range(i_rows):
                    r2[part, i, pl.ds(at, RANK), :] = r[part][i * RANK:(i + 1) * RANK]

    @pl.when(step < steps // 2)
    def _():
        products((sa,))

    @pl.when((step >= steps // 2) & (step < steps))
    def _():
        products((s0, s1, s2, s3, s4))

    @pl.when(step >= steps)
    def _():
        for k in range(pair.shape[0]):
            i = (step - steps) * pair.shape[0] + k
            both = dot(w2[...], r2[0, i])
            value = both[:LANES] + (both[LANES:] + dot(w2[:LANES], r2[1, i])) + out_bias[...]
            count = jnp.maximum(mask_s[place[0] * i_rows + i].astype(F32) * count_c[0], 1.0)
            out[k] = pair[k] + (value / count).T
        for k, piece in enumerate((t0, t1, t2, t3)):
            @pl.when((step - steps) // 2 == k)
            def _(piece=piece):
                state[...] = piece[...]


def outer_mean(place, mask, first, second, weight_t, out_bias, count, pair, state):
    rows, columns, channels = pair.shape
    members = sum(piece.shape[0] for piece in first)
    wide = rows * RANK
    group = 8
    steps = RANK // group
    half = steps // 2
    part = 2
    count_s, quarter, features = state[0].shape
    lines = count_s // 2
    whole_state = (count_s, quarter * len(state), features)

    def state_block(t, place, *_):
        at = jnp.clip(t - steps, 0, 2 * len(state) - 1)
        return (lax.rem(at, 2), place[1] ^ (at // 2), 0)

    def own(t, *_):
        return (jnp.maximum(t - steps, 0), 0, 0)

    def whole(shape):
        return pl.BlockSpec(shape, lambda t, *_: (0,) * len(shape))

    def columns_block(piece, low):
        lead = piece.shape[:-1]
        return pl.BlockSpec(
            lead + (group * columns,),
            lambda t, *_: (0,) * len(lead) + (jnp.clip(t - low, 0, half - 1),),
        )

    return pl.pallas_call(
        partial(outer_kernel, group),
        out_shape=[
            jax.ShapeDtypeStruct(pair.shape, F32),
            jax.ShapeDtypeStruct(whole_state, F32),
        ],
        grid_spec=pltpu.PrefetchScalarGridSpec(
            num_scalar_prefetch=2,
            grid=(steps + rows // part,),
            in_specs=[whole(piece.shape) for piece in first]
            + [columns_block(second[0], 0)]
            + [columns_block(piece, half) for piece in second[1]]
            + [
                whole((channels, RANK * RANK)),
                whole((channels, 1)),
                pl.BlockSpec((1, 1, columns), lambda t, place, *_: (place[1], 0, 0)),
                pl.BlockSpec((part, columns, channels), own),
            ] + [
                pl.BlockSpec((lines, quarter, features),
                             lambda t, *_, k=k: (jnp.clip(t - steps - 2 * k, 0, 1), 0, 0))
                for k in range(len(state))
            ],
            out_specs=[pl.BlockSpec((part, columns, channels), own),
                       pl.BlockSpec((lines, quarter, features), state_block)],
            scratch_shapes=[
                pltpu.VMEM((members, wide), F32),
                pltpu.VMEM((members, wide), F32),
                pltpu.VMEM((2, wide, members), BF16),
                pltpu.VMEM((2 * channels, RANK * RANK), BF16),
                pltpu.VMEM((2, rows, RANK * RANK, columns), BF16),
            ],
        ),
        compiler_params=params(1, 52),
        name="outer_mean",
    )(place, mask, *first, second[0], *second[1], weight_t, out_bias[:, None],
      count.reshape(-1, 1, columns), pair, *state)


Y_STEPS = (0, 3, 1, 2)
Z_STEPS = (0, 7, 1, 6, 2, 5, 3, 4)


def shift(block, axis, size, step):
    return lax.ppermute(block, axis, [(i, (i + step) % size) for i in range(size)])


def gather_both(block_a, block_b, ny, nz, early=()):
    along = [shift(block_a, "y", ny, -k) for k in Y_STEPS[1:]]
    one = [shift(block_b, "z", nz, k) for k in (1, -1)]
    two = [shift(block_b, "z", nz, k) for k in (2, -2)]
    along, one, two, early = lax.optimization_barrier((along, one, two, early))
    gathered_a = lax.all_gather(jnp.stack([block_a] + along), "z")
    three = [shift(one[0], "z", nz, 2), shift(one[1], "z", nz, -2)]
    cut = block_b.shape[0] // 2
    four = [shift(two[0][:cut], "z", nz, 2), shift(two[1][cut:], "z", nz, -2)]
    three, four = lax.optimization_barrier((three, four))
    gathered_b = jnp.stack([block_b] + one + two + three + [jnp.concatenate(four)])
    return gathered_a, gathered_b, early


def gather_y(block, ny, beside=()):
    one = [shift(block, "y", ny, k) for k in (1, -1)]
    one, beside = lax.optimization_barrier((one, beside))
    cut = block.shape[0] // 2
    two = [shift(one[0][:cut], "y", ny, 1), shift(one[1][cut:], "y", ny, -1)]
    return [block] + one + two, beside


def in_order(mine, other):
    low = lax.axis_index("xl") == 0
    return jnp.stack([jnp.where(low, mine, other), jnp.where(low, other, mine)])


def per_device(
    sizes,
    lineup_embedding,
    pairwise_state,
    lineup_scaling_coefficients,
    focus_projection_matrix,
    attention_gate_bias,
    focus_merge_matrix,
    pairwise_bias_weight,
    relative_bias_table,
    tensor_operand_matrices,
    outer_output_weight,
    outer_output_bias,
    lineup_member_flags,
    residue_presence_mask,
    chain_label,
    residue_numbering,
):
    ny, nz, nxl, nxh, nc = (sizes[a] for a in ("y", "z", "xl", "xh", "c"))
    nq = nxh * nc
    dap = (lax.axis_index("y") * nz + lax.axis_index("z")) * nxl + lax.axis_index("xl")
    head = lax.axis_index("xh") * nc + lax.axis_index("c")
    place = jnp.stack([dap, head, lax.axis_index("y"), lax.axis_index("z")]).astype(jnp.int32)
    count, positions, channels = lineup_embedding.shape
    block_rows, quarter, pair_channels = pairwise_state.shape
    presence = residue_presence_mask.astype(F32)

    narrow = focus_projection_matrix.shape[2]
    packed = jnp.concatenate(
        [
            focus_projection_matrix.reshape(-1, narrow),
            focus_merge_matrix.reshape(-1, narrow),
            jnp.broadcast_to(attention_gate_bias[None], (8, narrow)),
        ]
    )
    packed, pairwise_state = lax.optimization_barrier((packed, pairwise_state))
    packed = lax.all_gather(packed, HEAD_AXES)

    merge = packed[:, 4 * channels:5 * channels].reshape(HEADS, DEPTH, channels)
    merge = jnp.pad(jnp.concatenate([merge, merge], axis=1), ((0, 0), (0, LANES - 2 * DEPTH), (0, 0)))
    merge = merge.reshape(HEADS * LANES, channels)

    local = pair_bias(place, residue_numbering, chain_label, residue_presence_mask, pairwise_state,
                      pairwise_bias_weight, relative_bias_table)

    def swap(flip):
        perm = []
        for y in range(ny):
            for x in range(nxl):
                for q in range(nq):
                    perm.append(((y * nxl + x) * nq + q, (q * nxl + (x ^ flip)) * nq + y))
        return lax.ppermute(local, ("y", "xl") + HEAD_AXES, perm)

    bias = in_order(swap(0), swap(1))
    bias_a, bias_b, packed = gather_both(bias[:, :HEADS_A], bias[:, HEADS_A:], ny, nz, packed)
    bias_b, rows = lax.optimization_barrier((bias_b, lineup_embedding))
    projected = project(place, rows, lineup_scaling_coefficients, packed, quarter)
    bias_b, (kp, vp, qp, gp) = gather_y(bias_b, ny, projected)
    bias = (bias_a, bias_b)
    operand_t = jnp.swapaxes(tensor_operand_matrices, 1, 2).reshape(2 * RANK, channels)
    state, first, second = attend(place, lineup_member_flags, bias, kp, vp, qp, gp, merge,
                                  lineup_embedding, operand_t, presence, quarter)

    second = in_order(second, shift(second, "xl", nxl, 1)).reshape(nxl * count, -1)
    half = second.shape[1] // 2
    second_a, second_b, _ = gather_both(second[:, :half], second[:, half:], ny, nz)
    second_b, first, state = lax.optimization_barrier((second_b, first, state))

    parts = nz * nxl
    first = jnp.transpose(first.reshape(count, RANK, parts, block_rows), (2, 0, 3, 1))
    first = lax.all_to_all(first.reshape(parts, count, block_rows * RANK), ("z", "xl"), 0, 0, tiled=True)
    across = shift(state, "xh", nxh, 1)
    first, across = lax.optimization_barrier((first.reshape(parts * count, -1), across))
    first = [
        lax.ppermute(first, ("y",) + HEAD_AXES,
                     [(y * nq + q, q * nq + (y + r) % nq) for y in range(ny) for q in range(nq)])
        for r in (0, 2)
    ]

    pieces = [state, shift(state, "c", nc, 1), across, shift(across, "c", nc, 1)]
    second_b, _ = gather_y(second_b, ny)
    second = (second_a, second_b)
    first = first + [shift(piece, "c", nc, 1) for piece in first]

    weight_t = jnp.transpose(
        outer_output_weight.reshape(RANK, RANK, pair_channels), (2, 1, 0)
    ).reshape(pair_channels, RANK * RANK)
    count_columns = presence * jnp.sum(lineup_member_flags.astype(F32))
    pairs, state = outer_mean(place, residue_presence_mask, first, second, weight_t,
                              outer_output_bias, count_columns, pairwise_state, pieces)
    return state, pairs


def solution(mesh):
    sizes = dict(y=4, z=8, xl=2, xh=2, c=2)
    fine = Mesh(mesh.devices.reshape(tuple(sizes.values())), tuple(sizes))
    placed = (
        P(DAP_AXES, None, None),
        P(DAP_AXES, HEAD_AXES, None),
        P(),
        P(None, None, HEAD_AXES),
        P(HEAD_AXES),
        P(HEAD_AXES, None),
    ) + (P(),) * 9
    return jax.shard_map(
        partial(per_device, sizes),
        mesh=fine,
        in_specs=placed,
        out_specs=(P(DAP_AXES, None, None), P(DAP_AXES, HEAD_AXES, None)),
        check_vma=False,
    )
```

```python
import math
from functools import partial

import jax
import jax.numpy as jnp
from jax import lax
from jax.experimental import pallas as pl
from jax.experimental.pallas import tpu as pltpu
from jax.sharding import Mesh, PartitionSpec as P

F32, BF16 = jnp.float32, jnp.bfloat16
HEADS, DEPTH, RANK, BUCKETS = 8, 32, 32, 66
HEADS_A = 4
TABLE_ROWS = 72
LANES = 128
LOG2E = math.log2(math.e)
HEAD_AXES = ("xh", "c")
DAP_AXES = ("y", "z", "xl")


def dot(a, b, contract=((1,), (0,))):
    return lax.dot_general(a, b, (contract, ((), ())), preferred_element_type=F32)


def split(a):
    high = a.astype(BF16)
    return high, (a - high.astype(F32)).astype(BF16)


def dot3(a, b, contract=((1,), (0,))):
    return dot(a[0], b[0], contract) + (dot(a[0], b[1], contract) + dot(a[1], b[0], contract))


def normalize(values):
    center = values - jnp.mean(values, axis=-1, keepdims=True)
    spread = jnp.mean(center * center, axis=-1, keepdims=True)
    return center * lax.rsqrt(spread + 1e-05)


def params(n_axes, mib):
    return pltpu.CompilerParams(
        dimension_semantics=("arbitrary",) * n_axes, vmem_limit_bytes=mib * 2**20
    )


def bias_kernel(place, index_s, chain_s, pair, weight_t, table_t, index_c, chain_c, mask_c, out):
    step = pl.program_id(0)
    rows = pair.shape[0]
    columns = pair.shape[1]
    w = weight_t[...]
    table = table_t[...]
    lines = columns // LANES

    def own_columns(ref):
        return jnp.concatenate([ref[pl.ds(place[1] * lines + k, 1), :] for k in range(lines)], axis=1)

    cols_index = own_columns(index_c)
    cols_chain = own_columns(chain_c)
    mask = (own_columns(mask_c).astype(F32) - 1.0) * 1000000000.0
    reach = (BUCKETS - 2) // 2
    for r in range(rows):
        i = place[0] * (rows * pl.num_programs(0)) + step * rows + r
        normed = normalize(pair[r])
        linear = lax.dot_general(
            w, normed, (((1,), (1,)), ((), ())), precision=lax.Precision.HIGHEST,
            preferred_element_type=F32,
        )
        offset = jnp.clip(index_s[i] - cols_index, -reach, reach) + reach
        bucket = jnp.where(chain_s[i] == cols_chain, offset, BUCKETS - 1)
        classes = lax.broadcasted_iota(jnp.int32, (TABLE_ROWS, columns), 0)
        onehot = (classes == bucket).astype(F32)
        relative = lax.dot_general(
            table, onehot, (((1,), (0,)), ((), ())), precision=lax.Precision.HIGHEST,
            preferred_element_type=F32,
        )
        out[:, r, :] = (linear + relative + mask) * LOG2E


def pair_bias(place, numbering, chain, presence, pair, weight, table):
    rows, columns, channels = pair.shape
    part = 8

    def whole(shape):
        return pl.BlockSpec(shape, lambda r, *_: (0,) * len(shape))

    lines = numbering.shape[0] // LANES
    return pl.pallas_call(
        bias_kernel,
        out_shape=jax.ShapeDtypeStruct((HEADS, rows, columns), F32),
        grid_spec=pltpu.PrefetchScalarGridSpec(
            num_scalar_prefetch=3,
            grid=(rows // part,),
            in_specs=[
                pl.BlockSpec((part, columns, channels), lambda r, *_: (r, 0, 0)),
                whole((HEADS, channels)),
                whole((HEADS, TABLE_ROWS)),
            ] + [whole((lines, LANES))] * 3,
            out_specs=pl.BlockSpec((HEADS, part, columns), lambda r, *_: (0, r, 0)),
        ),
        compiler_params=params(1, 32),
        name="pair_bias",
    )(
        place, numbering, chain, pair, weight.T,
        jnp.pad(table, ((0, TABLE_ROWS - BUCKETS), (0, 0))).T,
        numbering.reshape(lines, LANES), chain.reshape(lines, LANES), presence.reshape(lines, LANES),
    )


def project_kernel(place, row, own, gain, packed, kp, vp, qp, gp, wk2, wv2, wq2, wg2, gate_bias):
    channels = row.shape[2]

    @pl.when(pl.program_id(0) == 0)
    def _():
        for q in range(0, packed.shape[0], 2):
            block = pl.ds(channels, channels)
            both = jnp.concatenate([packed[q, block, :], packed[q + 1, block, :]], axis=1).T
            at = pl.ds(q // 2 * both.shape[0], both.shape[0])
            wk2[0, at], wk2[1, at] = split(both)
        for h in range(HEADS):
            q, column = h // 2, h % 2 * DEPTH
            at = pl.ds(h * LANES, LANES)

            def lanes(start, rows, copies):
                part = packed[q, pl.ds(start, rows), :][:, column:column + DEPTH]
                rest = [jnp.zeros((rows, LANES - copies * DEPTH), F32)] if copies * DEPTH < LANES else []
                return jnp.concatenate([part] * copies + rest, axis=1)

            for t, copies, target in ((0, 4, wq2), (2, 2, wv2), (3, 2, wg2)):
                target[0, :, at], target[1, :, at] = split(lanes(t * channels, channels, copies))
            gate_bias[:, at] = lanes(5 * channels, 8, 2)[:1]

    positions = row.shape[1]
    own_positions = own.shape[1]
    n = split(normalize(row[0]) * gain[...])
    keys = split(dot3((wk2[0], wk2[1]), n, ((1,), (1,))))
    for h in range(HEADS):
        for part in range(4):
            kp[0, h, pl.ds(part * DEPTH, DEPTH), :] = keys[part % 2][h * DEPTH:(h + 1) * DEPTH]
    pair_lanes = 2 * LANES
    lane = lax.broadcasted_iota(jnp.int32, (positions, LANES), 1)
    for h in range(0, HEADS, 2):
        cut = pl.ds(h * LANES, pair_lanes)
        both = dot3(n, (wv2[0, :, cut], wv2[1, :, cut]))
        for k in range(2):
            value = both[:, k * LANES:(k + 1) * LANES]
            high = value.astype(BF16).astype(F32)
            packed = jnp.where(lane < DEPTH, high, jnp.where(lane < 2 * DEPTH, value - high, 1.0))
            vp[0, h + k] = packed.astype(BF16)
    m = split(normalize(own[0]) * gain[...])
    lane = lax.broadcasted_iota(jnp.int32, (own_positions, LANES), 1)
    for h in range(0, HEADS, 2):
        cut = pl.ds(h * LANES, pair_lanes)
        both = dot3(m, (wq2[0, :, cut], wq2[1, :, cut])) * (LOG2E / math.sqrt(DEPTH))
        gates = dot3(m, (wg2[0, :, cut], wg2[1, :, cut])) + gate_bias[:, cut]
        gates = jax.nn.sigmoid(gates)
        for k in range(2):
            value = both[:, k * LANES:(k + 1) * LANES]
            high = value.astype(BF16).astype(F32)
            qp[0, h + k] = jnp.where(lane < 2 * DEPTH, high, value - high).astype(BF16)
            gp[0, h + k] = gates[:, k * LANES:(k + 1) * LANES]


def project(place, rows, gain, packed, quarter):
    count, positions, channels = rows.shape
    wide = HEADS * LANES

    def whole(shape):
        return pl.BlockSpec(shape, lambda s, place: (0,) * len(shape))

    def out(rows_, columns, dtype):
        return (
            jax.ShapeDtypeStruct((count, HEADS, rows_, columns), dtype),
            pl.BlockSpec((1, HEADS, rows_, columns), lambda s, place: (s, 0, 0, 0)),
        )

    outs = [out(LANES, positions, BF16), out(positions, LANES, BF16),
            out(quarter, LANES, BF16), out(quarter, LANES, F32)]
    return pl.pallas_call(
        project_kernel,
        out_shape=[o[0] for o in outs],
        grid_spec=pltpu.PrefetchScalarGridSpec(
            num_scalar_prefetch=1,
            grid=(count,),
            in_specs=[
                pl.BlockSpec((1, positions, channels), lambda s, place: (s, 0, 0)),
                pl.BlockSpec((1, quarter, channels), lambda s, place: (s, place[1], 0)),
                whole((1, channels)), whole(packed.shape),
            ],
            out_specs=[o[1] for o in outs],
            scratch_shapes=[pltpu.VMEM((2, HEADS * DEPTH, channels), BF16)]
            + [pltpu.VMEM((2, channels, wide), BF16)] * 3 + [pltpu.VMEM((1, wide), F32)],
        ),
        compiler_params=params(1, 52),
        name="project",
    )(place, rows, rows, gain[None], packed)


def attend_kernel(place, flags_s, bias_a, b0, b1, b2, b3, b4, kp, vp, qp, gp, merge, own, operand_t,
                  mask_c, state_out, first_out, second_out, gated, head_bias):
    h = pl.program_id(0)
    count = own.shape[0]
    quarter = own.shape[1]
    nz, ny, width = bias_a.shape[0], bias_a.shape[1], bias_a.shape[5]
    group = quarter // nz

    def columns(k):
        return pl.ds(pl.multiple_of(lax.rem(place[2] + Y_STEPS[k], ny) * width, width), width)

    def rows(k):
        return pl.ds(pl.multiple_of(lax.rem(place[3] + Z_STEPS[k], nz) * group, group), group)

    @pl.when(h < HEADS_A)
    def _():
        for k in range(ny):
            head_bias[:, columns(k)] = bias_a[:, k, :, 0].reshape(quarter, width)

    @pl.when(h >= HEADS_A)
    def _():
        for y, pieces in enumerate(((b0,), (b1,), (b2,), (b3, b4))):
            k = 0
            for piece in pieces:
                for line in range(piece.shape[0]):
                    head_bias[rows(k), columns(y)] = piece[line, :, 0].reshape(group, width)
                    k += 1

    lane = lax.broadcasted_iota(jnp.int32, (quarter, LANES), 1)
    ahead = dot(qp[0, 0], kp[0, 0]) + head_bias[...]
    for s in range(count):
        logits = ahead
        if s + 1 < count:
            ahead = dot(qp[s + 1, 0], kp[s + 1, 0]) + head_bias[...]
        peak = jnp.max(logits, axis=1, keepdims=True)
        weights = jnp.exp2(logits - peak)
        mixed = dot(jnp.concatenate(split(weights), axis=0), vp[s, 0])
        mixed = mixed[:quarter] + mixed[quarter:]
        total_weight = jnp.where(lane < 2 * DEPTH, pltpu.roll(mixed, LANES // 2, 1), 1.0)
        parts = split(jnp.where(lane < 2 * DEPTH, mixed * gp[s, 0] / total_weight, 0.0))
        at = pl.ds(pl.multiple_of(h * LANES, LANES), LANES)
        gated[0, s, :, at], gated[1, s, :, at] = parts

    @pl.when(h == pl.num_programs(0) - 1)
    def _():
        ops = split(operand_t[...])
        m2 = split(merge[...])
        for s in range(count):
            state = own[s] + dot3((gated[0, s], gated[1, s]), m2)
            state_out[s] = state
            n = split(normalize(state))
            flag = flags_s[place[0] * count + s].astype(F32)
            factors = dot3(ops, n, ((1,), (1,))) * (mask_c[0] * flag)
            first_out[s] = factors[:RANK]
            for e in range(RANK):
                second_out[pl.ds(s, 1), pl.ds(e * quarter, quarter)] = factors[RANK + e:RANK + e + 1]


def attend(place, flags, bias, kp, vp, qp, gp, merge, rows, operand_t, mask, quarter):
    count, positions, channels = rows.shape

    def piece_block(piece, low, high):
        shape = list(piece.shape)
        shape[-3] = 1

        def at(h, *_):
            index = [0] * len(shape)
            index[-3] = jnp.clip(h - low, 0, high)
            return tuple(index)

        return pl.BlockSpec(tuple(shape), at)

    def head_block(rows_, columns):
        return pl.BlockSpec((count, 1, rows_, columns), lambda h, *_: (0, h, 0, 0))

    return pl.pallas_call(
        attend_kernel,
        out_shape=[
            jax.ShapeDtypeStruct((count, quarter, channels), F32),
            jax.ShapeDtypeStruct((count, RANK, quarter), F32),
            jax.ShapeDtypeStruct((count, RANK * quarter), F32),
        ],
        grid_spec=pltpu.PrefetchScalarGridSpec(
            num_scalar_prefetch=2,
            grid=(HEADS,),
            in_specs=[
                piece_block(bias[0], 0, HEADS_A - 1),
            ] + [piece_block(piece, HEADS_A, HEADS - HEADS_A - 1) for piece in bias[1]] + [
                head_block(LANES, positions), head_block(positions, LANES),
                head_block(quarter, LANES), head_block(quarter, LANES),
                pl.BlockSpec((HEADS * LANES, channels), lambda h, *_: (0, 0)),
                pl.BlockSpec((count, quarter, channels), lambda h, place, *_: (0, place[1], 0)),
                pl.BlockSpec((2 * RANK, channels), lambda h, *_: (0, 0)),
                pl.BlockSpec((1, 1, quarter), lambda h, place, *_: (place[1], 0, 0)),
            ],
            out_specs=[
                pl.BlockSpec((count, quarter, channels), lambda h, *_: (0, 0, 0)),
                pl.BlockSpec((count, RANK, quarter), lambda h, *_: (0, 0, 0)),
                pl.BlockSpec((count, RANK * quarter), lambda h, *_: (0, 0)),
            ],
            scratch_shapes=[
                pltpu.VMEM((2, count, quarter, HEADS * LANES), BF16),
                pltpu.VMEM((quarter, positions), F32),
            ],
        ),
        compiler_params=params(1, 52),
        name="attend",
    )(place, flags, bias[0], *bias[1], kp, vp, qp, gp, merge, rows, operand_t, mask.reshape(-1, 1, quarter))


def outer_kernel(group, place, mask_s, f0, f1, f2, f3, sa, s0, s1, s2, s3, s4, weight_t, out_bias,
                 count_c, pair, t0, t1, t2, t3, out, state, ordered, moved, a2, w2, r2):
    step = pl.program_id(0)
    steps = RANK // group
    i_rows = r2.shape[1]
    columns = pair.shape[1]
    nz, ny, eight = sa.shape[0], sa.shape[1], sa.shape[2]
    y_at = [lax.rem(place[2] + k, ny) for k in Y_STEPS]
    z_at = [lax.rem(place[3] + k, nz) for k in Z_STEPS]

    def row(y, z):
        return pl.ds(pl.multiple_of((y * nz + z) * eight, eight), eight)

    @pl.when(step == 0)
    def _():
        high, low = split(weight_t[...])
        w2[:LANES], w2[LANES:] = high, low
        for r, piece in enumerate((f0, f1, f2, f3)):
            y = lax.rem((place[1] ^ (r // 2)) + 2 * (r % 2), ny)
            ordered[pl.ds(pl.multiple_of(y * piece.shape[0], piece.shape[0]), piece.shape[0]), :] = piece[...]
        for z in range(nz):
            for k in range(ny):
                moved[pl.ds((z * ny + k) * eight, eight), :] = ordered[row(y_at[k], z), :]
        a2[0], a2[1] = split(moved[...].T)

    @pl.when(step == steps // 2)
    def _():
        for k in range(ny):
            for z in range(nz):
                moved[pl.ds((k * nz + z) * eight, eight), :] = ordered[row(y_at[k], z_at[z]), :]
        a2[0], a2[1] = split(moved[...].T)

    def products(blocks):
        for g in range(group):
            cut = pl.ds(g * columns, columns)
            b = [block[..., cut].reshape(-1, columns) for block in blocks]
            b = split(b[0] if len(b) == 1 else jnp.concatenate(b, axis=0))
            r = split(dot3((a2[0], a2[1]), b))
            at = pl.multiple_of((step * group + g) * RANK, RANK)
            for part in range(2):
                for i in range(i_rows):
                    r2[part, i, pl.ds(at, RANK), :] = r[part][i * RANK:(i + 1) * RANK]

    @pl.when(step < steps // 2)
    def _():
        products((sa,))

    @pl.when((step >= steps // 2) & (step < steps))
    def _():
        products((s0, s1, s2, s3, s4))

    @pl.when(step >= steps)
    def _():
        for k in range(pair.shape[0]):
            i = (step - steps) * pair.shape[0] + k
            both = dot(w2[...], r2[0, i])
            value = both[:LANES] + (both[LANES:] + dot(w2[:LANES], r2[1, i])) + out_bias[...]
            count = jnp.maximum(mask_s[place[0] * i_rows + i].astype(F32) * count_c[0], 1.0)
            out[k] = pair[k] + (value / count).T
        for k, piece in enumerate((t0, t1, t2, t3)):
            @pl.when((step - steps) // 2 == k)
            def _(piece=piece):
                state[...] = piece[...]


def outer_mean(place, mask, first, second, weight_t, out_bias, count, pair, state):
    rows, columns, channels = pair.shape
    members = sum(piece.shape[0] for piece in first)
    wide = rows * RANK
    group = 8
    steps = RANK // group
    half = steps // 2
    part = 2
    count_s, quarter, features = state[0].shape
    lines = count_s // 2
    whole_state = (count_s, quarter * len(state), features)

    def state_block(t, place, *_):
        at = jnp.clip(t - steps, 0, 2 * len(state) - 1)
        return (lax.rem(at, 2), place[1] ^ (at // 2), 0)

    def own(t, *_):
        return (jnp.maximum(t - steps, 0), 0, 0)

    def whole(shape):
        return pl.BlockSpec(shape, lambda t, *_: (0,) * len(shape))

    def columns_block(piece, low):
        lead = piece.shape[:-1]
        return pl.BlockSpec(
            lead + (group * columns,),
            lambda t, *_: (0,) * len(lead) + (jnp.clip(t - low, 0, half - 1),),
        )

    return pl.pallas_call(
        partial(outer_kernel, group),
        out_shape=[
            jax.ShapeDtypeStruct(pair.shape, F32),
            jax.ShapeDtypeStruct(whole_state, F32),
        ],
        grid_spec=pltpu.PrefetchScalarGridSpec(
            num_scalar_prefetch=2,
            grid=(steps + rows // part,),
            in_specs=[whole(piece.shape) for piece in first]
            + [columns_block(second[0], 0)]
            + [columns_block(piece, half) for piece in second[1]]
            + [
                whole((channels, RANK * RANK)),
                whole((channels, 1)),
                pl.BlockSpec((1, 1, columns), lambda t, place, *_: (place[1], 0, 0)),
                pl.BlockSpec((part, columns, channels), own),
            ] + [
                pl.BlockSpec((lines, quarter, features),
                             lambda t, *_, k=k: (jnp.clip(t - steps - 2 * k, 0, 1), 0, 0))
                for k in range(len(state))
            ],
            out_specs=[pl.BlockSpec((part, columns, channels), own),
                       pl.BlockSpec((lines, quarter, features), state_block)],
            scratch_shapes=[
                pltpu.VMEM((members, wide), F32),
                pltpu.VMEM((members, wide), F32),
                pltpu.VMEM((2, wide, members), BF16),
                pltpu.VMEM((2 * channels, RANK * RANK), BF16),
                pltpu.VMEM((2, rows, RANK * RANK, columns), BF16),
            ],
        ),
        compiler_params=params(1, 52),
        name="outer_mean",
    )(place, mask, *first, second[0], *second[1], weight_t, out_bias[:, None],
      count.reshape(-1, 1, columns), pair, *state)


Y_STEPS = (0, 3, 1, 2)
Z_STEPS = (0, 7, 1, 6, 2, 5, 3, 4)


def shift(block, axis, size, step):
    return lax.ppermute(block, axis, [(i, (i + step) % size) for i in range(size)])


def gather_both(block_a, block_b, ny, nz, early=()):
    along = [shift(block_a, "y", ny, -k) for k in Y_STEPS[1:]]
    one = [shift(block_b, "z", nz, k) for k in (1, -1)]
    two = [shift(block_b, "z", nz, k) for k in (2, -2)]
    along, early = lax.optimization_barrier((along, early))
    gathered_a = lax.all_gather(jnp.stack([block_a] + along), "z")
    three = [shift(one[0], "z", nz, 2), shift(one[1], "z", nz, -2)]
    cut = block_b.shape[0] // 2
    four = [shift(two[0][:cut], "z", nz, 2), shift(two[1][cut:], "z", nz, -2)]
    gathered_b = jnp.stack([block_b] + one + two + three + [jnp.concatenate(four)])
    return gathered_a, gathered_b, early


def gather_y(block, ny, beside=()):
    one = [shift(block, "y", ny, k) for k in (1, -1)]
    one, beside = lax.optimization_barrier((one, beside))
    cut = block.shape[0] // 2
    two = [shift(one[0][:cut], "y", ny, 1), shift(one[1][cut:], "y", ny, -1)]
    return [block] + one + two, beside


def in_order(mine, other):
    low = lax.axis_index("xl") == 0
    return jnp.stack([jnp.where(low, mine, other), jnp.where(low, other, mine)])


def per_device(
    sizes,
    lineup_embedding,
    pairwise_state,
    lineup_scaling_coefficients,
    focus_projection_matrix,
    attention_gate_bias,
    focus_merge_matrix,
    pairwise_bias_weight,
    relative_bias_table,
    tensor_operand_matrices,
    outer_output_weight,
    outer_output_bias,
    lineup_member_flags,
    residue_presence_mask,
    chain_label,
    residue_numbering,
):
    ny, nz, nxl, nxh, nc = (sizes[a] for a in ("y", "z", "xl", "xh", "c"))
    nq = nxh * nc
    dap = (lax.axis_index("y") * nz + lax.axis_index("z")) * nxl + lax.axis_index("xl")
    head = lax.axis_index("xh") * nc + lax.axis_index("c")
    place = jnp.stack([dap, head, lax.axis_index("y"), lax.axis_index("z")]).astype(jnp.int32)
    count, positions, channels = lineup_embedding.shape
    block_rows, quarter, pair_channels = pairwise_state.shape
    presence = residue_presence_mask.astype(F32)

    narrow = focus_projection_matrix.shape[2]
    packed = jnp.concatenate(
        [
            focus_projection_matrix.reshape(-1, narrow),
            focus_merge_matrix.reshape(-1, narrow),
            jnp.broadcast_to(attention_gate_bias[None], (8, narrow)),
        ]
    )
    packed, pairwise_state = lax.optimization_barrier((packed, pairwise_state))
    packed = lax.all_gather(packed, HEAD_AXES)

    merge = packed[:, 4 * channels:5 * channels].reshape(HEADS, DEPTH, channels)
    merge = jnp.pad(jnp.concatenate([merge, merge], axis=1), ((0, 0), (0, LANES - 2 * DEPTH), (0, 0)))
    merge = merge.reshape(HEADS * LANES, channels)

    local = pair_bias(place, residue_numbering, chain_label, residue_presence_mask, pairwise_state,
                      pairwise_bias_weight, relative_bias_table)

    def swap(flip):
        perm = []
        for y in range(ny):
            for x in range(nxl):
                for q in range(nq):
                    perm.append(((y * nxl + x) * nq + q, (q * nxl + (x ^ flip)) * nq + y))
        return lax.ppermute(local, ("y", "xl") + HEAD_AXES, perm)

    bias = in_order(swap(0), swap(1))
    bias_a, bias_b, packed = gather_both(bias[:, :HEADS_A], bias[:, HEADS_A:], ny, nz, packed)
    bias_b, rows = lax.optimization_barrier((bias_b, lineup_embedding))
    projected = project(place, rows, lineup_scaling_coefficients, packed, quarter)
    bias_b, (kp, vp, qp, gp) = gather_y(bias_b, ny, projected)
    bias = (bias_a, bias_b)
    operand_t = jnp.swapaxes(tensor_operand_matrices, 1, 2).reshape(2 * RANK, channels)
    state, first, second = attend(place, lineup_member_flags, bias, kp, vp, qp, gp, merge,
                                  lineup_embedding, operand_t, presence, quarter)

    second = in_order(second, shift(second, "xl", nxl, 1)).reshape(nxl * count, -1)
    half = second.shape[1] // 2
    second_a, second_b, _ = gather_both(second[:, :half], second[:, half:], ny, nz)
    second_b, first, state = lax.optimization_barrier((second_b, first, state))

    parts = nz * nxl
    first = jnp.transpose(first.reshape(count, RANK, parts, block_rows), (2, 0, 3, 1))
    first = lax.all_to_all(first.reshape(parts, count, block_rows * RANK), ("z", "xl"), 0, 0, tiled=True)
    across = shift(state, "xh", nxh, 1)
    first, across = lax.optimization_barrier((first.reshape(parts * count, -1), across))
    first = [
        lax.ppermute(first, ("y",) + HEAD_AXES,
                     [(y * nq + q, q * nq + (y + r) % nq) for y in range(ny) for q in range(nq)])
        for r in (0, 2)
    ]

    pieces = [state, shift(state, "c", nc, 1), across, shift(across, "c", nc, 1)]
    second_b, _ = gather_y(second_b, ny)
    second = (second_a, second_b)
    first = first + [shift(piece, "c", nc, 1) for piece in first]

    weight_t = jnp.transpose(
        outer_output_weight.reshape(RANK, RANK, pair_channels), (2, 1, 0)
    ).reshape(pair_channels, RANK * RANK)
    count_columns = presence * jnp.sum(lineup_member_flags.astype(F32))
    pairs, state = outer_mean(place, residue_presence_mask, first, second, weight_t,
                              outer_output_bias, count_columns, pairwise_state, pieces)
    return state, pairs


def solution(mesh):
    sizes = dict(y=4, z=8, xl=2, xh=2, c=2)
    fine = Mesh(mesh.devices.reshape(tuple(sizes.values())), tuple(sizes))
    placed = (
        P(DAP_AXES, None, None),
        P(DAP_AXES, HEAD_AXES, None),
        P(),
        P(None, None, HEAD_AXES),
        P(HEAD_AXES),
        P(HEAD_AXES, None),
    ) + (P(),) * 9
    return jax.shard_map(
        partial(per_device, sizes),
        mesh=fine,
        in_specs=placed,
        out_specs=(P(DAP_AXES, None, None), P(DAP_AXES, HEAD_AXES, None)),
        check_vma=False,
    )
```

```python
import math
from functools import partial

import jax
import jax.numpy as jnp
from jax import lax
from jax.experimental import pallas as pl
from jax.experimental.pallas import tpu as pltpu
from jax.sharding import Mesh, PartitionSpec as P

F32, BF16 = jnp.float32, jnp.bfloat16
HEADS, DEPTH, RANK, BUCKETS = 8, 32, 32, 66
HEADS_A = 4
TABLE_ROWS = 72
LANES = 128
LOG2E = math.log2(math.e)
HEAD_AXES = ("xh", "c")
DAP_AXES = ("y", "z", "xl")


def dot(a, b, contract=((1,), (0,))):
    return lax.dot_general(a, b, (contract, ((), ())), preferred_element_type=F32)


def split(a):
    high = a.astype(BF16)
    return high, (a - high.astype(F32)).astype(BF16)


def dot3(a, b, contract=((1,), (0,))):
    return dot(a[0], b[0], contract) + (dot(a[0], b[1], contract) + dot(a[1], b[0], contract))


def normalize(values):
    center = values - jnp.mean(values, axis=-1, keepdims=True)
    spread = jnp.mean(center * center, axis=-1, keepdims=True)
    return center * lax.rsqrt(spread + 1e-05)


def params(n_axes, mib):
    return pltpu.CompilerParams(
        dimension_semantics=("arbitrary",) * n_axes, vmem_limit_bytes=mib * 2**20
    )


def bias_kernel(place, index_s, chain_s, pair, weight_t, table_t, index_c, chain_c, mask_c, out):
    step = pl.program_id(0)
    rows = pair.shape[0]
    columns = pair.shape[1]
    w = weight_t[...]
    table = table_t[...]
    lines = columns // LANES

    def own_columns(ref):
        return jnp.concatenate([ref[pl.ds(place[1] * lines + k, 1), :] for k in range(lines)], axis=1)

    cols_index = own_columns(index_c)
    cols_chain = own_columns(chain_c)
    mask = (own_columns(mask_c).astype(F32) - 1.0) * 1000000000.0
    reach = (BUCKETS - 2) // 2
    for r in range(rows):
        i = place[0] * (rows * pl.num_programs(0)) + step * rows + r
        normed = normalize(pair[r])
        linear = lax.dot_general(
            w, normed, (((1,), (1,)), ((), ())), precision=lax.Precision.HIGHEST,
            preferred_element_type=F32,
        )
        offset = jnp.clip(index_s[i] - cols_index, -reach, reach) + reach
        bucket = jnp.where(chain_s[i] == cols_chain, offset, BUCKETS - 1)
        classes = lax.broadcasted_iota(jnp.int32, (TABLE_ROWS, columns), 0)
        onehot = (classes == bucket).astype(F32)
        relative = lax.dot_general(
            table, onehot, (((1,), (0,)), ((), ())), precision=lax.Precision.HIGHEST,
            preferred_element_type=F32,
        )
        out[:, r, :] = (linear + relative + mask) * LOG2E


def pair_bias(place, numbering, chain, presence, pair, weight, table):
    rows, columns, channels = pair.shape
    part = 8

    def whole(shape):
        return pl.BlockSpec(shape, lambda r, *_: (0,) * len(shape))

    lines = numbering.shape[0] // LANES
    return pl.pallas_call(
        bias_kernel,
        out_shape=jax.ShapeDtypeStruct((HEADS, rows, columns), F32),
        grid_spec=pltpu.PrefetchScalarGridSpec(
            num_scalar_prefetch=3,
            grid=(rows // part,),
            in_specs=[
                pl.BlockSpec((part, columns, channels), lambda r, *_: (r, 0, 0)),
                whole((HEADS, channels)),
                whole((HEADS, TABLE_ROWS)),
            ] + [whole((lines, LANES))] * 3,
            out_specs=pl.BlockSpec((HEADS, part, columns), lambda r, *_: (0, r, 0)),
        ),
        compiler_params=params(1, 32),
        name="pair_bias",
    )(
        place, numbering, chain, pair, weight.T,
        jnp.pad(table, ((0, TABLE_ROWS - BUCKETS), (0, 0))).T,
        numbering.reshape(lines, LANES), chain.reshape(lines, LANES), presence.reshape(lines, LANES),
    )


def pack_kernel(w, merge, gate_bias, out):
    channels, narrow = w.shape[1:]
    for t in range(0, w.shape[0], 2):
        out[pl.ds(t // 2 * channels, channels), :] = jnp.concatenate([w[t], w[t + 1]], axis=1)
    start = w.shape[0] // 2 * channels
    for c in range(channels // LANES):
        out[pl.ds(start + c * narrow, narrow), :] = merge[:, c * LANES:(c + 1) * LANES]
    gate = jnp.concatenate([gate_bias[...]] * 2, axis=1)
    out[pl.ds(out.shape[0] - 8, 8), :] = jnp.broadcast_to(gate, (8, LANES))


def pack(w, merge, gate_bias):
    rows = (w.size + merge.size) // LANES + 8
    return pl.pallas_call(
        pack_kernel, out_shape=jax.ShapeDtypeStruct((rows, LANES), F32), name="pack"
    )(w, merge, gate_bias[None])


def project_kernel(place, row, own, gain, packed, kp, vp, qp, gp, wk2, wv2, wq2, wg2, gate_bias):
    channels = row.shape[2]

    @pl.when(pl.program_id(0) == 0)
    def _():
        narrow = LANES // 2
        for q in range(0, packed.shape[0], 2):
            block = pl.ds(0, channels)
            both = [packed[q + k, block, :][:, narrow:] for k in range(2)]
            both = jnp.concatenate(both, axis=1).T
            at = pl.ds(q // 2 * LANES, LANES)
            wk2[0, at], wk2[1, at] = split(both)
        for h in range(HEADS):
            q = h // 2
            at = pl.ds(h * LANES, LANES)

            def lanes(start, rows, t, copies):
                column = t % 2 * narrow + h % 2 * DEPTH
                part = packed[q, pl.ds(start, rows), :][:, column:column + DEPTH]
                rest = [jnp.zeros((rows, LANES - copies * DEPTH), F32)] if copies * DEPTH < LANES else []
                return jnp.concatenate([part] * copies + rest, axis=1)

            for t, copies, target in ((0, 4, wq2), (2, 2, wv2), (3, 2, wg2)):
                target[0, :, at], target[1, :, at] = split(lanes(t // 2 * channels, channels, t, copies))
            gate_bias[:, at] = lanes(packed.shape[1] - 8, 8, 0, 2)[:1]

    positions = row.shape[1]
    own_positions = own.shape[1]
    n = split(normalize(row[0]) * gain[...])
    keys = split(dot3((wk2[0], wk2[1]), n, ((1,), (1,))))
    for h in range(HEADS):
        for part in range(4):
            kp[0, h, pl.ds(part * DEPTH, DEPTH), :] = keys[part % 2][h * DEPTH:(h + 1) * DEPTH]
    pair_lanes = 2 * LANES
    lane = lax.broadcasted_iota(jnp.int32, (positions, LANES), 1)
    for h in range(0, HEADS, 2):
        cut = pl.ds(h * LANES, pair_lanes)
        both = dot3(n, (wv2[0, :, cut], wv2[1, :, cut]))
        for k in range(2):
            value = both[:, k * LANES:(k + 1) * LANES]
            high = value.astype(BF16).astype(F32)
            packed = jnp.where(lane < DEPTH, high, jnp.where(lane < 2 * DEPTH, value - high, 1.0))
            vp[0, h + k] = packed.astype(BF16)
    m = split(normalize(own[0]) * gain[...])
    lane = lax.broadcasted_iota(jnp.int32, (own_positions, LANES), 1)
    for h in range(0, HEADS, 2):
        cut = pl.ds(h * LANES, pair_lanes)
        both = dot3(m, (wq2[0, :, cut], wq2[1, :, cut])) * (LOG2E / math.sqrt(DEPTH))
        gates = dot3(m, (wg2[0, :, cut], wg2[1, :, cut])) + gate_bias[:, cut]
        gates = jax.nn.sigmoid(gates)
        for k in range(2):
            value = both[:, k * LANES:(k + 1) * LANES]
            high = value.astype(BF16).astype(F32)
            qp[0, h + k] = jnp.where(lane < 2 * DEPTH, high, value - high).astype(BF16)
            gp[0, h + k] = gates[:, k * LANES:(k + 1) * LANES]


def project(place, rows, gain, packed, quarter):
    count, positions, channels = rows.shape
    wide = HEADS * LANES

    def whole(shape):
        return pl.BlockSpec(shape, lambda s, place: (0,) * len(shape))

    def out(rows_, columns, dtype):
        return (
            jax.ShapeDtypeStruct((count, HEADS, rows_, columns), dtype),
            pl.BlockSpec((1, HEADS, rows_, columns), lambda s, place: (s, 0, 0, 0)),
        )

    outs = [out(LANES, positions, BF16), out(positions, LANES, BF16),
            out(quarter, LANES, BF16), out(quarter, LANES, F32)]
    return pl.pallas_call(
        project_kernel,
        out_shape=[o[0] for o in outs],
        grid_spec=pltpu.PrefetchScalarGridSpec(
            num_scalar_prefetch=1,
            grid=(count,),
            in_specs=[
                pl.BlockSpec((1, positions, channels), lambda s, place: (s, 0, 0)),
                pl.BlockSpec((1, quarter, channels), lambda s, place: (s, place[1], 0)),
                whole((1, channels)), whole(packed.shape),
            ],
            out_specs=[o[1] for o in outs],
            scratch_shapes=[pltpu.VMEM((2, HEADS * DEPTH, channels), BF16)]
            + [pltpu.VMEM((2, channels, wide), BF16)] * 3 + [pltpu.VMEM((1, wide), F32)],
        ),
        compiler_params=params(1, 52),
        name="project",
    )(place, rows, rows, gain[None], packed)


def attend_kernel(place, flags_s, bias_a, b0, b1, b2, b3, b4, kp, vp, qp, gp, merge, own, operand_t,
                  mask_c, state_out, first_out, second_out, gated, head_bias, merge_rows):
    h = pl.program_id(0)
    count = own.shape[0]
    quarter = own.shape[1]
    nz, ny, width = bias_a.shape[0], bias_a.shape[1], bias_a.shape[5]
    group = quarter // nz

    def columns(k):
        return pl.ds(pl.multiple_of(lax.rem(place[2] + Y_STEPS[k], ny) * width, width), width)

    def rows(k):
        return pl.ds(pl.multiple_of(lax.rem(place[3] + Z_STEPS[k], nz) * group, group), group)

    @pl.when(h < HEADS_A)
    def _():
        for k in range(ny):
            head_bias[:, columns(k)] = bias_a[:, k, :, 0].reshape(quarter, width)

    @pl.when(h >= HEADS_A)
    def _():
        for y, pieces in enumerate(((b0,), (b1,), (b2,), (b3, b4))):
            k = 0
            for piece in pieces:
                for line in range(piece.shape[0]):
                    head_bias[rows(k), columns(y)] = piece[line, :, 0].reshape(group, width)
                    k += 1

    lane = lax.broadcasted_iota(jnp.int32, (quarter, LANES), 1)
    ahead = dot(qp[0, 0], kp[0, 0]) + head_bias[...]
    for s in range(count):
        logits = ahead
        if s + 1 < count:
            ahead = dot(qp[s + 1, 0], kp[s + 1, 0]) + head_bias[...]
        peak = jnp.max(logits, axis=1, keepdims=True)
        weights = jnp.exp2(logits - peak)
        mixed = dot(jnp.concatenate(split(weights), axis=0), vp[s, 0])
        mixed = mixed[:quarter] + mixed[quarter:]
        total_weight = jnp.where(lane < 2 * DEPTH, pltpu.roll(mixed, LANES // 2, 1), 1.0)
        parts = split(jnp.where(lane < 2 * DEPTH, mixed * gp[s, 0] / total_weight, 0.0))
        at = pl.ds(pl.multiple_of(h * LANES, LANES), LANES)
        gated[0, s, :, at], gated[1, s, :, at] = parts

    @pl.when(h == pl.num_programs(0) - 1)
    def _():
        ops = split(operand_t[...])
        merge_rows[...] = jnp.zeros_like(merge_rows)
        narrow = merge.shape[1] * LANES // own.shape[2]
        for k in range(HEADS):
            start = k % 2 * DEPTH
            rows_k = [merge[k // 2, pl.ds(c + start, DEPTH), :] for c in range(0, merge.shape[1], narrow)]
            for copy in range(2):
                merge_rows[pl.ds(k * LANES + copy * DEPTH, DEPTH), :] = jnp.concatenate(rows_k, axis=1)
        m2 = split(merge_rows[...])
        for s in range(count):
            state = own[s] + dot3((gated[0, s], gated[1, s]), m2)
            state_out[s] = state
            n = split(normalize(state))
            flag = flags_s[place[0] * count + s].astype(F32)
            factors = dot3(ops, n, ((1,), (1,))) * (mask_c[0] * flag)
            first_out[s] = factors[:RANK]
            for e in range(RANK):
                second_out[pl.ds(s, 1), pl.ds(e * quarter, quarter)] = factors[RANK + e:RANK + e + 1]


def attend(place, flags, bias, kp, vp, qp, gp, merge, rows, operand_t, mask, quarter):
    count, positions, channels = rows.shape

    merge_size = HEADS * DEPTH // merge.shape[0] * channels // LANES

    def piece_block(piece, low, high):
        shape = list(piece.shape)
        shape[-3] = 1

        def at(h, *_):
            index = [0] * len(shape)
            index[-3] = jnp.clip(h - low, 0, high)
            return tuple(index)

        return pl.BlockSpec(tuple(shape), at)

    def head_block(rows_, columns):
        return pl.BlockSpec((count, 1, rows_, columns), lambda h, *_: (0, h, 0, 0))

    return pl.pallas_call(
        attend_kernel,
        out_shape=[
            jax.ShapeDtypeStruct((count, quarter, channels), F32),
            jax.ShapeDtypeStruct((count, RANK, quarter), F32),
            jax.ShapeDtypeStruct((count, RANK * quarter), F32),
        ],
        grid_spec=pltpu.PrefetchScalarGridSpec(
            num_scalar_prefetch=2,
            grid=(HEADS,),
            in_specs=[
                piece_block(bias[0], 0, HEADS_A - 1),
            ] + [piece_block(piece, HEADS_A, HEADS - HEADS_A - 1) for piece in bias[1]] + [
                head_block(LANES, positions), head_block(positions, LANES),
                head_block(quarter, LANES), head_block(quarter, LANES),
                pl.BlockSpec((merge.shape[0], merge_size, LANES),
                             lambda h, *_: (0, 2 * channels // merge_size, 0)),
                pl.BlockSpec((count, quarter, channels), lambda h, place, *_: (0, place[1], 0)),
                pl.BlockSpec((2 * RANK, channels), lambda h, *_: (0, 0)),
                pl.BlockSpec((1, 1, quarter), lambda h, place, *_: (place[1], 0, 0)),
            ],
            out_specs=[
                pl.BlockSpec((count, quarter, channels), lambda h, *_: (0, 0, 0)),
                pl.BlockSpec((count, RANK, quarter), lambda h, *_: (0, 0, 0)),
                pl.BlockSpec((count, RANK * quarter), lambda h, *_: (0, 0)),
            ],
            scratch_shapes=[
                pltpu.VMEM((2, count, quarter, HEADS * LANES), BF16),
                pltpu.VMEM((quarter, positions), F32),
                pltpu.VMEM((HEADS * LANES, channels), F32),
            ],
        ),
        compiler_params=params(1, 52),
        name="attend",
    )(place, flags, bias[0], *bias[1], kp, vp, qp, gp, merge, rows, operand_t, mask.reshape(-1, 1, quarter))


def outer_kernel(group, place, mask_s, f0, f1, sa, s0, s1, s2, s3, s4, weight_t, out_bias,
                 count_c, pair, t0, t1, t2, t3, out, state, ordered, moved, a2, w2, r2):
    step = pl.program_id(0)
    steps = RANK // group
    i_rows = r2.shape[1]
    columns = pair.shape[1]
    nz, ny, eight = sa.shape[0], sa.shape[1], sa.shape[2]
    y_at = [lax.rem(place[2] + k, ny) for k in Y_STEPS]
    z_at = [lax.rem(place[3] + k, nz) for k in Z_STEPS]

    def row(y, z):
        return pl.ds(pl.multiple_of((y * nz + z) * eight, eight), eight)

    @pl.when(step == 0)
    def _():
        high, low = split(weight_t[...])
        w2[:LANES], w2[LANES:] = high, low
        for r, piece in enumerate((f0, f1)):
            size = piece.shape[1]
            for k in range(piece.shape[0]):
                y = lax.rem((place[1] ^ r) + 2 * k, ny)
                ordered[pl.ds(pl.multiple_of(y * size, size), size), :] = piece[k]
        for z in range(nz):
            for k in range(ny):
                moved[pl.ds((z * ny + k) * eight, eight), :] = ordered[row(y_at[k], z), :]
        a2[0], a2[1] = split(moved[...].T)

    @pl.when(step == steps // 2)
    def _():
        for k in range(ny):
            for z in range(nz):
                moved[pl.ds((k * nz + z) * eight, eight), :] = ordered[row(y_at[k], z_at[z]), :]
        a2[0], a2[1] = split(moved[...].T)

    def products(blocks):
        for g in range(group):
            cut = pl.ds(g * columns, columns)
            b = [block[..., cut].reshape(-1, columns) for block in blocks]
            b = split(b[0] if len(b) == 1 else jnp.concatenate(b, axis=0))
            r = split(dot3((a2[0], a2[1]), b))
            at = pl.multiple_of((step * group + g) * RANK, RANK)
            for part in range(2):
                for i in range(i_rows):
                    r2[part, i, pl.ds(at, RANK), :] = r[part][i * RANK:(i + 1) * RANK]

    @pl.when(step < steps // 2)
    def _():
        products((sa,))

    @pl.when((step >= steps // 2) & (step < steps))
    def _():
        products((s0, s1, s2, s3, s4))

    @pl.when(step >= steps)
    def _():
        for k in range(pair.shape[0]):
            i = (step - steps) * pair.shape[0] + k
            both = dot(w2[...], r2[0, i])
            value = both[:LANES] + (both[LANES:] + dot(w2[:LANES], r2[1, i])) + out_bias[...]
            count = jnp.maximum(mask_s[place[0] * i_rows + i].astype(F32) * count_c[0], 1.0)
            out[k] = pair[k] + (value / count).T
        for k, piece in enumerate((t0, t1, t2, t3)):
            @pl.when((step - steps) // 2 == k)
            def _(piece=piece):
                state[...] = piece[...]


def outer_mean(place, mask, first, second, weight_t, out_bias, count, pair, state):
    rows, columns, channels = pair.shape
    members = sum(piece.shape[0] * piece.shape[1] for piece in first)
    wide = rows * RANK
    group = 8
    steps = RANK // group
    half = steps // 2
    part = 2
    count_s, quarter, features = state[0].shape
    lines = count_s // 2
    whole_state = (count_s, quarter * len(state), features)

    def state_block(t, place, *_):
        at = jnp.clip(t - steps, 0, 2 * len(state) - 1)
        return (lax.rem(at, 2), place[1] ^ (at // 2), 0)

    def own(t, *_):
        return (jnp.maximum(t - steps, 0), 0, 0)

    def whole(shape):
        return pl.BlockSpec(shape, lambda t, *_: (0,) * len(shape))

    def columns_block(piece, low):
        lead = piece.shape[:-1]
        return pl.BlockSpec(
            lead + (group * columns,),
            lambda t, *_: (0,) * len(lead) + (jnp.clip(t - low, 0, half - 1),),
        )

    return pl.pallas_call(
        partial(outer_kernel, group),
        out_shape=[
            jax.ShapeDtypeStruct(pair.shape, F32),
            jax.ShapeDtypeStruct(whole_state, F32),
        ],
        grid_spec=pltpu.PrefetchScalarGridSpec(
            num_scalar_prefetch=2,
            grid=(steps + rows // part,),
            in_specs=[whole(piece.shape) for piece in first]
            + [columns_block(second[0], 0)]
            + [columns_block(piece, half) for piece in second[1]]
            + [
                whole((channels, RANK * RANK)),
                whole((channels, 1)),
                pl.BlockSpec((1, 1, columns), lambda t, place, *_: (place[1], 0, 0)),
                pl.BlockSpec((part, columns, channels), own),
            ] + [
                pl.BlockSpec((lines, quarter, features),
                             lambda t, *_, k=k: (jnp.clip(t - steps - 2 * k, 0, 1), 0, 0))
                for k in range(len(state))
            ],
            out_specs=[pl.BlockSpec((part, columns, channels), own),
                       pl.BlockSpec((lines, quarter, features), state_block)],
            scratch_shapes=[
                pltpu.VMEM((members, wide), F32),
                pltpu.VMEM((members, wide), F32),
                pltpu.VMEM((2, wide, members), BF16),
                pltpu.VMEM((2 * channels, RANK * RANK), BF16),
                pltpu.VMEM((2, rows, RANK * RANK, columns), BF16),
            ],
        ),
        compiler_params=params(1, 52),
        name="outer_mean",
    )(place, mask, *first, second[0], *second[1], weight_t, out_bias[:, None],
      count.reshape(-1, 1, columns), pair, *state)


Y_STEPS = (0, 3, 1, 2)
Z_STEPS = (0, 7, 1, 6, 2, 5, 3, 4)


def shift(block, axis, size, step):
    return lax.ppermute(block, axis, [(i, (i + step) % size) for i in range(size)])


def gather_both(block_a, block_b, ny, nz, early=()):
    along = [shift(block_a, "y", ny, -k) for k in Y_STEPS[1:]]
    one = [shift(block_b, "z", nz, k) for k in (1, -1)]
    two = [shift(block_b, "z", nz, k) for k in (2, -2)]
    along, early = lax.optimization_barrier((along, early))
    gathered_a = lax.all_gather(jnp.stack([block_a] + along), "z")
    three = [shift(one[0], "z", nz, 2), shift(one[1], "z", nz, -2)]
    cut = block_b.shape[0] // 2
    four = [shift(two[0][:cut], "z", nz, 2), shift(two[1][cut:], "z", nz, -2)]
    gathered_b = jnp.stack([block_b] + one + two + three + [jnp.concatenate(four)])
    return gathered_a, gathered_b, early


def gather_y(block, ny, beside=()):
    one = [shift(block, "y", ny, k) for k in (1, -1)]
    one, beside = lax.optimization_barrier((one, beside))
    cut = block.shape[0] // 2
    two = [shift(one[0][:cut], "y", ny, 1), shift(one[1][cut:], "y", ny, -1)]
    return [block] + one + two, beside


def in_order(mine, other):
    low = lax.axis_index("xl") == 0
    return jnp.stack([jnp.where(low, mine, other), jnp.where(low, other, mine)])


def per_device(
    sizes,
    lineup_embedding,
    pairwise_state,
    lineup_scaling_coefficients,
    focus_projection_matrix,
    attention_gate_bias,
    focus_merge_matrix,
    pairwise_bias_weight,
    relative_bias_table,
    tensor_operand_matrices,
    outer_output_weight,
    outer_output_bias,
    lineup_member_flags,
    residue_presence_mask,
    chain_label,
    residue_numbering,
):
    ny, nz, nxl, nxh, nc = (sizes[a] for a in ("y", "z", "xl", "xh", "c"))
    nq = nxh * nc
    dap = (lax.axis_index("y") * nz + lax.axis_index("z")) * nxl + lax.axis_index("xl")
    head = lax.axis_index("xh") * nc + lax.axis_index("c")
    place = jnp.stack([dap, head, lax.axis_index("y"), lax.axis_index("z")]).astype(jnp.int32)
    count, positions, channels = lineup_embedding.shape
    block_rows, quarter, pair_channels = pairwise_state.shape
    presence = residue_presence_mask.astype(F32)

    packed = pack(focus_projection_matrix, focus_merge_matrix, attention_gate_bias)
    packed, pairwise_state = lax.optimization_barrier((packed, pairwise_state))
    packed = lax.all_gather(packed, HEAD_AXES)

    local = pair_bias(place, residue_numbering, chain_label, residue_presence_mask, pairwise_state,
                      pairwise_bias_weight, relative_bias_table)

    def swap(flip):
        perm = []
        for y in range(ny):
            for x in range(nxl):
                for q in range(nq):
                    perm.append(((y * nxl + x) * nq + q, (q * nxl + (x ^ flip)) * nq + y))
        return lax.ppermute(local, ("y", "xl") + HEAD_AXES, perm)

    bias = in_order(swap(0), swap(1))
    bias_a, bias_b, packed = gather_both(bias[:, :HEADS_A], bias[:, HEADS_A:], ny, nz, packed)
    bias_b, rows = lax.optimization_barrier((bias_b, lineup_embedding))
    projected = project(place, rows, lineup_scaling_coefficients, packed, quarter)
    bias_b, (kp, vp, qp, gp) = gather_y(bias_b, ny, projected)
    bias = (bias_a, bias_b)
    operand_t = jnp.swapaxes(tensor_operand_matrices, 1, 2).reshape(2 * RANK, channels)
    state, first, second = attend(place, lineup_member_flags, bias, kp, vp, qp, gp, packed,
                                  lineup_embedding, operand_t, presence, quarter)

    second = in_order(second, shift(second, "xl", nxl, 1)).reshape(nxl * count, -1)
    half = second.shape[1] // 2
    second_a, second_b, _ = gather_both(second[:, :half], second[:, half:], ny, nz)
    second_b, first, state = lax.optimization_barrier((second_b, first, state))

    parts = nz * nxl
    first = jnp.transpose(first.reshape(count, RANK, parts, block_rows), (2, 0, 3, 1))
    first = lax.all_to_all(first.reshape(parts, count, block_rows * RANK), ("z", "xl"), 0, 0, tiled=True)
    across = shift(state, "xh", nxh, 1)
    first, across = lax.optimization_barrier((first.reshape(parts * count, -1), across))
    first = [
        lax.ppermute(first, ("y",) + HEAD_AXES,
                     [(y * nq + q, q * nq + (y + r) % nq) for y in range(ny) for q in range(nq)])
        for r in (0, 2)
    ]

    pieces = [state, shift(state, "c", nc, 1), across, shift(across, "c", nc, 1)]
    second_b, _ = gather_y(second_b, ny)
    second = (second_a, second_b)
    first = jnp.stack(first)
    first = [first, shift(first, "c", nc, 1)]

    weight_t = jnp.transpose(
        outer_output_weight.reshape(RANK, RANK, pair_channels), (2, 1, 0)
    ).reshape(pair_channels, RANK * RANK)
    count_columns = presence * jnp.sum(lineup_member_flags.astype(F32))
    pairs, state = outer_mean(place, residue_presence_mask, first, second, weight_t,
                              outer_output_bias, count_columns, pairwise_state, pieces)
    return state, pairs


def solution(mesh):
    sizes = dict(y=4, z=8, xl=2, xh=2, c=2)
    fine = Mesh(mesh.devices.reshape(tuple(sizes.values())), tuple(sizes))
    placed = (
        P(DAP_AXES, None, None),
        P(DAP_AXES, HEAD_AXES, None),
        P(),
        P(None, None, HEAD_AXES),
        P(HEAD_AXES),
        P(HEAD_AXES, None),
    ) + (P(),) * 9
    return jax.shard_map(
        partial(per_device, sizes),
        mesh=fine,
        in_specs=placed,
        out_specs=(P(DAP_AXES, None, None), P(DAP_AXES, HEAD_AXES, None)),
        check_vma=False,
    )
```

```python
import math
from functools import partial

import jax
import jax.numpy as jnp
from jax import lax
from jax.experimental import pallas as pl
from jax.experimental.pallas import tpu as pltpu
from jax.sharding import Mesh, PartitionSpec as P

F32, BF16 = jnp.float32, jnp.bfloat16
HEADS, DEPTH, RANK, BUCKETS = 8, 32, 32, 66
HEADS_A = 4
TABLE_ROWS = 72
LANES = 128
LOG2E = math.log2(math.e)
HEAD_AXES = ("xh", "c")
DAP_AXES = ("y", "z", "xl")


def dot(a, b, contract=((1,), (0,))):
    return lax.dot_general(a, b, (contract, ((), ())), preferred_element_type=F32)


def split(a):
    high = a.astype(BF16)
    return high, (a - high.astype(F32)).astype(BF16)


def dot3(a, b, contract=((1,), (0,))):
    return dot(a[0], b[0], contract) + (dot(a[0], b[1], contract) + dot(a[1], b[0], contract))


def normalize(values):
    center = values - jnp.mean(values, axis=-1, keepdims=True)
    spread = jnp.mean(center * center, axis=-1, keepdims=True)
    return center * lax.rsqrt(spread + 1e-05)


def params(n_axes, mib):
    return pltpu.CompilerParams(
        dimension_semantics=("arbitrary",) * n_axes, vmem_limit_bytes=mib * 2**20
    )


def bias_kernel(place, index_s, chain_s, pair, weight_t, table_t, index_c, chain_c, mask_c, out):
    step = pl.program_id(0)
    rows = pair.shape[0]
    columns = pair.shape[1]
    w = weight_t[...]
    table = table_t[...]
    lines = columns // LANES

    def own_columns(ref):
        return jnp.concatenate([ref[pl.ds(place[1] * lines + k, 1), :] for k in range(lines)], axis=1)

    cols_index = own_columns(index_c)
    cols_chain = own_columns(chain_c)
    mask = (own_columns(mask_c).astype(F32) - 1.0) * 1000000000.0
    reach = (BUCKETS - 2) // 2
    for r in range(rows):
        i = place[0] * (rows * pl.num_programs(0)) + step * rows + r
        normed = normalize(pair[r])
        linear = lax.dot_general(
            w, normed, (((1,), (1,)), ((), ())), precision=lax.Precision.HIGHEST,
            preferred_element_type=F32,
        )
        offset = jnp.clip(index_s[i] - cols_index, -reach, reach) + reach
        bucket = jnp.where(chain_s[i] == cols_chain, offset, BUCKETS - 1)
        classes = lax.broadcasted_iota(jnp.int32, (TABLE_ROWS, columns), 0)
        onehot = (classes == bucket).astype(F32)
        relative = lax.dot_general(
            table, onehot, (((1,), (0,)), ((), ())), precision=lax.Precision.HIGHEST,
            preferred_element_type=F32,
        )
        out[:, r, :] = (linear + relative + mask) * LOG2E


def pair_bias(place, numbering, chain, presence, pair, weight, table):
    rows, columns, channels = pair.shape
    part = 8

    def whole(shape):
        return pl.BlockSpec(shape, lambda r, *_: (0,) * len(shape))

    lines = numbering.shape[0] // LANES
    return pl.pallas_call(
        bias_kernel,
        out_shape=jax.ShapeDtypeStruct((HEADS, rows, columns), F32),
        grid_spec=pltpu.PrefetchScalarGridSpec(
            num_scalar_prefetch=3,
            grid=(rows // part,),
            in_specs=[
                pl.BlockSpec((part, columns, channels), lambda r, *_: (r, 0, 0)),
                whole((HEADS, channels)),
                whole((HEADS, TABLE_ROWS)),
            ] + [whole((lines, LANES))] * 3,
            out_specs=pl.BlockSpec((HEADS, part, columns), lambda r, *_: (0, r, 0)),
        ),
        compiler_params=params(1, 32),
        name="pair_bias",
    )(
        place, numbering, chain, pair, weight.T,
        jnp.pad(table, ((0, TABLE_ROWS - BUCKETS), (0, 0))).T,
        numbering.reshape(lines, LANES), chain.reshape(lines, LANES), presence.reshape(lines, LANES),
    )


def pack_kernel(w, merge, gate_bias, out):
    rows = w.shape[0] * w.shape[1]
    for t in range(w.shape[0]):
        out[pl.ds(t * w.shape[1], w.shape[1]), :] = w[t]
    out[pl.ds(rows, merge.shape[0]), :] = merge[...]
    copies = out.shape[1] // gate_bias.shape[1]
    gate = jnp.concatenate([gate_bias[...]] * copies, axis=1)
    out[pl.ds(out.shape[0] - 8, 8), :] = jnp.broadcast_to(gate, (8, out.shape[1]))


def pack(w, merge, gate_bias):
    w = jnp.swapaxes(w, 1, 2)
    rows = w.shape[0] * w.shape[1] + merge.shape[0] + 8
    return pl.pallas_call(
        pack_kernel, out_shape=jax.ShapeDtypeStruct((rows, merge.shape[1]), F32), name="pack"
    )(w, merge, gate_bias[None])


def project_kernel(place, row, own, gain, packed, kp, vp, qp, gp, wk2, wv2, wq2, wg2, gate_bias):
    channels = row.shape[2]

    @pl.when(pl.program_id(0) == 0)
    def _():
        narrow = HEADS * DEPTH // packed.shape[0]
        for q in range(packed.shape[0]):
            at = pl.ds(q * narrow, narrow)
            wk2[0, at], wk2[1, at] = split(packed[q, pl.ds(narrow, narrow), :])
        for h in range(HEADS):
            q, start = h // 2, h % 2 * DEPTH
            at = pl.ds(h * LANES, LANES)
            for t, copies, target in ((0, 4, wq2), (2, 2, wv2), (3, 2, wg2)):
                part = packed[q, pl.ds(t * narrow + start, DEPTH), :]
                rest = [jnp.zeros((LANES - copies * DEPTH, channels), F32)] if copies * DEPTH < LANES else []
                target[0, at], target[1, at] = split(jnp.concatenate([part] * copies + rest, axis=0))
            gate = packed[q, pl.ds(packed.shape[1] - 8, 8), :][:1, start:start + DEPTH]
            gate_bias[:, at] = jnp.concatenate([gate, gate, jnp.zeros((1, LANES - 2 * DEPTH), F32)], axis=1)

    positions = row.shape[1]
    own_positions = own.shape[1]
    n = split(normalize(row[0]) * gain[...])
    keys = split(dot3((wk2[0], wk2[1]), n, ((1,), (1,))))
    for h in range(HEADS):
        for part in range(4):
            kp[0, h, pl.ds(part * DEPTH, DEPTH), :] = keys[part % 2][h * DEPTH:(h + 1) * DEPTH]
    pair_lanes = 2 * LANES
    lane = lax.broadcasted_iota(jnp.int32, (positions, LANES), 1)
    for h in range(0, HEADS, 2):
        cut = pl.ds(h * LANES, pair_lanes)
        both = dot3(n, (wv2[0, cut], wv2[1, cut]), ((1,), (1,)))
        for k in range(2):
            value = both[:, k * LANES:(k + 1) * LANES]
            high = value.astype(BF16).astype(F32)
            packed = jnp.where(lane < DEPTH, high, jnp.where(lane < 2 * DEPTH, value - high, 1.0))
            vp[0, h + k] = packed.astype(BF16)
    m = split(normalize(own[0]) * gain[...])
    lane = lax.broadcasted_iota(jnp.int32, (own_positions, LANES), 1)
    for h in range(0, HEADS, 2):
        cut = pl.ds(h * LANES, pair_lanes)
        both = dot3(m, (wq2[0, cut], wq2[1, cut]), ((1,), (1,))) * (LOG2E / math.sqrt(DEPTH))
        gates = dot3(m, (wg2[0, cut], wg2[1, cut]), ((1,), (1,))) + gate_bias[:, cut]
        gates = jax.nn.sigmoid(gates)
        for k in range(2):
            value = both[:, k * LANES:(k + 1) * LANES]
            high = value.astype(BF16).astype(F32)
            qp[0, h + k] = jnp.where(lane < 2 * DEPTH, high, value - high).astype(BF16)
            gp[0, h + k] = gates[:, k * LANES:(k + 1) * LANES]


def project(place, rows, gain, packed, quarter):
    count, positions, channels = rows.shape
    wide = HEADS * LANES

    def whole(shape):
        return pl.BlockSpec(shape, lambda s, place: (0,) * len(shape))

    def out(rows_, columns, dtype):
        return (
            jax.ShapeDtypeStruct((count, HEADS, rows_, columns), dtype),
            pl.BlockSpec((1, HEADS, rows_, columns), lambda s, place: (s, 0, 0, 0)),
        )

    outs = [out(LANES, positions, BF16), out(positions, LANES, BF16),
            out(quarter, LANES, BF16), out(quarter, LANES, F32)]
    return pl.pallas_call(
        project_kernel,
        out_shape=[o[0] for o in outs],
        grid_spec=pltpu.PrefetchScalarGridSpec(
            num_scalar_prefetch=1,
            grid=(count,),
            in_specs=[
                pl.BlockSpec((1, positions, channels), lambda s, place: (s, 0, 0)),
                pl.BlockSpec((1, quarter, channels), lambda s, place: (s, place[1], 0)),
                whole((1, channels)), whole(packed.shape),
            ],
            out_specs=[o[1] for o in outs],
            scratch_shapes=[pltpu.VMEM((2, HEADS * DEPTH, channels), BF16)]
            + [pltpu.VMEM((2, wide, channels), BF16)] * 3 + [pltpu.VMEM((1, wide), F32)],
        ),
        compiler_params=params(1, 52),
        name="project",
    )(place, rows, rows, gain[None], packed)


def attend_kernel(place, flags_s, bias_a, b0, b1, b2, b3, b4, kp, vp, qp, gp, merge, own, operand_t,
                  mask_c, state_out, first_out, second_out, gated, head_bias, merge_rows):
    h = pl.program_id(0)
    count = own.shape[0]
    quarter = own.shape[1]
    nz, ny, width = bias_a.shape[0], bias_a.shape[1], bias_a.shape[5]
    group = quarter // nz

    def columns(k):
        return pl.ds(pl.multiple_of(lax.rem(place[2] + Y_STEPS[k], ny) * width, width), width)

    def rows(k):
        return pl.ds(pl.multiple_of(lax.rem(place[3] + Z_STEPS[k], nz) * group, group), group)

    @pl.when(h < HEADS_A)
    def _():
        for k in range(ny):
            head_bias[:, columns(k)] = bias_a[:, k, :, 0].reshape(quarter, width)

    @pl.when(h >= HEADS_A)
    def _():
        for y, pieces in enumerate(((b0,), (b1,), (b2,), (b3, b4))):
            k = 0
            for piece in pieces:
                for line in range(piece.shape[0]):
                    head_bias[rows(k), columns(y)] = piece[line, :, 0].reshape(group, width)
                    k += 1

    lane = lax.broadcasted_iota(jnp.int32, (quarter, LANES), 1)
    ahead = dot(qp[0, 0], kp[0, 0]) + head_bias[...]
    for s in range(count):
        logits = ahead
        if s + 1 < count:
            ahead = dot(qp[s + 1, 0], kp[s + 1, 0]) + head_bias[...]
        peak = jnp.max(logits, axis=1, keepdims=True)
        weights = jnp.exp2(logits - peak)
        mixed = dot(jnp.concatenate(split(weights), axis=0), vp[s, 0])
        mixed = mixed[:quarter] + mixed[quarter:]
        total_weight = jnp.where(lane < 2 * DEPTH, pltpu.roll(mixed, LANES // 2, 1), 1.0)
        parts = split(jnp.where(lane < 2 * DEPTH, mixed * gp[s, 0] / total_weight, 0.0))
        at = pl.ds(pl.multiple_of(h * LANES, LANES), LANES)
        gated[0, s, :, at], gated[1, s, :, at] = parts

    @pl.when(h == pl.num_programs(0) - 1)
    def _():
        ops = split(operand_t[...])
        merge_rows[...] = jnp.zeros_like(merge_rows)
        for k in range(HEADS):
            rows_k = merge[k // 2, pl.ds(k % 2 * DEPTH, DEPTH), :]
            for copy in range(2):
                merge_rows[pl.ds(k * LANES + copy * DEPTH, DEPTH), :] = rows_k
        m2 = split(merge_rows[...])
        for s in range(count):
            state = own[s] + dot3((gated[0, s], gated[1, s]), m2)
            state_out[s] = state
            n = split(normalize(state))
            flag = flags_s[place[0] * count + s].astype(F32)
            factors = dot3(ops, n, ((1,), (1,))) * (mask_c[0] * flag)
            first_out[s] = factors[:RANK]
            for e in range(RANK):
                second_out[pl.ds(s, 1), pl.ds(e * quarter, quarter)] = factors[RANK + e:RANK + e + 1]


def attend(place, flags, bias, kp, vp, qp, gp, merge, rows, operand_t, mask, quarter):
    count, positions, channels = rows.shape

    merge_size = HEADS * DEPTH // merge.shape[0]

    def piece_block(piece, low, high):
        shape = list(piece.shape)
        shape[-3] = 1

        def at(h, *_):
            index = [0] * len(shape)
            index[-3] = jnp.clip(h - low, 0, high)
            return tuple(index)

        return pl.BlockSpec(tuple(shape), at)

    def head_block(rows_, columns):
        return pl.BlockSpec((count, 1, rows_, columns), lambda h, *_: (0, h, 0, 0))

    return pl.pallas_call(
        attend_kernel,
        out_shape=[
            jax.ShapeDtypeStruct((count, quarter, channels), F32),
            jax.ShapeDtypeStruct((count, RANK, quarter), F32),
            jax.ShapeDtypeStruct((count, RANK * quarter), F32),
        ],
        grid_spec=pltpu.PrefetchScalarGridSpec(
            num_scalar_prefetch=2,
            grid=(HEADS,),
            in_specs=[
                piece_block(bias[0], 0, HEADS_A - 1),
            ] + [piece_block(piece, HEADS_A, HEADS - HEADS_A - 1) for piece in bias[1]] + [
                head_block(LANES, positions), head_block(positions, LANES),
                head_block(quarter, LANES), head_block(quarter, LANES),
                pl.BlockSpec((merge.shape[0], merge_size, channels), lambda h, *_: (0, 4, 0)),
                pl.BlockSpec((count, quarter, channels), lambda h, place, *_: (0, place[1], 0)),
                pl.BlockSpec((2 * RANK, channels), lambda h, *_: (0, 0)),
                pl.BlockSpec((1, 1, quarter), lambda h, place, *_: (place[1], 0, 0)),
            ],
            out_specs=[
                pl.BlockSpec((count, quarter, channels), lambda h, *_: (0, 0, 0)),
                pl.BlockSpec((count, RANK, quarter), lambda h, *_: (0, 0, 0)),
                pl.BlockSpec((count, RANK * quarter), lambda h, *_: (0, 0)),
            ],
            scratch_shapes=[
                pltpu.VMEM((2, count, quarter, HEADS * LANES), BF16),
                pltpu.VMEM((quarter, positions), F32),
                pltpu.VMEM((HEADS * LANES, channels), F32),
            ],
        ),
        compiler_params=params(1, 52),
        name="attend",
    )(place, flags, bias[0], *bias[1], kp, vp, qp, gp, merge, rows, operand_t, mask.reshape(-1, 1, quarter))


def outer_kernel(group, place, mask_s, f0, f1, sa, s0, s1, s2, s3, s4, weight_t, out_bias,
                 count_c, pair, t0, t1, t2, t3, out, state, ordered, moved, a2, w2, r2):
    step = pl.program_id(0)
    steps = RANK // group
    i_rows = r2.shape[1]
    columns = pair.shape[1]
    nz, ny, eight = sa.shape[0], sa.shape[1], sa.shape[2]
    y_at = [lax.rem(place[2] + k, ny) for k in Y_STEPS]
    z_at = [lax.rem(place[3] + k, nz) for k in Z_STEPS]

    def row(y, z):
        return pl.ds(pl.multiple_of((y * nz + z) * eight, eight), eight)

    @pl.when(step == 0)
    def _():
        high, low = split(weight_t[...])
        w2[:LANES], w2[LANES:] = high, low
        for r, piece in enumerate((f0, f1)):
            size = piece.shape[1]
            for k in range(piece.shape[0]):
                y = lax.rem((place[1] ^ r) + 2 * k, ny)
                ordered[pl.ds(pl.multiple_of(y * size, size), size), :] = piece[k]
        for z in range(nz):
            for k in range(ny):
                moved[pl.ds((z * ny + k) * eight, eight), :] = ordered[row(y_at[k], z), :]
        a2[0], a2[1] = split(moved[...].T)

    @pl.when(step == steps // 2)
    def _():
        for k in range(ny):
            for z in range(nz):
                moved[pl.ds((k * nz + z) * eight, eight), :] = ordered[row(y_at[k], z_at[z]), :]
        a2[0], a2[1] = split(moved[...].T)

    def products(blocks):
        for g in range(group):
            cut = pl.ds(g * columns, columns)
            b = [block[..., cut].reshape(-1, columns) for block in blocks]
            b = split(b[0] if len(b) == 1 else jnp.concatenate(b, axis=0))
            r = split(dot3((a2[0], a2[1]), b))
            at = pl.multiple_of((step * group + g) * RANK, RANK)
            for part in range(2):
                for i in range(i_rows):
                    r2[part, i, pl.ds(at, RANK), :] = r[part][i * RANK:(i + 1) * RANK]

    @pl.when(step < steps // 2)
    def _():
        products((sa,))

    @pl.when((step >= steps // 2) & (step < steps))
    def _():
        products((s0, s1, s2, s3, s4))

    @pl.when(step >= steps)
    def _():
        for k in range(pair.shape[0]):
            i = (step - steps) * pair.shape[0] + k
            both = dot(w2[...], r2[0, i])
            value = both[:LANES] + (both[LANES:] + dot(w2[:LANES], r2[1, i])) + out_bias[...]
            count = jnp.maximum(mask_s[place[0] * i_rows + i].astype(F32) * count_c[0], 1.0)
            out[k] = pair[k] + (value / count).T
        for k, piece in enumerate((t0, t1, t2, t3)):
            @pl.when((step - steps) // 2 == k)
            def _(piece=piece):
                state[...] = piece[...]


def outer_mean(place, mask, first, second, weight_t, out_bias, count, pair, state):
    rows, columns, channels = pair.shape
    members = sum(piece.shape[0] * piece.shape[1] for piece in first)
    wide = rows * RANK
    group = 8
    steps = RANK // group
    half = steps // 2
    part = 2
    count_s, quarter, features = state[0].shape
    lines = count_s // 2
    whole_state = (count_s, quarter * len(state), features)

    def state_block(t, place, *_):
        at = jnp.clip(t - steps, 0, 2 * len(state) - 1)
        return (lax.rem(at, 2), place[1] ^ (at // 2), 0)

    def own(t, *_):
        return (jnp.maximum(t - steps, 0), 0, 0)

    def whole(shape):
        return pl.BlockSpec(shape, lambda t, *_: (0,) * len(shape))

    def columns_block(piece, low):
        lead = piece.shape[:-1]
        return pl.BlockSpec(
            lead + (group * columns,),
            lambda t, *_: (0,) * len(lead) + (jnp.clip(t - low, 0, half - 1),),
        )

    return pl.pallas_call(
        partial(outer_kernel, group),
        out_shape=[
            jax.ShapeDtypeStruct(pair.shape, F32),
            jax.ShapeDtypeStruct(whole_state, F32),
        ],
        grid_spec=pltpu.PrefetchScalarGridSpec(
            num_scalar_prefetch=2,
            grid=(steps + rows // part,),
            in_specs=[whole(piece.shape) for piece in first]
            + [columns_block(second[0], 0)]
            + [columns_block(piece, half) for piece in second[1]]
            + [
                whole((channels, RANK * RANK)),
                whole((channels, 1)),
                pl.BlockSpec((1, 1, columns), lambda t, place, *_: (place[1], 0, 0)),
                pl.BlockSpec((part, columns, channels), own),
            ] + [
                pl.BlockSpec((lines, quarter, features),
                             lambda t, *_, k=k: (jnp.clip(t - steps - 2 * k, 0, 1), 0, 0))
                for k in range(len(state))
            ],
            out_specs=[pl.BlockSpec((part, columns, channels), own),
                       pl.BlockSpec((lines, quarter, features), state_block)],
            scratch_shapes=[
                pltpu.VMEM((members, wide), F32),
                pltpu.VMEM((members, wide), F32),
                pltpu.VMEM((2, wide, members), BF16),
                pltpu.VMEM((2 * channels, RANK * RANK), BF16),
                pltpu.VMEM((2, rows, RANK * RANK, columns), BF16),
            ],
        ),
        compiler_params=params(1, 52),
        name="outer_mean",
    )(place, mask, *first, second[0], *second[1], weight_t, out_bias[:, None],
      count.reshape(-1, 1, columns), pair, *state)


Y_STEPS = (0, 3, 1, 2)
Z_STEPS = (0, 7, 1, 6, 2, 5, 3, 4)


def shift(block, axis, size, step):
    return lax.ppermute(block, axis, [(i, (i + step) % size) for i in range(size)])


def gather_both(block_a, block_b, ny, nz, early=()):
    along = [shift(block_a, "y", ny, -k) for k in Y_STEPS[1:]]
    one = [shift(block_b, "z", nz, k) for k in (1, -1)]
    two = [shift(block_b, "z", nz, k) for k in (2, -2)]
    along, early = lax.optimization_barrier((along, early))
    gathered_a = lax.all_gather(jnp.stack([block_a] + along), "z")
    three = [shift(one[0], "z", nz, 2), shift(one[1], "z", nz, -2)]
    cut = block_b.shape[0] // 2
    four = [shift(two[0][:cut], "z", nz, 2), shift(two[1][cut:], "z", nz, -2)]
    gathered_b = jnp.stack([block_b] + one + two + three + [jnp.concatenate(four)])
    return gathered_a, gathered_b, early


def gather_y(block, ny, beside=()):
    one = [shift(block, "y", ny, k) for k in (1, -1)]
    one, beside = lax.optimization_barrier((one, beside))
    cut = block.shape[0] // 2
    two = [shift(one[0][:cut], "y", ny, 1), shift(one[1][cut:], "y", ny, -1)]
    return [block] + one + two, beside


def in_order(mine, other):
    low = lax.axis_index("xl") == 0
    return jnp.stack([jnp.where(low, mine, other), jnp.where(low, other, mine)])


def per_device(
    sizes,
    lineup_embedding,
    pairwise_state,
    lineup_scaling_coefficients,
    focus_projection_matrix,
    attention_gate_bias,
    focus_merge_matrix,
    pairwise_bias_weight,
    relative_bias_table,
    tensor_operand_matrices,
    outer_output_weight,
    outer_output_bias,
    lineup_member_flags,
    residue_presence_mask,
    chain_label,
    residue_numbering,
):
    ny, nz, nxl, nxh, nc = (sizes[a] for a in ("y", "z", "xl", "xh", "c"))
    nq = nxh * nc
    dap = (lax.axis_index("y") * nz + lax.axis_index("z")) * nxl + lax.axis_index("xl")
    head = lax.axis_index("xh") * nc + lax.axis_index("c")
    place = jnp.stack([dap, head, lax.axis_index("y"), lax.axis_index("z")]).astype(jnp.int32)
    count, positions, channels = lineup_embedding.shape
    block_rows, quarter, pair_channels = pairwise_state.shape
    presence = residue_presence_mask.astype(F32)

    packed = pack(focus_projection_matrix, focus_merge_matrix, attention_gate_bias)
    packed, pairwise_state = lax.optimization_barrier((packed, pairwise_state))
    packed = lax.all_gather(packed, HEAD_AXES)

    local = pair_bias(place, residue_numbering, chain_label, residue_presence_mask, pairwise_state,
                      pairwise_bias_weight, relative_bias_table)

    def swap(flip):
        perm = []
        for y in range(ny):
            for x in range(nxl):
                for q in range(nq):
                    perm.append(((y * nxl + x) * nq + q, (q * nxl + (x ^ flip)) * nq + y))
        return lax.ppermute(local, ("y", "xl") + HEAD_AXES, perm)

    bias = in_order(swap(0), swap(1))
    bias_a, bias_b, packed = gather_both(bias[:, :HEADS_A], bias[:, HEADS_A:], ny, nz, packed)
    bias_b, rows = lax.optimization_barrier((bias_b, lineup_embedding))
    projected = project(place, rows, lineup_scaling_coefficients, packed, quarter)
    bias_b, (kp, vp, qp, gp) = gather_y(bias_b, ny, projected)
    bias = (bias_a, bias_b)
    operand_t = jnp.swapaxes(tensor_operand_matrices, 1, 2).reshape(2 * RANK, channels)
    state, first, second = attend(place, lineup_member_flags, bias, kp, vp, qp, gp, packed,
                                  lineup_embedding, operand_t, presence, quarter)

    second = in_order(second, shift(second, "xl", nxl, 1)).reshape(nxl * count, -1)
    half = second.shape[1] // 2
    second_a, second_b, _ = gather_both(second[:, :half], second[:, half:], ny, nz)
    second_b, first, state = lax.optimization_barrier((second_b, first, state))

    parts = nz * nxl
    first = jnp.transpose(first.reshape(count, RANK, parts, block_rows), (2, 0, 3, 1))
    first = lax.all_to_all(first.reshape(parts, count, block_rows * RANK), ("z", "xl"), 0, 0, tiled=True)
    across = shift(state, "xh", nxh, 1)
    first, across = lax.optimization_barrier((first.reshape(parts * count, -1), across))
    first = [
        lax.ppermute(first, ("y",) + HEAD_AXES,
                     [(y * nq + q, q * nq + (y + r) % nq) for y in range(ny) for q in range(nq)])
        for r in (0, 2)
    ]

    pieces = [state, shift(state, "c", nc, 1), across, shift(across, "c", nc, 1)]
    second_b, _ = gather_y(second_b, ny)
    second = (second_a, second_b)
    first = jnp.stack(first)
    first = [first, shift(first, "c", nc, 1)]

    weight_t = jnp.transpose(
        outer_output_weight.reshape(RANK, RANK, pair_channels), (2, 1, 0)
    ).reshape(pair_channels, RANK * RANK)
    count_columns = presence * jnp.sum(lineup_member_flags.astype(F32))
    pairs, state = outer_mean(place, residue_presence_mask, first, second, weight_t,
                              outer_output_bias, count_columns, pairwise_state, pieces)
    return state, pairs


def solution(mesh):
    sizes = dict(y=4, z=8, xl=2, xh=2, c=2)
    fine = Mesh(mesh.devices.reshape(tuple(sizes.values())), tuple(sizes))
    placed = (
        P(DAP_AXES, None, None),
        P(DAP_AXES, HEAD_AXES, None),
        P(),
        P(None, None, HEAD_AXES),
        P(HEAD_AXES),
        P(HEAD_AXES, None),
    ) + (P(),) * 9
    return jax.shard_map(
        partial(per_device, sizes),
        mesh=fine,
        in_specs=placed,
        out_specs=(P(DAP_AXES, None, None), P(DAP_AXES, HEAD_AXES, None)),
        check_vma=False,
    )
```

```python
import math
from functools import partial

import jax
import jax.numpy as jnp
from jax import lax
from jax.experimental import pallas as pl
from jax.experimental.pallas import tpu as pltpu
from jax.sharding import Mesh, PartitionSpec as P

F32, BF16 = jnp.float32, jnp.bfloat16
HEADS, DEPTH, RANK, BUCKETS = 8, 32, 32, 66
HEADS_A = 4
TABLE_ROWS = 72
LANES = 128
LOG2E = math.log2(math.e)
HEAD_AXES = ("xh", "c")
DAP_AXES = ("y", "z", "xl")


def dot(a, b, contract=((1,), (0,))):
    return lax.dot_general(a, b, (contract, ((), ())), preferred_element_type=F32)


def split(a):
    high = a.astype(BF16)
    return high, (a - high.astype(F32)).astype(BF16)


def dot3(a, b, contract=((1,), (0,))):
    return dot(a[0], b[0], contract) + (dot(a[0], b[1], contract) + dot(a[1], b[0], contract))


def normalize(values):
    center = values - jnp.mean(values, axis=-1, keepdims=True)
    spread = jnp.mean(center * center, axis=-1, keepdims=True)
    return center * lax.rsqrt(spread + 1e-05)


def params(n_axes, mib):
    return pltpu.CompilerParams(
        dimension_semantics=("arbitrary",) * n_axes, vmem_limit_bytes=mib * 2**20
    )


def bias_kernel(place, index_s, chain_s, pair, weight_t, table_t, index_c, chain_c, mask_c, out):
    step = pl.program_id(0)
    rows = pair.shape[0]
    columns = pair.shape[1]
    w = weight_t[...]
    table = table_t[...]
    lines = columns // LANES

    def own_columns(ref):
        return jnp.concatenate([ref[pl.ds(place[1] * lines + k, 1), :] for k in range(lines)], axis=1)

    cols_index = own_columns(index_c)
    cols_chain = own_columns(chain_c)
    mask = (own_columns(mask_c).astype(F32) - 1.0) * 1000000000.0
    reach = (BUCKETS - 2) // 2
    for r in range(rows):
        i = place[0] * (rows * pl.num_programs(0)) + step * rows + r
        normed = normalize(pair[r])
        linear = lax.dot_general(
            w, normed, (((1,), (1,)), ((), ())), precision=lax.Precision.HIGHEST,
            preferred_element_type=F32,
        )
        offset = jnp.clip(index_s[i] - cols_index, -reach, reach) + reach
        bucket = jnp.where(chain_s[i] == cols_chain, offset, BUCKETS - 1)
        classes = lax.broadcasted_iota(jnp.int32, (TABLE_ROWS, columns), 0)
        onehot = (classes == bucket).astype(F32)
        relative = lax.dot_general(
            table, onehot, (((1,), (0,)), ((), ())), precision=lax.Precision.HIGHEST,
            preferred_element_type=F32,
        )
        out[:, r, :] = (linear + relative + mask) * LOG2E


def pair_bias(place, numbering, chain, presence, pair, weight, table):
    rows, columns, channels = pair.shape
    part = 8

    def whole(shape):
        return pl.BlockSpec(shape, lambda r, *_: (0,) * len(shape))

    lines = numbering.shape[0] // LANES
    return pl.pallas_call(
        bias_kernel,
        out_shape=jax.ShapeDtypeStruct((HEADS, rows, columns), F32),
        grid_spec=pltpu.PrefetchScalarGridSpec(
            num_scalar_prefetch=3,
            grid=(rows // part,),
            in_specs=[
                pl.BlockSpec((part, columns, channels), lambda r, *_: (r, 0, 0)),
                whole((HEADS, channels)),
                whole((HEADS, TABLE_ROWS)),
            ] + [whole((lines, LANES))] * 3,
            out_specs=pl.BlockSpec((HEADS, part, columns), lambda r, *_: (0, r, 0)),
        ),
        compiler_params=params(1, 32),
        name="pair_bias",
    )(
        place, numbering, chain, pair, weight.T,
        jnp.pad(table, ((0, TABLE_ROWS - BUCKETS), (0, 0))).T,
        numbering.reshape(lines, LANES), chain.reshape(lines, LANES), presence.reshape(lines, LANES),
    )


def pack_kernel(w, merge, gate_bias, out):
    rows = w.shape[0] * w.shape[1]
    for t in range(w.shape[0]):
        out[pl.ds(t * w.shape[1], w.shape[1]), :] = w[t]
    out[pl.ds(rows, merge.shape[0]), :] = merge[...]
    copies = out.shape[1] // gate_bias.shape[1]
    gate = jnp.concatenate([gate_bias[...]] * copies, axis=1)
    out[pl.ds(out.shape[0] - 8, 8), :] = jnp.broadcast_to(gate, (8, out.shape[1]))


def pack(w, merge, gate_bias):
    w = jnp.swapaxes(w, 1, 2)
    rows = w.shape[0] * w.shape[1] + merge.shape[0] + 8
    return pl.pallas_call(
        pack_kernel, out_shape=jax.ShapeDtypeStruct((rows, merge.shape[1]), F32), name="pack"
    )(w, merge, gate_bias[None])


def project_kernel(place, row, own, gain, packed, kp, vp, qp, gp, wk2, wv2, wq2, wg2, gate_bias):
    channels = row.shape[2]

    @pl.when(pl.program_id(0) == 0)
    def _():
        narrow = HEADS * DEPTH // packed.shape[0]
        for q in range(packed.shape[0]):
            at = pl.ds(q * narrow, narrow)
            wk2[0, at], wk2[1, at] = split(packed[q, pl.ds(narrow, narrow), :])
        for h in range(HEADS):
            q, start = h // 2, h % 2 * DEPTH
            at = pl.ds(h * LANES, LANES)
            for t, copies, target in ((0, 4, wq2), (2, 2, wv2), (3, 2, wg2)):
                part = packed[q, pl.ds(t * narrow + start, DEPTH), :]
                rest = [jnp.zeros((LANES - copies * DEPTH, channels), F32)] if copies * DEPTH < LANES else []
                parts = [part] * copies + rest if h % 2 == 0 else rest + [part] * copies
                target[0, at], target[1, at] = split(jnp.concatenate(parts, axis=0))
            gate = packed[q, pl.ds(packed.shape[1] - 8, 8), :][:1, start:start + DEPTH]
            rest = jnp.zeros((1, LANES - 2 * DEPTH), F32)
            gate_bias[:, at] = jnp.concatenate([gate, gate, rest] if h % 2 == 0 else [rest, gate, gate], axis=1)

    positions = row.shape[1]
    own_positions = own.shape[1]
    n = split(normalize(row[0]) * gain[...])
    keys = split(dot3((wk2[0], wk2[1]), n, ((1,), (1,))))
    for h in range(HEADS):
        for part in range(4):
            kp[0, h, pl.ds(part * DEPTH, DEPTH), :] = keys[part % 2][h * DEPTH:(h + 1) * DEPTH]
    pair_lanes = 2 * LANES
    lane = lax.broadcasted_iota(jnp.int32, (positions, LANES), 1)
    for h in range(0, HEADS, 2):
        cut = pl.ds(h * LANES, pair_lanes)
        both = dot3(n, (wv2[0, cut], wv2[1, cut]), ((1,), (1,)))
        for k in range(2):
            value = both[:, k * LANES:(k + 1) * LANES]
            high = value.astype(BF16).astype(F32)
            at = lane - k * (LANES // 2)
            packed = jnp.where((at >= 0) & (at < DEPTH), high,
                               jnp.where((at >= DEPTH) & (at < 2 * DEPTH), value - high, 1.0))
            vp[0, h + k] = packed.astype(BF16)
    m = split(normalize(own[0]) * gain[...])
    lane = lax.broadcasted_iota(jnp.int32, (own_positions, LANES), 1)
    for h in range(0, HEADS, 2):
        cut = pl.ds(h * LANES, pair_lanes)
        both = dot3(m, (wq2[0, cut], wq2[1, cut]), ((1,), (1,))) * (LOG2E / math.sqrt(DEPTH))
        gates = dot3(m, (wg2[0, cut], wg2[1, cut]), ((1,), (1,))) + gate_bias[:, cut]
        gates = jax.nn.sigmoid(gates)
        for k in range(2):
            value = both[:, k * LANES:(k + 1) * LANES]
            high = value.astype(BF16).astype(F32)
            qp[0, h + k] = jnp.where(lane < 2 * DEPTH, high, value - high).astype(BF16)
            gp[0, h + k] = gates[:, k * LANES:(k + 1) * LANES]


def project(place, rows, gain, packed, quarter):
    count, positions, channels = rows.shape
    wide = HEADS * LANES

    def whole(shape):
        return pl.BlockSpec(shape, lambda s, place: (0,) * len(shape))

    def out(rows_, columns, dtype):
        return (
            jax.ShapeDtypeStruct((count, HEADS, rows_, columns), dtype),
            pl.BlockSpec((1, HEADS, rows_, columns), lambda s, place: (s, 0, 0, 0)),
        )

    outs = [out(LANES, positions, BF16), out(positions, LANES, BF16),
            out(quarter, LANES, BF16), out(quarter, LANES, F32)]
    return pl.pallas_call(
        project_kernel,
        out_shape=[o[0] for o in outs],
        grid_spec=pltpu.PrefetchScalarGridSpec(
            num_scalar_prefetch=1,
            grid=(count,),
            in_specs=[
                pl.BlockSpec((1, positions, channels), lambda s, place: (s, 0, 0)),
                pl.BlockSpec((1, quarter, channels), lambda s, place: (s, place[1], 0)),
                whole((1, channels)), whole(packed.shape),
            ],
            out_specs=[o[1] for o in outs],
            scratch_shapes=[pltpu.VMEM((2, HEADS * DEPTH, channels), BF16)]
            + [pltpu.VMEM((2, wide, channels), BF16)] * 3 + [pltpu.VMEM((1, wide), F32)],
        ),
        compiler_params=params(1, 52),
        name="project",
    )(place, rows, rows, gain[None], packed)


def attend_kernel(place, flags_s, bias_a, b0, b1, b2, b3, b4, kp, vp, qp, gp, merge, own, operand_t,
                  mask_c, state_out, first_out, second_out, gated, head_bias, merge_rows):
    h = pl.program_id(0)
    count = own.shape[0]
    quarter = own.shape[1]
    nz, ny, width = bias_a.shape[0], bias_a.shape[1], bias_a.shape[5]
    group = quarter // nz

    def columns(k):
        return pl.ds(pl.multiple_of(lax.rem(place[2] + Y_STEPS[k], ny) * width, width), width)

    def rows(k):
        return pl.ds(pl.multiple_of(lax.rem(place[3] + Z_STEPS[k], nz) * group, group), group)

    @pl.when(h == 0)
    def _():
        gated[...] = jnp.zeros_like(gated)

    @pl.when(h < HEADS_A)
    def _():
        for k in range(ny):
            head_bias[:, columns(k)] = bias_a[:, k, :, 0].reshape(quarter, width)

    @pl.when(h >= HEADS_A)
    def _():
        for y, pieces in enumerate(((b0,), (b1,), (b2,), (b3, b4))):
            k = 0
            for piece in pieces:
                for line in range(piece.shape[0]):
                    head_bias[rows(k), columns(y)] = piece[line, :, 0].reshape(group, width)
                    k += 1

    half = LANES // 2
    lane = lax.broadcasted_iota(jnp.int32, (quarter, LANES), 1)
    own_lanes = lane // half == lax.rem(h, 2)
    at = pl.ds(pl.multiple_of(h // 2 * LANES, LANES), LANES)
    ahead = dot(qp[0, 0], kp[0, 0]) + head_bias[...]
    for s in range(count):
        logits = ahead
        if s + 1 < count:
            ahead = dot(qp[s + 1, 0], kp[s + 1, 0]) + head_bias[...]
        peak = jnp.max(logits, axis=1, keepdims=True)
        weights = jnp.exp2(logits - peak)
        mixed = dot(jnp.concatenate(split(weights), axis=0), vp[s, 0])
        mixed = mixed[:quarter] + mixed[quarter:]
        total_weight = jnp.where(own_lanes, pltpu.roll(mixed, half, 1), 1.0)
        parts = split(jnp.where(own_lanes, mixed * gp[s, 0] / total_weight, 0.0))
        gated[0, s, :, at] += parts[0]
        gated[1, s, :, at] += parts[1]

    @pl.when(h == pl.num_programs(0) - 1)
    def _():
        ops = split(operand_t[...])
        for k in range(HEADS):
            rows_k = merge[k // 2, pl.ds(k % 2 * DEPTH, DEPTH), :]
            for copy in range(2):
                merge_rows[pl.ds((2 * k + copy) * DEPTH, DEPTH), :] = rows_k
        m2 = split(merge_rows[...])
        for s in range(count):
            state = own[s] + dot3((gated[0, s], gated[1, s]), m2)
            state_out[s] = state
            n = split(normalize(state))
            flag = flags_s[place[0] * count + s].astype(F32)
            factors = dot3(ops, n, ((1,), (1,))) * (mask_c[0] * flag)
            first_out[s] = factors[:RANK]
            for e in range(RANK):
                second_out[pl.ds(s, 1), pl.ds(e * quarter, quarter)] = factors[RANK + e:RANK + e + 1]


def attend(place, flags, bias, kp, vp, qp, gp, merge, rows, operand_t, mask, quarter):
    count, positions, channels = rows.shape

    merge_size = HEADS * DEPTH // merge.shape[0]

    def piece_block(piece, low, high):
        shape = list(piece.shape)
        shape[-3] = 1

        def at(h, *_):
            index = [0] * len(shape)
            index[-3] = jnp.clip(h - low, 0, high)
            return tuple(index)

        return pl.BlockSpec(tuple(shape), at)

    def head_block(rows_, columns):
        return pl.BlockSpec((count, 1, rows_, columns), lambda h, *_: (0, h, 0, 0))

    return pl.pallas_call(
        attend_kernel,
        out_shape=[
            jax.ShapeDtypeStruct((count, quarter, channels), F32),
            jax.ShapeDtypeStruct((count, RANK, quarter), F32),
            jax.ShapeDtypeStruct((count, RANK * quarter), F32),
        ],
        grid_spec=pltpu.PrefetchScalarGridSpec(
            num_scalar_prefetch=2,
            grid=(HEADS,),
            in_specs=[
                piece_block(bias[0], 0, HEADS_A - 1),
            ] + [piece_block(piece, HEADS_A, HEADS - HEADS_A - 1) for piece in bias[1]] + [
                head_block(LANES, positions), head_block(positions, LANES),
                head_block(quarter, LANES), head_block(quarter, LANES),
                pl.BlockSpec((merge.shape[0], merge_size, channels), lambda h, *_: (0, 4, 0)),
                pl.BlockSpec((count, quarter, channels), lambda h, place, *_: (0, place[1], 0)),
                pl.BlockSpec((2 * RANK, channels), lambda h, *_: (0, 0)),
                pl.BlockSpec((1, 1, quarter), lambda h, place, *_: (place[1], 0, 0)),
            ],
            out_specs=[
                pl.BlockSpec((count, quarter, channels), lambda h, *_: (0, 0, 0)),
                pl.BlockSpec((count, RANK, quarter), lambda h, *_: (0, 0, 0)),
                pl.BlockSpec((count, RANK * quarter), lambda h, *_: (0, 0)),
            ],
            scratch_shapes=[
                pltpu.VMEM((2, count, quarter, 2 * HEADS * DEPTH), BF16),
                pltpu.VMEM((quarter, positions), F32),
                pltpu.VMEM((2 * HEADS * DEPTH, channels), F32),
            ],
        ),
        compiler_params=params(1, 52),
        name="attend",
    )(place, flags, bias[0], *bias[1], kp, vp, qp, gp, merge, rows, operand_t, mask.reshape(-1, 1, quarter))


def outer_kernel(group, place, mask_s, f0, f1, sa, s0, s1, s2, s3, s4, weight_t, out_bias,
                 count_c, pair, t0, t1, t2, t3, out, state, ordered, moved, a2, w2, r2):
    step = pl.program_id(0)
    steps = RANK // group
    i_rows = r2.shape[1]
    columns = pair.shape[1]
    nz, ny, eight = sa.shape[0], sa.shape[1], sa.shape[2]
    y_at = [lax.rem(place[2] + k, ny) for k in Y_STEPS]
    z_at = [lax.rem(place[3] + k, nz) for k in Z_STEPS]

    def row(y, z):
        return pl.ds(pl.multiple_of((y * nz + z) * eight, eight), eight)

    @pl.when(step == 0)
    def _():
        high, low = split(weight_t[...])
        w2[:LANES], w2[LANES:] = high, low
        for r, piece in enumerate((f0, f1)):
            size = piece.shape[1]
            for k in range(piece.shape[0]):
                y = lax.rem((place[1] ^ r) + 2 * k, ny)
                ordered[pl.ds(pl.multiple_of(y * size, size), size), :] = piece[k]
        for z in range(nz):
            for k in range(ny):
                moved[pl.ds((z * ny + k) * eight, eight), :] = ordered[row(y_at[k], z), :]
        a2[0], a2[1] = split(moved[...].T)

    @pl.when(step == steps // 2)
    def _():
        for k in range(ny):
            for z in range(nz):
                moved[pl.ds((k * nz + z) * eight, eight), :] = ordered[row(y_at[k], z_at[z]), :]
        a2[0], a2[1] = split(moved[...].T)

    def products(blocks):
        for g in range(group):
            cut = pl.ds(g * columns, columns)
            b = [block[..., cut].reshape(-1, columns) for block in blocks]
            b = split(b[0] if len(b) == 1 else jnp.concatenate(b, axis=0))
            r = split(dot3((a2[0], a2[1]), b))
            at = pl.multiple_of((step * group + g) * RANK, RANK)
            for part in range(2):
                for i in range(i_rows):
                    r2[part, i, pl.ds(at, RANK), :] = r[part][i * RANK:(i + 1) * RANK]

    @pl.when(step < steps // 2)
    def _():
        products((sa,))

    @pl.when((step >= steps // 2) & (step < steps))
    def _():
        products((s0, s1, s2, s3, s4))

    @pl.when(step >= steps)
    def _():
        for k in range(pair.shape[0]):
            i = (step - steps) * pair.shape[0] + k
            both = dot(w2[...], r2[0, i])
            value = both[:LANES] + (both[LANES:] + dot(w2[:LANES], r2[1, i])) + out_bias[...]
            count = jnp.maximum(mask_s[place[0] * i_rows + i].astype(F32) * count_c[0], 1.0)
            out[k] = pair[k] + (value * (1.0 / count)).T
        for k, piece in enumerate((t0, t1, t2, t3)):
            @pl.when((step - steps) // 2 == k)
            def _(piece=piece):
                state[...] = piece[...]


def outer_mean(place, mask, first, second, weight_t, out_bias, count, pair, state):
    rows, columns, channels = pair.shape
    members = sum(piece.shape[0] * piece.shape[1] for piece in first)
    wide = rows * RANK
    group = 8
    steps = RANK // group
    half = steps // 2
    part = 2
    count_s, quarter, features = state[0].shape
    lines = count_s // 2
    whole_state = (count_s, quarter * len(state), features)

    def state_block(t, place, *_):
        at = jnp.clip(t - steps, 0, 2 * len(state) - 1)
        return (lax.rem(at, 2), place[1] ^ (at // 2), 0)

    def own(t, *_):
        return (jnp.maximum(t - steps, 0), 0, 0)

    def whole(shape):
        return pl.BlockSpec(shape, lambda t, *_: (0,) * len(shape))

    def columns_block(piece, low):
        lead = piece.shape[:-1]
        return pl.BlockSpec(
            lead + (group * columns,),
            lambda t, *_: (0,) * len(lead) + (jnp.clip(t - low, 0, half - 1),),
        )

    return pl.pallas_call(
        partial(outer_kernel, group),
        out_shape=[
            jax.ShapeDtypeStruct(pair.shape, F32),
            jax.ShapeDtypeStruct(whole_state, F32),
        ],
        grid_spec=pltpu.PrefetchScalarGridSpec(
            num_scalar_prefetch=2,
            grid=(steps + rows // part,),
            in_specs=[whole(piece.shape) for piece in first]
            + [columns_block(second[0], 0)]
            + [columns_block(piece, half) for piece in second[1]]
            + [
                whole((channels, RANK * RANK)),
                whole((channels, 1)),
                pl.BlockSpec((1, 1, columns), lambda t, place, *_: (place[1], 0, 0)),
                pl.BlockSpec((part, columns, channels), own),
            ] + [
                pl.BlockSpec((lines, quarter, features),
                             lambda t, *_, k=k: (jnp.clip(t - steps - 2 * k, 0, 1), 0, 0))
                for k in range(len(state))
            ],
            out_specs=[pl.BlockSpec((part, columns, channels), own),
                       pl.BlockSpec((lines, quarter, features), state_block)],
            scratch_shapes=[
                pltpu.VMEM((members, wide), F32),
                pltpu.VMEM((members, wide), F32),
                pltpu.VMEM((2, wide, members), BF16),
                pltpu.VMEM((2 * channels, RANK * RANK), BF16),
                pltpu.VMEM((2, rows, RANK * RANK, columns), BF16),
            ],
        ),
        compiler_params=params(1, 52),
        name="outer_mean",
    )(place, mask, *first, second[0], *second[1], weight_t, out_bias[:, None],
      count.reshape(-1, 1, columns), pair, *state)


Y_STEPS = (0, 3, 1, 2)
Z_STEPS = (0, 7, 1, 6, 2, 5, 3, 4)


def shift(block, axis, size, step):
    return lax.ppermute(block, axis, [(i, (i + step) % size) for i in range(size)])


def gather_both(block_a, block_b, ny, nz, early=()):
    along = [shift(block_a, "y", ny, -k) for k in Y_STEPS[1:]]
    one = [shift(block_b, "z", nz, k) for k in (1, -1)]
    two = [shift(block_b, "z", nz, k) for k in (2, -2)]
    along, early = lax.optimization_barrier((along, early))
    gathered_a = lax.all_gather(jnp.stack([block_a] + along), "z")
    three = [shift(one[0], "z", nz, 2), shift(one[1], "z", nz, -2)]
    cut = block_b.shape[0] // 2
    four = [shift(two[0][:cut], "z", nz, 2), shift(two[1][cut:], "z", nz, -2)]
    gathered_b = jnp.stack([block_b] + one + two + three + [jnp.concatenate(four)])
    return gathered_a, gathered_b, early


def gather_y(block, ny, beside=()):
    one = [shift(block, "y", ny, k) for k in (1, -1)]
    one, beside = lax.optimization_barrier((one, beside))
    cut = block.shape[0] // 2
    two = [shift(one[0][:cut], "y", ny, 1), shift(one[1][cut:], "y", ny, -1)]
    return [block] + one + two, beside


def in_order(mine, other):
    low = lax.axis_index("xl") == 0
    return jnp.stack([jnp.where(low, mine, other), jnp.where(low, other, mine)])


def per_device(
    sizes,
    lineup_embedding,
    pairwise_state,
    lineup_scaling_coefficients,
    focus_projection_matrix,
    attention_gate_bias,
    focus_merge_matrix,
    pairwise_bias_weight,
    relative_bias_table,
    tensor_operand_matrices,
    outer_output_weight,
    outer_output_bias,
    lineup_member_flags,
    residue_presence_mask,
    chain_label,
    residue_numbering,
):
    ny, nz, nxl, nxh, nc = (sizes[a] for a in ("y", "z", "xl", "xh", "c"))
    nq = nxh * nc
    dap = (lax.axis_index("y") * nz + lax.axis_index("z")) * nxl + lax.axis_index("xl")
    head = lax.axis_index("xh") * nc + lax.axis_index("c")
    place = jnp.stack([dap, head, lax.axis_index("y"), lax.axis_index("z")]).astype(jnp.int32)
    count, positions, channels = lineup_embedding.shape
    block_rows, quarter, pair_channels = pairwise_state.shape
    presence = residue_presence_mask.astype(F32)

    packed = pack(focus_projection_matrix, focus_merge_matrix, attention_gate_bias)
    packed, pairwise_state = lax.optimization_barrier((packed, pairwise_state))
    packed = lax.all_gather(packed, HEAD_AXES)

    local = pair_bias(place, residue_numbering, chain_label, residue_presence_mask, pairwise_state,
                      pairwise_bias_weight, relative_bias_table)

    def swap(flip):
        perm = []
        for y in range(ny):
            for x in range(nxl):
                for q in range(nq):
                    perm.append(((y * nxl + x) * nq + q, (q * nxl + (x ^ flip)) * nq + y))
        return lax.ppermute(local, ("y", "xl") + HEAD_AXES, perm)

    bias = in_order(swap(0), swap(1))
    bias_a, bias_b, packed = gather_both(bias[:, :HEADS_A], bias[:, HEADS_A:], ny, nz, packed)
    bias_b, rows = lax.optimization_barrier((bias_b, lineup_embedding))
    projected = project(place, rows, lineup_scaling_coefficients, packed, quarter)
    bias_b, (kp, vp, qp, gp) = gather_y(bias_b, ny, projected)
    bias = (bias_a, bias_b)
    operand_t = jnp.swapaxes(tensor_operand_matrices, 1, 2).reshape(2 * RANK, channels)
    state, first, second = attend(place, lineup_member_flags, bias, kp, vp, qp, gp, packed,
                                  lineup_embedding, operand_t, presence, quarter)

    second = in_order(second, shift(second, "xl", nxl, 1)).reshape(nxl * count, -1)
    half = second.shape[1] // 2
    second_a, second_b, _ = gather_both(second[:, :half], second[:, half:], ny, nz)
    second_b, first, state = lax.optimization_barrier((second_b, first, state))

    parts = nz * nxl
    first = jnp.transpose(first.reshape(count, RANK, parts, block_rows), (2, 0, 3, 1))
    first = lax.all_to_all(first.reshape(parts, count, block_rows * RANK), ("z", "xl"), 0, 0, tiled=True)
    across = shift(state, "xh", nxh, 1)
    first, across = lax.optimization_barrier((first.reshape(parts * count, -1), across))
    first = [
        lax.ppermute(first, ("y",) + HEAD_AXES,
                     [(y * nq + q, q * nq + (y + r) % nq) for y in range(ny) for q in range(nq)])
        for r in (0, 2)
    ]

    pieces = [state, shift(state, "c", nc, 1), across, shift(across, "c", nc, 1)]
    second_b, _ = gather_y(second_b, ny)
    second = (second_a, second_b)
    first = jnp.stack(first)
    first = [first, shift(first, "c", nc, 1)]

    weight_t = jnp.transpose(
        outer_output_weight.reshape(RANK, RANK, pair_channels), (2, 1, 0)
    ).reshape(pair_channels, RANK * RANK)
    count_columns = presence * jnp.sum(lineup_member_flags.astype(F32))
    pairs, state = outer_mean(place, residue_presence_mask, first, second, weight_t,
                              outer_output_bias, count_columns, pairwise_state, pieces)
    return state, pairs


def solution(mesh):
    sizes = dict(y=4, z=8, xl=2, xh=2, c=2)
    fine = Mesh(mesh.devices.reshape(tuple(sizes.values())), tuple(sizes))
    placed = (
        P(DAP_AXES, None, None),
        P(DAP_AXES, HEAD_AXES, None),
        P(),
        P(None, None, HEAD_AXES),
        P(HEAD_AXES),
        P(HEAD_AXES, None),
    ) + (P(),) * 9
    return jax.shard_map(
        partial(per_device, sizes),
        mesh=fine,
        in_specs=placed,
        out_specs=(P(DAP_AXES, None, None), P(DAP_AXES, HEAD_AXES, None)),
        check_vma=False,
    )
```

```python
import math
from functools import partial

import jax
import jax.numpy as jnp
from jax import lax
from jax.experimental import pallas as pl
from jax.experimental.pallas import tpu as pltpu
from jax.sharding import Mesh, PartitionSpec as P

F32, BF16 = jnp.float32, jnp.bfloat16
HEADS, DEPTH, RANK, BUCKETS = 8, 32, 32, 66
HEADS_A = 4
TABLE_ROWS = 72
LANES = 128
LOG2E = math.log2(math.e)
HEAD_AXES = ("xh", "c")
DAP_AXES = ("y", "z", "xl")


def dot(a, b, contract=((1,), (0,))):
    return lax.dot_general(a, b, (contract, ((), ())), preferred_element_type=F32)


def split(a):
    high = a.astype(BF16)
    return high, (a - high.astype(F32)).astype(BF16)


def dot3(a, b, contract=((1,), (0,))):
    return dot(a[0], b[0], contract) + (dot(a[0], b[1], contract) + dot(a[1], b[0], contract))


def normalize(values):
    center = values - jnp.mean(values, axis=-1, keepdims=True)
    spread = jnp.mean(center * center, axis=-1, keepdims=True)
    return center * lax.rsqrt(spread + 1e-05)


def params(n_axes, mib):
    return pltpu.CompilerParams(
        dimension_semantics=("arbitrary",) * n_axes, vmem_limit_bytes=mib * 2**20
    )


def bias_kernel(place, index_s, chain_s, pair, weight_t, table_t, index_c, chain_c, mask_c, out):
    step = pl.program_id(0)
    rows = pair.shape[0]
    columns = pair.shape[1]
    w = weight_t[...]
    table = table_t[...]
    lines = columns // LANES

    def own_columns(ref):
        return jnp.concatenate([ref[pl.ds(place[1] * lines + k, 1), :] for k in range(lines)], axis=1)

    cols_index = own_columns(index_c)
    cols_chain = own_columns(chain_c)
    mask = (own_columns(mask_c).astype(F32) - 1.0) * 1000000000.0
    reach = (BUCKETS - 2) // 2
    for r in range(rows):
        i = place[0] * (rows * pl.num_programs(0)) + step * rows + r
        normed = normalize(pair[r])
        linear = lax.dot_general(
            w, normed, (((1,), (1,)), ((), ())), precision=lax.Precision.HIGHEST,
            preferred_element_type=F32,
        )
        offset = jnp.clip(index_s[i] - cols_index, -reach, reach) + reach
        bucket = jnp.where(chain_s[i] == cols_chain, offset, BUCKETS - 1)
        classes = lax.broadcasted_iota(jnp.int32, (TABLE_ROWS, columns), 0)
        onehot = (classes == bucket).astype(F32)
        relative = lax.dot_general(
            table, onehot, (((1,), (0,)), ((), ())), precision=lax.Precision.HIGHEST,
            preferred_element_type=F32,
        )
        out[:, r, :] = (linear + relative + mask) * LOG2E


def pair_bias(place, numbering, chain, presence, pair, weight, table):
    rows, columns, channels = pair.shape
    part = 16

    def whole(shape):
        return pl.BlockSpec(shape, lambda r, *_: (0,) * len(shape))

    lines = numbering.shape[0] // LANES
    return pl.pallas_call(
        bias_kernel,
        out_shape=jax.ShapeDtypeStruct((HEADS, rows, columns), F32),
        grid_spec=pltpu.PrefetchScalarGridSpec(
            num_scalar_prefetch=3,
            grid=(rows // part,),
            in_specs=[
                pl.BlockSpec((part, columns, channels), lambda r, *_: (r, 0, 0)),
                whole((HEADS, channels)),
                whole((HEADS, TABLE_ROWS)),
            ] + [whole((lines, LANES))] * 3,
            out_specs=pl.BlockSpec((HEADS, part, columns), lambda r, *_: (0, r, 0)),
        ),
        compiler_params=params(1, 32),
        name="pair_bias",
    )(
        place, numbering, chain, pair, weight.T,
        jnp.pad(table, ((0, TABLE_ROWS - BUCKETS), (0, 0))).T,
        numbering.reshape(lines, LANES), chain.reshape(lines, LANES), presence.reshape(lines, LANES),
    )


def pack_kernel(w, merge, gate_bias, out):
    rows = w.shape[0] * w.shape[1]
    for t in range(w.shape[0]):
        out[pl.ds(t * w.shape[1], w.shape[1]), :] = w[t]
    out[pl.ds(rows, merge.shape[0]), :] = merge[...]
    copies = out.shape[1] // gate_bias.shape[1]
    gate = jnp.concatenate([gate_bias[...]] * copies, axis=1)
    out[pl.ds(out.shape[0] - 8, 8), :] = jnp.broadcast_to(gate, (8, out.shape[1]))


def pack(w, merge, gate_bias):
    w = jnp.swapaxes(w, 1, 2)
    rows = w.shape[0] * w.shape[1] + merge.shape[0] + 8
    return pl.pallas_call(
        pack_kernel, out_shape=jax.ShapeDtypeStruct((rows, merge.shape[1]), F32), name="pack"
    )(w, merge, gate_bias[None])


def project_kernel(place, row, own, gain, packed, kp, vp, qp, gp, wk2, wv2, wq2, wg2, gate_bias):
    channels = row.shape[2]

    @pl.when(pl.program_id(0) == 0)
    def _():
        narrow = HEADS * DEPTH // packed.shape[0]
        for q in range(packed.shape[0]):
            at = pl.ds(q * narrow, narrow)
            wk2[0, at], wk2[1, at] = split(packed[q, pl.ds(narrow, narrow), :])
        for h in range(HEADS):
            q, start = h // 2, h % 2 * DEPTH
            at = pl.ds(h * LANES, LANES)
            for t, copies, target in ((0, 4, wq2), (2, 2, wv2), (3, 2, wg2)):
                part = packed[q, pl.ds(t * narrow + start, DEPTH), :]
                rest = [jnp.zeros((LANES - copies * DEPTH, channels), F32)] if copies * DEPTH < LANES else []
                parts = [part] * copies + rest if h % 2 == 0 else rest + [part] * copies
                target[0, at], target[1, at] = split(jnp.concatenate(parts, axis=0))
            gate = packed[q, pl.ds(packed.shape[1] - 8, 8), :][:1, start:start + DEPTH]
            rest = jnp.zeros((1, LANES - 2 * DEPTH), F32)
            gate_bias[:, at] = jnp.concatenate([gate, gate, rest] if h % 2 == 0 else [rest, gate, gate], axis=1)

    positions = row.shape[1]
    own_positions = own.shape[1]
    n = split(normalize(row[0]) * gain[...])
    keys = split(dot3((wk2[0], wk2[1]), n, ((1,), (1,))))
    for h in range(HEADS):
        for part in range(4):
            kp[0, h, pl.ds(part * DEPTH, DEPTH), :] = keys[part % 2][h * DEPTH:(h + 1) * DEPTH]
    pair_lanes = 2 * LANES
    lane = lax.broadcasted_iota(jnp.int32, (positions, LANES), 1)
    for h in range(0, HEADS, 2):
        cut = pl.ds(h * LANES, pair_lanes)
        both = dot3(n, (wv2[0, cut], wv2[1, cut]), ((1,), (1,)))
        for k in range(2):
            value = both[:, k * LANES:(k + 1) * LANES]
            high = value.astype(BF16).astype(F32)
            at = lane - k * (LANES // 2)
            packed = jnp.where((at >= 0) & (at < DEPTH), high,
                               jnp.where((at >= DEPTH) & (at < 2 * DEPTH), value - high, 1.0))
            vp[0, h + k] = packed.astype(BF16)
    m = split(normalize(own[0]) * gain[...])
    lane = lax.broadcasted_iota(jnp.int32, (own_positions, LANES), 1)
    for h in range(0, HEADS, 2):
        cut = pl.ds(h * LANES, pair_lanes)
        both = dot3(m, (wq2[0, cut], wq2[1, cut]), ((1,), (1,))) * (LOG2E / math.sqrt(DEPTH))
        gates = dot3(m, (wg2[0, cut], wg2[1, cut]), ((1,), (1,))) + gate_bias[:, cut]
        gates = jax.nn.sigmoid(gates)
        for k in range(2):
            value = both[:, k * LANES:(k + 1) * LANES]
            high = value.astype(BF16).astype(F32)
            qp[0, h + k] = jnp.where(lane < 2 * DEPTH, high, value - high).astype(BF16)
            gp[0, h + k] = gates[:, k * LANES:(k + 1) * LANES]


def project(place, rows, gain, packed, quarter):
    count, positions, channels = rows.shape
    wide = HEADS * LANES

    def whole(shape):
        return pl.BlockSpec(shape, lambda s, place: (0,) * len(shape))

    def out(rows_, columns, dtype):
        return (
            jax.ShapeDtypeStruct((count, HEADS, rows_, columns), dtype),
            pl.BlockSpec((1, HEADS, rows_, columns), lambda s, place: (s, 0, 0, 0)),
        )

    outs = [out(LANES, positions, BF16), out(positions, LANES, BF16),
            out(quarter, LANES, BF16), out(quarter, LANES, F32)]
    return pl.pallas_call(
        project_kernel,
        out_shape=[o[0] for o in outs],
        grid_spec=pltpu.PrefetchScalarGridSpec(
            num_scalar_prefetch=1,
            grid=(count,),
            in_specs=[
                pl.BlockSpec((1, positions, channels), lambda s, place: (s, 0, 0)),
                pl.BlockSpec((1, quarter, channels), lambda s, place: (s, place[1], 0)),
                whole((1, channels)), whole(packed.shape),
            ],
            out_specs=[o[1] for o in outs],
            scratch_shapes=[pltpu.VMEM((2, HEADS * DEPTH, channels), BF16)]
            + [pltpu.VMEM((2, wide, channels), BF16)] * 3 + [pltpu.VMEM((1, wide), F32)],
        ),
        compiler_params=params(1, 52),
        name="project",
    )(place, rows, rows, gain[None], packed)


def attend_kernel(place, flags_s, bias_a, b0, b1, b2, b3, b4, kp, vp, qp, gp, merge, own, operand_t,
                  mask_c, state_out, first_out, second_out, gated, head_bias, merge_rows):
    h = pl.program_id(0)
    count = own.shape[0]
    quarter = own.shape[1]
    nz, ny, width = bias_a.shape[0], bias_a.shape[1], bias_a.shape[5]
    group = quarter // nz

    def columns(k):
        return pl.ds(pl.multiple_of(lax.rem(place[2] + Y_STEPS[k], ny) * width, width), width)

    def rows(k):
        return pl.ds(pl.multiple_of(lax.rem(place[3] + Z_STEPS[k], nz) * group, group), group)

    @pl.when(h == 0)
    def _():
        gated[...] = jnp.zeros_like(gated)

    @pl.when(h < HEADS_A)
    def _():
        for k in range(ny):
            head_bias[:, columns(k)] = bias_a[:, k, :, 0].reshape(quarter, width)

    @pl.when(h >= HEADS_A)
    def _():
        for y, pieces in enumerate(((b0,), (b1,), (b2,), (b3, b4))):
            k = 0
            for piece in pieces:
                for line in range(piece.shape[0]):
                    head_bias[rows(k), columns(y)] = piece[line, :, 0].reshape(group, width)
                    k += 1

    half = LANES // 2
    lane = lax.broadcasted_iota(jnp.int32, (quarter, LANES), 1)
    own_lanes = lane // half == lax.rem(h, 2)
    at = pl.ds(pl.multiple_of(h // 2 * LANES, LANES), LANES)
    ahead = dot(qp[0, 0], kp[0, 0]) + head_bias[...]
    for s in range(count):
        logits = ahead
        if s + 1 < count:
            ahead = dot(qp[s + 1, 0], kp[s + 1, 0]) + head_bias[...]
        peak = jnp.max(logits, axis=1, keepdims=True)
        weights = jnp.exp2(logits - peak)
        mixed = dot(jnp.concatenate(split(weights), axis=0), vp[s, 0])
        mixed = mixed[:quarter] + mixed[quarter:]
        total_weight = jnp.where(own_lanes, pltpu.roll(mixed, half, 1), 1.0)
        parts = split(jnp.where(own_lanes, mixed * gp[s, 0] / total_weight, 0.0))
        gated[0, s, :, at] += parts[0]
        gated[1, s, :, at] += parts[1]

    @pl.when(h == pl.num_programs(0) - 1)
    def _():
        ops = split(operand_t[...])
        for k in range(HEADS):
            rows_k = merge[k // 2, pl.ds(k % 2 * DEPTH, DEPTH), :]
            for copy in range(2):
                merge_rows[pl.ds((2 * k + copy) * DEPTH, DEPTH), :] = rows_k
        m2 = split(merge_rows[...])
        for s in range(count):
            state = own[s] + dot3((gated[0, s], gated[1, s]), m2)
            state_out[s] = state
            n = split(normalize(state))
            flag = flags_s[place[0] * count + s].astype(F32)
            factors = dot3(ops, n, ((1,), (1,))) * (mask_c[0] * flag)
            first_out[s] = factors[:RANK]
            for e in range(RANK):
                second_out[pl.ds(s, 1), pl.ds(e * quarter, quarter)] = factors[RANK + e:RANK + e + 1]


def attend(place, flags, bias, kp, vp, qp, gp, merge, rows, operand_t, mask, quarter):
    count, positions, channels = rows.shape

    merge_size = HEADS * DEPTH // merge.shape[0]

    def piece_block(piece, low, high):
        shape = list(piece.shape)
        shape[-3] = 1

        def at(h, *_):
            index = [0] * len(shape)
            index[-3] = jnp.clip(h - low, 0, high)
            return tuple(index)

        return pl.BlockSpec(tuple(shape), at)

    def head_block(rows_, columns):
        return pl.BlockSpec((count, 1, rows_, columns), lambda h, *_: (0, h, 0, 0))

    return pl.pallas_call(
        attend_kernel,
        out_shape=[
            jax.ShapeDtypeStruct((count, quarter, channels), F32),
            jax.ShapeDtypeStruct((count, RANK, quarter), F32),
            jax.ShapeDtypeStruct((count, RANK * quarter), F32),
        ],
        grid_spec=pltpu.PrefetchScalarGridSpec(
            num_scalar_prefetch=2,
            grid=(HEADS,),
            in_specs=[
                piece_block(bias[0], 0, HEADS_A - 1),
            ] + [piece_block(piece, HEADS_A, HEADS - HEADS_A - 1) for piece in bias[1]] + [
                head_block(LANES, positions), head_block(positions, LANES),
                head_block(quarter, LANES), head_block(quarter, LANES),
                pl.BlockSpec((merge.shape[0], merge_size, channels), lambda h, *_: (0, 4, 0)),
                pl.BlockSpec((count, quarter, channels), lambda h, place, *_: (0, place[1], 0)),
                pl.BlockSpec((2 * RANK, channels), lambda h, *_: (0, 0)),
                pl.BlockSpec((1, 1, quarter), lambda h, place, *_: (place[1], 0, 0)),
            ],
            out_specs=[
                pl.BlockSpec((count, quarter, channels), lambda h, *_: (0, 0, 0)),
                pl.BlockSpec((count, RANK, quarter), lambda h, *_: (0, 0, 0)),
                pl.BlockSpec((count, RANK * quarter), lambda h, *_: (0, 0)),
            ],
            scratch_shapes=[
                pltpu.VMEM((2, count, quarter, 2 * HEADS * DEPTH), BF16),
                pltpu.VMEM((quarter, positions), F32),
                pltpu.VMEM((2 * HEADS * DEPTH, channels), F32),
            ],
        ),
        compiler_params=params(1, 52),
        name="attend",
    )(place, flags, bias[0], *bias[1], kp, vp, qp, gp, merge, rows, operand_t, mask.reshape(-1, 1, quarter))


def outer_kernel(group, place, mask_s, f0, f1, sa, s0, s1, s2, s3, s4, weight_t, out_bias,
                 count_c, pair, t0, t1, t2, t3, out, state, ordered, moved, a2, w2, r2):
    step = pl.program_id(0)
    steps = RANK // group
    i_rows = r2.shape[1]
    columns = pair.shape[1]
    nz, ny, eight = sa.shape[0], sa.shape[1], sa.shape[2]
    y_at = [lax.rem(place[2] + k, ny) for k in Y_STEPS]
    z_at = [lax.rem(place[3] + k, nz) for k in Z_STEPS]

    def row(y, z):
        return pl.ds(pl.multiple_of((y * nz + z) * eight, eight), eight)

    @pl.when(step == 0)
    def _():
        high, low = split(weight_t[...])
        w2[:LANES], w2[LANES:] = high, low
        for r, piece in enumerate((f0, f1)):
            size = piece.shape[1]
            for k in range(piece.shape[0]):
                y = lax.rem((place[1] ^ r) + 2 * k, ny)
                ordered[pl.ds(pl.multiple_of(y * size, size), size), :] = piece[k]
        for z in range(nz):
            for k in range(ny):
                moved[pl.ds((z * ny + k) * eight, eight), :] = ordered[row(y_at[k], z), :]
        a2[0], a2[1] = split(moved[...].T)

    @pl.when(step == steps // 2)
    def _():
        for k in range(ny):
            for z in range(nz):
                moved[pl.ds((k * nz + z) * eight, eight), :] = ordered[row(y_at[k], z_at[z]), :]
        a2[0], a2[1] = split(moved[...].T)

    def products(blocks):
        for g in range(group):
            cut = pl.ds(g * columns, columns)
            b = [block[..., cut].reshape(-1, columns) for block in blocks]
            b = split(b[0] if len(b) == 1 else jnp.concatenate(b, axis=0))
            r = split(dot3((a2[0], a2[1]), b))
            at = pl.multiple_of((step * group + g) * RANK, RANK)
            for part in range(2):
                for i in range(i_rows):
                    r2[part, i, pl.ds(at, RANK), :] = r[part][i * RANK:(i + 1) * RANK]

    @pl.when(step < steps // 2)
    def _():
        products((sa,))

    @pl.when((step >= steps // 2) & (step < steps))
    def _():
        products((s0, s1, s2, s3, s4))

    @pl.when(step >= steps)
    def _():
        for k in range(pair.shape[0]):
            i = (step - steps) * pair.shape[0] + k
            both = dot(w2[...], r2[0, i])
            value = both[:LANES] + (both[LANES:] + dot(w2[:LANES], r2[1, i])) + out_bias[...]
            count = jnp.maximum(mask_s[place[0] * i_rows + i].astype(F32) * count_c[0], 1.0)
            out[k] = pair[k] + (value * (1.0 / count)).T
        for k, piece in enumerate((t0, t1, t2, t3)):
            @pl.when((step - steps) // 2 == k)
            def _(piece=piece):
                state[...] = piece[...]


def outer_mean(place, mask, first, second, weight_t, out_bias, count, pair, state):
    rows, columns, channels = pair.shape
    members = sum(piece.shape[0] * piece.shape[1] for piece in first)
    wide = rows * RANK
    group = 8
    steps = RANK // group
    half = steps // 2
    part = 2
    count_s, quarter, features = state[0].shape
    lines = count_s // 2
    whole_state = (count_s, quarter * len(state), features)

    def state_block(t, place, *_):
        at = jnp.clip(t - steps, 0, 2 * len(state) - 1)
        return (lax.rem(at, 2), place[1] ^ (at // 2), 0)

    def own(t, *_):
        return (jnp.maximum(t - steps, 0), 0, 0)

    def whole(shape):
        return pl.BlockSpec(shape, lambda t, *_: (0,) * len(shape))

    def columns_block(piece, low):
        lead = piece.shape[:-1]
        return pl.BlockSpec(
            lead + (group * columns,),
            lambda t, *_: (0,) * len(lead) + (jnp.clip(t - low, 0, half - 1),),
        )

    return pl.pallas_call(
        partial(outer_kernel, group),
        out_shape=[
            jax.ShapeDtypeStruct(pair.shape, F32),
            jax.ShapeDtypeStruct(whole_state, F32),
        ],
        grid_spec=pltpu.PrefetchScalarGridSpec(
            num_scalar_prefetch=2,
            grid=(steps + rows // part,),
            in_specs=[whole(piece.shape) for piece in first]
            + [columns_block(second[0], 0)]
            + [columns_block(piece, half) for piece in second[1]]
            + [
                whole((channels, RANK * RANK)),
                whole((channels, 1)),
                pl.BlockSpec((1, 1, columns), lambda t, place, *_: (place[1], 0, 0)),
                pl.BlockSpec((part, columns, channels), own),
            ] + [
                pl.BlockSpec((lines, quarter, features),
                             lambda t, *_, k=k: (jnp.clip(t - steps - 2 * k, 0, 1), 0, 0))
                for k in range(len(state))
            ],
            out_specs=[pl.BlockSpec((part, columns, channels), own),
                       pl.BlockSpec((lines, quarter, features), state_block)],
            scratch_shapes=[
                pltpu.VMEM((members, wide), F32),
                pltpu.VMEM((members, wide), F32),
                pltpu.VMEM((2, wide, members), BF16),
                pltpu.VMEM((2 * channels, RANK * RANK), BF16),
                pltpu.VMEM((2, rows, RANK * RANK, columns), BF16),
            ],
        ),
        compiler_params=params(1, 52),
        name="outer_mean",
    )(place, mask, *first, second[0], *second[1], weight_t, out_bias[:, None],
      count.reshape(-1, 1, columns), pair, *state)


Y_STEPS = (0, 3, 1, 2)
Z_STEPS = (0, 7, 1, 6, 2, 5, 3, 4)


def shift(block, axis, size, step):
    return lax.ppermute(block, axis, [(i, (i + step) % size) for i in range(size)])


def gather_both(block_a, block_b, ny, nz, early=()):
    along = [shift(block_a, "y", ny, -k) for k in Y_STEPS[1:]]
    one = [shift(block_b, "z", nz, k) for k in (1, -1)]
    two = [shift(block_b, "z", nz, k) for k in (2, -2)]
    along, early = lax.optimization_barrier((along, early))
    gathered_a = lax.all_gather(jnp.stack([block_a] + along), "z")
    three = [shift(one[0], "z", nz, 2), shift(one[1], "z", nz, -2)]
    cut = block_b.shape[0] // 2
    four = [shift(two[0][:cut], "z", nz, 2), shift(two[1][cut:], "z", nz, -2)]
    gathered_b = jnp.stack([block_b] + one + two + three + [jnp.concatenate(four)])
    return gathered_a, gathered_b, early


def gather_y(block, ny, beside=()):
    one = [shift(block, "y", ny, k) for k in (1, -1)]
    one, beside = lax.optimization_barrier((one, beside))
    cut = block.shape[0] // 2
    two = [shift(one[0][:cut], "y", ny, 1), shift(one[1][cut:], "y", ny, -1)]
    return [block] + one + two, beside


def in_order(mine, other):
    low = lax.axis_index("xl") == 0
    return jnp.stack([jnp.where(low, mine, other), jnp.where(low, other, mine)])


def per_device(
    sizes,
    lineup_embedding,
    pairwise_state,
    lineup_scaling_coefficients,
    focus_projection_matrix,
    attention_gate_bias,
    focus_merge_matrix,
    pairwise_bias_weight,
    relative_bias_table,
    tensor_operand_matrices,
    outer_output_weight,
    outer_output_bias,
    lineup_member_flags,
    residue_presence_mask,
    chain_label,
    residue_numbering,
):
    ny, nz, nxl, nxh, nc = (sizes[a] for a in ("y", "z", "xl", "xh", "c"))
    nq = nxh * nc
    dap = (lax.axis_index("y") * nz + lax.axis_index("z")) * nxl + lax.axis_index("xl")
    head = lax.axis_index("xh") * nc + lax.axis_index("c")
    place = jnp.stack([dap, head, lax.axis_index("y"), lax.axis_index("z")]).astype(jnp.int32)
    count, positions, channels = lineup_embedding.shape
    block_rows, quarter, pair_channels = pairwise_state.shape
    presence = residue_presence_mask.astype(F32)

    packed = pack(focus_projection_matrix, focus_merge_matrix, attention_gate_bias)
    packed, pairwise_state = lax.optimization_barrier((packed, pairwise_state))
    packed = lax.all_gather(packed, HEAD_AXES)

    local = pair_bias(place, residue_numbering, chain_label, residue_presence_mask, pairwise_state,
                      pairwise_bias_weight, relative_bias_table)

    def swap(flip):
        perm = []
        for y in range(ny):
            for x in range(nxl):
                for q in range(nq):
                    perm.append(((y * nxl + x) * nq + q, (q * nxl + (x ^ flip)) * nq + y))
        return lax.ppermute(local, ("y", "xl") + HEAD_AXES, perm)

    bias = in_order(swap(0), swap(1))
    bias_a, bias_b, packed = gather_both(bias[:, :HEADS_A], bias[:, HEADS_A:], ny, nz, packed)
    bias_b, rows = lax.optimization_barrier((bias_b, lineup_embedding))
    projected = project(place, rows, lineup_scaling_coefficients, packed, quarter)
    bias_b, (kp, vp, qp, gp) = gather_y(bias_b, ny, projected)
    bias = (bias_a, bias_b)
    operand_t = jnp.swapaxes(tensor_operand_matrices, 1, 2).reshape(2 * RANK, channels)
    state, first, second = attend(place, lineup_member_flags, bias, kp, vp, qp, gp, packed,
                                  lineup_embedding, operand_t, presence, quarter)

    second = in_order(second, shift(second, "xl", nxl, 1)).reshape(nxl * count, -1)
    half = second.shape[1] // 2
    second_a, second_b, _ = gather_both(second[:, :half], second[:, half:], ny, nz)
    second_b, first, state = lax.optimization_barrier((second_b, first, state))

    parts = nz * nxl
    first = jnp.transpose(first.reshape(count, RANK, parts, block_rows), (2, 0, 3, 1))
    first = lax.all_to_all(first.reshape(parts, count, block_rows * RANK), ("z", "xl"), 0, 0, tiled=True)
    across = shift(state, "xh", nxh, 1)
    first, across = lax.optimization_barrier((first.reshape(parts * count, -1), across))
    first = [
        lax.ppermute(first, ("y",) + HEAD_AXES,
                     [(y * nq + q, q * nq + (y + r) % nq) for y in range(ny) for q in range(nq)])
        for r in (0, 2)
    ]

    pieces = [state, shift(state, "c", nc, 1), across, shift(across, "c", nc, 1)]
    second_b, _ = gather_y(second_b, ny)
    second = (second_a, second_b)
    first = jnp.stack(first)
    first = [first, shift(first, "c", nc, 1)]

    weight_t = jnp.transpose(
        outer_output_weight.reshape(RANK, RANK, pair_channels), (2, 1, 0)
    ).reshape(pair_channels, RANK * RANK)
    count_columns = presence * jnp.sum(lineup_member_flags.astype(F32))
    pairs, state = outer_mean(place, residue_presence_mask, first, second, weight_t,
                              outer_output_bias, count_columns, pairwise_state, pieces)
    return state, pairs


def solution(mesh):
    sizes = dict(y=4, z=8, xl=2, xh=2, c=2)
    fine = Mesh(mesh.devices.reshape(tuple(sizes.values())), tuple(sizes))
    placed = (
        P(DAP_AXES, None, None),
        P(DAP_AXES, HEAD_AXES, None),
        P(),
        P(None, None, HEAD_AXES),
        P(HEAD_AXES),
        P(HEAD_AXES, None),
    ) + (P(),) * 9
    return jax.shard_map(
        partial(per_device, sizes),
        mesh=fine,
        in_specs=placed,
        out_specs=(P(DAP_AXES, None, None), P(DAP_AXES, HEAD_AXES, None)),
        check_vma=False,
    )
```
